32 devices in a mesh: wide: 16 (over z, x, core), heads: 2 (over y).
Axes of the slice: x: 2, y: 2, z: 4, core: 2. Of those that a mesh axis runs over, the one named last changes fastest.
Arguments:
- inputs: bfloat16 [32768, 1280], P('wide'), may hold values from -6 to 6
- segment_ids: int32 [32768], P('wide'), may hold values from 0 to 4095, never falling along the last dimension, each value on 1 to 16 neighbouring positions
- cotangent: bfloat16 [32768, 1280], P('wide'), may hold values from -6 to 6
- w_query: bfloat16 [1280, 1280], P('wide', 'heads'), may hold values from -0.15625 to 0.15625
- w_key: bfloat16 [1280, 1280], P('wide', 'heads'), may hold values from -0.15625 to 0.15625
- w_value: bfloat16 [1280, 1280], P('wide', 'heads'), may hold values from -0.15625 to 0.15625
- w_out: bfloat16 [1280, 1280], P('heads', 'wide'), may hold values from -0.3125 to 0.3125
- w_up: bfloat16 [1280, 1280], P('wide', 'heads'), may hold values from -0.15625 to 0.15625
- w_down: bfloat16 [1280, 1280], P('heads', 'wide'), may hold values from -0.25 to 0.25
- b_query: float32 [1280], replicated, may hold values from -3 to 3
- b_value: float32 [1280], replicated, may hold values from -3 to 3
- b_out: float32 [1280], replicated, may hold values from -3 to 3
- b_up: float32 [1280], replicated, may hold values from -3 to 3
- b_down: float32 [1280], replicated, may hold values from -3 to 3
- dim_scale: float32 [80], replicated, may hold values from -1 to 1.5
- gain_attn: float32 [1280], replicated, may hold values from 0.5 to 1.5
- gain_mlp: float32 [1280], replicated, may hold values from 0.5 to 1.5
Outputs:
- output: bfloat16 [32768, 1280], P(('wide', 'heads'))
- input_grad: float32 [32768, 1280], P(('wide', 'heads'))
- grad_w_query: float32 [1280, 1280], P('wide', 'heads')
- grad_w_key: float32 [1280, 1280], P('wide', 'heads')
- grad_w_value: float32 [1280, 1280], P('wide', 'heads')
- grad_w_out: float32 [1280, 1280], P('heads', 'wide')
- grad_w_up: float32 [1280, 1280], P('wide', 'heads')
- grad_w_down: float32 [1280, 1280], P('heads', 'wide')
- grad_b_query: float32 [1280], replicated
- grad_b_value: float32 [1280], replicated
- grad_b_out: float32 [1280], replicated
- grad_b_up: float32 [1280], replicated
- grad_b_down: float32 [1280], replicated
- grad_dim_scale: float32 [80], replicated
- grad_gain_attn: float32 [1280], replicated
- grad_gain_mlp: float32 [1280], replicated
The draws below stay inside these ranges and needn't reach their ends.
Inputs may be any that keep to these rules, and one draw needn't show every extreme that they name: `segment_ids`: segment numbers never fall along the tokens; a segment has 1 to 16 tokens.
All inputs are finite; a program needn't handle non-finite values.
Results may differ from the reference program's by a relative error of at most 0.015.
Values may be sent and summed in bfloat16 or wider, within the bound.
A program may use at most 192 MiB of HBM per device.

```python
import math
import jax
import jax.numpy as jnp
import numpy as np
from jax import lax

D = 1280
H = 16
DH = 80
FF = 1280
PATCHES = 16
TOKENS = 32768


def strengthened(values, own_key, source, target, blocks, factor):
    owner, partner = [(jnp.arange(values.shape[dim]) // (values.shape[dim] // blocks)).reshape([-1 if axis == dim else 1 for axis in range(values.ndim)]) for dim in (source, target)]
    chosen = jax.random.permutation(own_key, blocks)[partner]
    strong = (owner == chosen) | (owner == (partner + blocks // 2) % blocks)
    return jnp.where(strong, factor * values, values)


def block_scale(rng, shape, shards, low, top_value):
    def one(dim, shards_of):
        steps = jax.random.uniform(jax.random.fold_in(jax.random.fold_in(rng, 6), dim), (shards_of,), jnp.float32, low / len(shards), top_value / len(shards))
        return jnp.repeat(jnp.exp(steps), shape[dim] // shards_of).reshape((-1,) + (1,) * (len(shape) - dim - 1))

    factor_of = one(*shards[0])
    for cut in shards[1:]:
        factor_of = factor_of * one(*cut)
    return factor_of


def split_up(amount, total, bound, lean):
    weights = [(1 << 20) // math.isqrt(grade ** lean) + 1 for grade in range(2, amount + 1)]
    spare, counts = total - bound - (amount - 1), [1] * (amount - 1)
    while spare > 0:
        movable = [i for i in range(amount - 1) if counts[i] < bound]
        pool, remaining = sum([weights[i] for i in movable]), spare
        for i in movable:
            addition = min(bound - counts[i], max(1, remaining * weights[i] // pool), spare)
            counts[i] = counts[i] + addition
            spare = spare - addition
    return np.array([bound] + counts)


def ragged_sizes(key, amount, total, reach, lean):
    if amount == 2:
        one = jax.random.randint(key, (), max(1, total - reach), min(reach, total - 1) + 1)
        return jnp.stack([one, total - one])
    sizes = jnp.asarray(split_up(amount, total, reach, lean), jnp.int32)
    pairs = (amount - 1) // 2
    donor, sink = sizes[1:1 + 2 * pairs:2], sizes[2:2 + 2 * pairs:2]
    room = jnp.minimum(donor - 1, reach - sink)
    passed = jax.random.randint(jax.random.fold_in(key, 1), (pairs,), 0, 1 << 20) % (room + 1)
    sizes = sizes.at[1:1 + 2 * pairs:2].set(donor - passed).at[2:2 + 2 * pairs:2].set(sink + passed)
    return sizes[jax.random.permutation(jax.random.fold_in(key, 2), amount)]


def centred(key, dims, scale, limit, cuts=(), kind=jnp.bfloat16):
    values = scale * jax.random.normal(key, dims, jnp.float32)
    if cuts:
        values = values * block_scale(key, dims, cuts, -0.22, 0.18)
    return jnp.clip(values, -limit, limit).astype(kind)


def noise_with(key, dims, scale, limit, cuts, heavy, kind=jnp.bfloat16):
    entries = scale * jax.random.normal(key, dims, jnp.float32)
    if cuts:
        entries = entries * block_scale(key, dims, cuts, -0.22, 0.18)
    return jnp.clip(strengthened(entries, jax.random.fold_in(key, 3), *heavy), -limit, limit).astype(kind)


def setup_inputs(seed: int = 0) -> dict:
    key_list = jax.random.split(jax.random.key(seed), 18)
    inputs = noise_with(key_list[0], (TOKENS, D), 1.0, 6.0, ((0, 16),), (0, 1, 16, 2.0))
    segment_ids = jnp.searchsorted(jnp.cumsum(ragged_sizes(key_list[1], TOKENS // 8, TOKENS, PATCHES, 1)), jnp.arange(TOKENS), side="right").astype(jnp.int32)
    cotangent = noise_with(key_list[2], (TOKENS, D), 1.0, 6.0, ((0, 16),), (0, 1, 16, 2.0))
    w_query = centred(key_list[3], (D, H * DH), D ** -0.5, 0.15625, ((0, 16), (1, 2)))
    w_key = centred(key_list[4], (D, H * DH), D ** -0.5, 0.15625, ((0, 16), (1, 2)))
    w_value = centred(key_list[5], (D, H * DH), D ** -0.5, 0.15625, ((0, 16), (1, 2)))
    w_out = centred(key_list[6], (H * DH, D), (H * DH // 4) ** -0.5, 0.3125, ((0, 2), (1, 16)))
    w_up = centred(key_list[7], (D, FF), D ** -0.5, 0.15625, ((0, 16), (1, 2)))
    w_down = centred(key_list[8], (FF, D), (FF // 2) ** -0.5, 0.25, ((0, 2), (1, 16)))
    b_query = centred(key_list[9], (H * DH,), 0.5, 3.0, (), jnp.float32)
    b_value = centred(key_list[10], (H * DH,), 0.5, 3.0, (), jnp.float32)
    b_out = centred(key_list[11], (D,), 0.5, 3.0, (), jnp.float32)
    b_up = centred(key_list[12], (FF,), 0.5, 3.0, (), jnp.float32)
    b_down = centred(key_list[13], (D,), 0.5, 3.0, (), jnp.float32)
    dim_scale = jnp.clip(jax.random.uniform(key_list[14], (DH,), jnp.float32, -1.0, 1.5), -1.0, 1.5)
    gain_attn = jnp.clip(1.0 + 0.1 * jax.random.normal(key_list[15], (D,), jnp.float32), 0.5, 1.5)
    gain_mlp = jnp.clip(1.0 + 0.1 * jax.random.normal(key_list[16], (D,), jnp.float32), 0.5, 1.5)
    return dict(inputs=inputs, segment_ids=segment_ids, cotangent=cotangent, w_query=w_query, w_key=w_key, w_value=w_value, w_out=w_out, w_up=w_up, w_down=w_down, b_query=b_query, b_value=b_value, b_out=b_out, b_up=b_up, b_down=b_down, dim_scale=dim_scale, gain_attn=gain_attn, gain_mlp=gain_mlp)


@jax.custom_vjp
def low(v):
    return lax.optimization_barrier(v.astype(jnp.bfloat16)).astype(jnp.float32)

@jax.custom_vjp
def low_back(v):
    return v

def low_keep(v):
    return (low(v), None)

def low_pass(kept, grad):
    return (grad,)

def back_keep(v):
    return (v, None)

def back_low(kept, grad):
    return (low(grad),)
low.defvjp(low_keep, low_pass)
low_back.defvjp(back_keep, back_low)
eps = 1e-06
query_base = 1.442695041
highest_prec = lax.Precision.HIGHEST

def matmul(left, right):
    return jnp.dot(left, right, precision=highest_prec, preferred_element_type=jnp.float32)

def rms_norm(values, gain_vec):
    return values * lax.rsqrt(lax.optimization_barrier(jnp.mean(values * values, axis=-1, keepdims=True)) + eps) * gain_vec

def layer_block(block_in, seg_block, params):
    w_query, w_key, w_value, w_out, w_up, w_down, b_query, b_value, b_out, b_up, b_down, dim_scale, gain_attn, gain_mlp = params
    block_len = block_in.shape[0]
    seq_count = block_len // PATCHES
    normed_one = low(rms_norm(block_in, gain_attn))
    query_proj = low_back(matmul(normed_one, w_query) + b_query)
    key_proj = low(low_back(matmul(normed_one, w_key)))
    value_proj = low(low_back(matmul(normed_one, w_value) + b_value))
    query_scale = query_base / math.sqrt(DH) * jax.nn.softplus(dim_scale)
    query_seq = low(query_proj.reshape(seq_count, PATCHES, H, DH) * query_scale)
    key_seq = key_proj.reshape(seq_count, PATCHES, H, DH)
    value_seq = value_proj.reshape(seq_count, PATCHES, H, DH)
    scores = low_back(jnp.einsum('sqhe,skhe->shqk', query_seq, key_seq, precision=highest_prec))
    seg_rows = seg_block.reshape(seq_count, PATCHES)
    position = jnp.arange(PATCHES)
    allowed = (seg_rows[:, :, None] == seg_rows[:, None, :]) & (position[:, None] >= position[None, :])[None]
    scores = jnp.where(allowed[:, None], scores, -1e+30)
    attn_probs = jax.nn.softmax(scores, axis=-1)
    attended = jnp.einsum('shqk,skhe->sqhe', low(attn_probs), value_seq, precision=highest_prec)
    attended = low(low_back(attended.reshape(block_len, H * DH)))
    residual = block_in + low_back(matmul(attended, w_out)) + b_out
    normed_two = low(rms_norm(residual, gain_mlp))
    up_proj = low_back(matmul(normed_two, w_up) + b_up)
    activated = low(jax.nn.gelu(up_proj))
    return residual + low_back(matmul(activated, w_down)) + b_down

def reference(inputs, segment_ids, cotangent, w_query, w_key, w_value, w_out, w_up, w_down, b_query, b_value, b_out, b_up, b_down, dim_scale, gain_attn, gain_mlp):
    params = tuple((item.astype(jnp.float32) for item in (w_query, w_key, w_value, w_out, w_up, w_down, b_query, b_value, b_out, b_up, b_down, dim_scale, gain_attn, gain_mlp)))
    block_len = min(4096, TOKENS)
    block_count = TOKENS // block_len
    input_blocks = inputs.astype(jnp.float32).reshape(block_count, block_len, D)
    seg_blocks = segment_ids.reshape(block_count, block_len)
    cot_blocks = cotangent.astype(jnp.float32).reshape(block_count, block_len, D)
    zero_grads = jax.tree.map(jnp.zeros_like, params)

    def block_step(running, pieces):
        block_in, seg_block, cot_block = pieces
        result, pullback = jax.vjp(lambda inner_in, inner_params: layer_block(inner_in, seg_block, inner_params), block_in, params)
        grad_in, grad_params = pullback(cot_block)
        return (jax.tree.map(jnp.add, running, grad_params), (result, grad_in))
    summed, (out_blocks, grad_blocks) = lax.scan(block_step, zero_grads, (input_blocks, seg_blocks, cot_blocks))
    output = out_blocks.reshape(TOKENS, D).astype(jnp.bfloat16)
    input_grad = grad_blocks.reshape(TOKENS, D)
    return (output, input_grad, summed[0], summed[1], summed[2], summed[3], summed[4], summed[5], summed[6], summed[7], summed[8], summed[9], summed[10], summed[11], summed[12], summed[13])
```

```python
import functools
import math

import jax
import jax.numpy as jnp
from jax import lax
from jax.experimental import pallas as pl
from jax.experimental.pallas import tpu as pltpu
from jax.sharding import PartitionSpec as P

DH = 80
PATCHES = 16
EPS = 1e-06
QUERY_BASE = 1.442695041
BF = jnp.bfloat16
F32 = jnp.float32
MESH = pl.DeviceIdType.MESH
ROWS = 256
SEQ = 128
GELU_C = math.sqrt(2.0 / math.pi)


def nn(left, right):
    return jnp.dot(left, right, preferred_element_type=F32)


def nt(left, right):
    return lax.dot_general(left, right, (((1,), (1,)), ((), ())), preferred_element_type=F32)


def tn(left, right):
    return lax.dot_general(left, right, (((0,), (0,)), ((), ())), preferred_element_type=F32)


def inverse_rms(values):
    return lax.rsqrt(jnp.mean(values * values, axis=-1, keepdims=True) + EPS)


def tile(index, size):
    return pl.ds(pl.multiple_of(index * size, size), size)


def head_window(pair):
    return (2 * DH * pair) // 128 * 128


def head_masks(pair):
    lanes = head_window(pair) + lax.broadcasted_iota(jnp.int32, (SEQ, 256), 1)
    picks = []
    for head in (2 * pair, 2 * pair + 1):
        inside = (lanes >= DH * head) & (lanes < DH * (head + 1))
        picks.append(jnp.where(inside, 1.0, 0.0).astype(BF))
    return picks


def block_offset():
    row = lax.broadcasted_iota(jnp.int32, (SEQ, SEQ), 0) // PATCHES
    col = lax.broadcasted_iota(jnp.int32, (SEQ, SEQ), 1) // PATCHES
    return row, col


def roll_rows(values, blocks):
    shift = (blocks % 8) * PATCHES
    if shift == 0:
        return values
    return jnp.concatenate([values[SEQ - shift :], values[: SEQ - shift]], axis=0)


def split_heads(window, masks):
    return jnp.concatenate([window * masks[0], window * masks[1]], axis=0)


def split_rolled(window, masks, slots):
    return jnp.concatenate(
        [roll_rows(window, slots[0]) * masks[0], roll_rows(window, slots[1]) * masks[1]], axis=0
    )


def pack_scores(left_ref, right_ref, rows, group):
    row, col = block_offset()
    offset = lax.rem(row - col + 8, 8)
    packed = jnp.zeros((SEQ, SEQ), F32)
    for pair in range(4 * group, 4 * group + 4):
        win = pl.ds(head_window(pair), 256)
        both = nt(left_ref[rows, win], split_heads(right_ref[rows, win], head_masks(pair)))
        for side in range(2):
            slot = (2 * pair + side) % 8
            one = roll_rows(both[:, SEQ * side : SEQ * (side + 1)], slot)
            packed = jnp.where(offset == slot, one, packed)
    return packed


def spread(packed, group, right_ref, rows):
    row, col = block_offset()
    offset = lax.rem(col - row + 8, 8)
    parts = []
    for pair in range(4 * group, 4 * group + 4):
        slots = (2 * pair % 8, (2 * pair + 1) % 8)
        left = jnp.concatenate(
            [packed * jnp.where(offset == s, 1.0, 0.0).astype(BF) for s in slots], axis=1
        )
        win = pl.ds(head_window(pair), 256)
        parts.append(nn(left, split_rolled(right_ref[rows, win], head_masks(pair), slots)))
    return join_windows(parts)


def join_windows(parts):
    tiles = [parts[0][:, :128]]
    for before, after in zip(parts[:-1], parts[1:]):
        tiles.append(before[:, 128:] + after[:, :128])
    tiles.append(parts[-1][:, 128:])
    return jnp.concatenate(tiles, axis=1)


def softmax_packed(packed, allowed):
    scores = jnp.where(allowed > 0.5, packed, -1e30).reshape(8, PATCHES, SEQ)
    exps = jnp.exp(scores - jnp.max(scores, axis=1, keepdims=True))
    return (exps / jnp.sum(exps, axis=1, keepdims=True)).reshape(SEQ, SEQ)


class Peers:
    def __init__(self):
        wide = lax.axis_index("wide")
        self.y = lax.axis_index("heads")
        self.z = wide // 4
        self.x = lax.rem(wide // 2, 2)
        self.c = lax.rem(wide, 2)

    def device(self, z, x, y, c):
        return ((z * 2 + x) * 2 + c, y)

    def across_x(self):
        return self.device(self.z, 1 - self.x, self.y, self.c)

    def across_y(self):
        return self.device(self.z, self.x, 1 - self.y, self.c)

    def across_core(self):
        return self.device(self.z, self.x, self.y, 1 - self.c)

    def along_z(self, step):
        return self.device(lax.rem(self.z + step, 4), self.x, self.y, self.c)

    def enter(self):
        barrier = pltpu.get_barrier_semaphore()
        others = [self.across_x(), self.across_y(), self.across_core()]
        others += [self.along_z(step) for step in (1, 2, 3)]
        for other in others:
            pl.semaphore_signal(barrier, inc=1, device_id=other, device_id_type=MESH)
        pl.semaphore_wait(barrier, len(others))


class Gather:
    def __init__(self, blocks, full, send_sem, recv_sem, own_sem):
        self.blocks, self.full = blocks, full
        self.send_sem, self.recv_sem, self.own_sem = send_sem, recv_sem, own_sem
        self.peers = Peers()
        self.depth, self.width = blocks[0].shape
        self.sent = [0] * len(blocks)

    def at(self, k, z, x, y, c):
        rows = pl.ds(pl.multiple_of((z * 4 + x * 2 + c) * self.depth, 16), self.depth)
        cols = pl.ds(pl.multiple_of(y * self.width, 128), self.width)
        return self.full.at[k, rows, cols]

    def copy(self, k, place, target, slot, source=None):
        z, x, y, c = place
        there = self.at(k, *place)
        return pltpu.make_async_remote_copy(
            src_ref=there if source is None else source,
            dst_ref=there,
            send_sem=self.send_sem.at[k, slot],
            recv_sem=self.recv_sem.at[k, ((z * 2 + x) * 2 + y) * 2 + c],
            device_id=target,
            device_id_type=MESH,
        )

    def send(self, k, place, target, source=None):
        self.copy(k, place, target, self.sent[k], source).start()
        self.sent[k] += 1

    def arrived(self, k, place):
        self.copy(k, place, self.peers.across_core(), 0).wait_recv()

    def own_copy(self, k):
        p = self.peers
        return pltpu.make_async_copy(self.blocks[k], self.at(k, p.z, p.x, p.y, p.c), self.own_sem.at[k])

    def begin(self):
        p = self.peers
        p.enter()
        own = (p.z, p.x, p.y, p.c)
        for k, block in enumerate(self.blocks):
            for step in (1, 2, 3):
                self.send(k, own, p.along_z(step), block)
            self.send(k, own, p.across_x(), block)
            self.send(k, own, p.across_y(), block)
            self.send(k, own, p.across_core(), block)
            self.own_copy(k).start()

    def from_z(self, k):
        if k >= len(self.blocks):
            return
        p = self.peers
        for step in (1, 3, 2):
            place = (lax.rem(p.z + step, 4), p.x, p.y, p.c)
            self.arrived(k, place)
            for target in (p.across_x(), p.across_y(), p.across_core()):
                self.send(k, place, target)

    def from_plane(self, k):
        if k >= len(self.blocks):
            return
        p = self.peers
        for z in range(4):
            place = (z, 1 - p.x, p.y, p.c)
            self.arrived(k, place)
            if z % 2 == 1:
                self.send(k, place, p.across_y())
            self.send(k, place, p.across_core())
            place = (z, p.x, 1 - p.y, p.c)
            self.arrived(k, place)
            if z % 2 == 0:
                self.send(k, place, p.across_x())
            self.send(k, place, p.across_core())

    def from_corner(self, k):
        p = self.peers
        for z in range(4):
            place = (z, 1 - p.x, 1 - p.y, p.c)
            self.arrived(k, place)
            self.send(k, place, p.across_core())

    def ready(self, k):
        p = self.peers
        self.own_copy(k).wait()
        for z in range(4):
            for x in range(2):
                for y in range(2):
                    self.arrived(k, (z, x, y, 1 - p.c))

    def lead(self):
        self.from_z(0)
        self.from_z(1)
        self.from_plane(0)

    def advance(self, k):
        self.from_z(k + 2)
        self.from_plane(k + 1)
        self.from_corner(k)
        self.ready(k)

    def end(self):
        p = self.peers
        for k in range(len(self.blocks)):
            for slot in range(self.sent[k]):
                self.copy(k, (p.z, p.x, p.y, p.c), p.across_core(), slot).wait_send()


class Loaded:
    def __init__(self, blocks, full, own_sem):
        self.blocks, self.full, self.own_sem = blocks, full, own_sem

    def own_copy(self, k):
        return pltpu.make_async_copy(self.blocks[k], self.full.at[k], self.own_sem.at[k])

    def begin(self):
        for k in range(len(self.blocks)):
            self.own_copy(k).start()

    def lead(self):
        pass

    def advance(self, k):
        self.own_copy(k).wait()

    def end(self):
        pass


def forward_kernel(
    remote,
    x_hbm, g_hbm, allow_ref, vec_ref, w0, w1, w2, w3, w4, w5,
    full_out, n1_out, q_out, k_out, v_out, att_out, n2_out, gp_out, res_out, probs_out, gwd_out, y_out,
    full, xs, n1, qs, ks, vs, att, n2, act, gp, res, probs, gwd,
    own_sem, in_sem, out_sem, *remote_sems,
):
    blocks = (w0, w1, w2, w3, w4, w5)
    tokens = xs.shape[0]
    half = lax.axis_index("heads") * tokens
    x_copy = pltpu.make_async_copy(x_hbm.at[pl.ds(pl.multiple_of(half, 16), tokens)], xs, in_sem.at[0])
    g_copy = pltpu.make_async_copy(g_hbm.at[pl.ds(pl.multiple_of(half, 16), tokens)], xs, in_sem.at[1])
    x_copy.start()
    if remote:
        moves = Gather(blocks, full, *remote_sems, own_sem)
    else:
        moves = Loaded(blocks, full, own_sem)
    moves.begin()
    gain_attn, gain_mlp = vec_ref[0:1], vec_ref[1:2]
    bias_q, bias_v, bias_o = vec_ref[2:3], vec_ref[3:4], vec_ref[4:5]
    bias_up, bias_down, scale = vec_ref[5:6], vec_ref[6:7], vec_ref[7:8]
    stores = []

    def store(source, target):
        copy = pltpu.make_async_copy(source, target, out_sem.at[len(stores)])
        copy.start()
        stores.append(copy)
        return copy

    steps = tokens // ROWS
    x_copy.wait()

    @pl.loop(0, steps)
    def _(i):
        rows = tile(i, ROWS)
        values = xs[rows].astype(F32)
        n1[rows] = (values * inverse_rms(values) * gain_attn).astype(BF)

    store(n1, n1_out)
    moves.lead()
    moves.advance(0)

    @pl.loop(0, steps)
    def _(i):
        rows = tile(i, ROWS)
        qs[rows] = ((nn(n1[rows], full[0]) + bias_q) * scale).astype(BF)

    store(qs, q_out)
    moves.advance(1)

    @pl.loop(0, steps)
    def _(i):
        rows = tile(i, ROWS)
        ks[rows] = nn(n1[rows], full[1]).astype(BF)

    store(ks, k_out)
    moves.advance(2)

    @pl.loop(0, steps)
    def _(i):
        rows = tile(i, ROWS)
        vs[rows] = (nn(n1[rows], full[2]) + bias_v).astype(BF)

    v_store = store(vs, v_out)

    @pl.loop(0, tokens // SEQ)
    def _(i):
        rows = tile(i, SEQ)
        allowed = jnp.concatenate([allow_ref[i]] * 8, axis=0)
        for group in range(2):
            part = softmax_packed(pack_scores(ks, qs, rows, group), allowed)
            probs[i, group] = part.astype(BF)
            att[rows, 640 * group : 640 * (group + 1)] = spread(
                part.T.astype(BF), group, vs, rows
            ).astype(BF)

    store(att, att_out)
    store(probs, probs_out)
    moves.advance(3)

    @pl.loop(0, steps)
    def _(i):
        rows = tile(i, ROWS)
        total = xs[rows].astype(F32) + nt(att[rows], full[3]) + bias_o
        res[rows] = total
        n2[rows] = (total * inverse_rms(total) * gain_mlp).astype(BF)

    g_copy.start()
    store(res, res_out)
    store(n2, n2_out)
    moves.advance(4)

    @pl.loop(0, steps)
    def _(i):
        rows = tile(i, ROWS)
        up = nn(n2[rows], full[4]) + bias_up
        square = up * up
        tanh = jnp.tanh(GELU_C * up * (1.0 + 0.044715 * square))
        act[rows] = (0.5 * up * (1.0 + tanh)).astype(BF)
        slope = 0.5 * (1.0 + tanh) + 0.5 * up * (1.0 - tanh * tanh) * (
            GELU_C * (1.0 + 3 * 0.044715 * square)
        )
        gp[rows] = slope.astype(BF)

    store(gp, gp_out)
    g_copy.wait()

    @pl.loop(0, xs.shape[1] // ROWS)
    def _(i):
        cols = tile(i, ROWS)
        gwd[cols] = tn(xs[:, cols], act[...]).astype(BF)

    store(gwd, gwd_out)
    moves.advance(5)
    if remote:
        for k in range(6):
            store(full.at[k], full_out.at[k])

    v_store.wait()

    @pl.loop(0, steps)
    def _(i):
        rows = tile(i, ROWS)
        vs[rows] = (res[rows] + nt(act[rows], full[5]) + bias_down).astype(BF)

    store(vs, y_out)
    for copy in stores:
        if copy is not v_store:
            copy.wait()
    moves.end()


def forward(remote, tokens, x, g, allow, vecs, weights):
    d = x.shape[1]
    big = jax.ShapeDtypeStruct((tokens, d), BF)
    probs = (tokens // SEQ, 2, SEQ, SEQ)
    outs = [jax.ShapeDtypeStruct((6, d, d), BF)] + [big] * 7 + [
        jax.ShapeDtypeStruct((tokens, d), F32),
        jax.ShapeDtypeStruct(probs, BF),
        jax.ShapeDtypeStruct((d, d), BF),
        big,
    ]
    hbm, vmem = pl.BlockSpec(memory_space=pl.ANY), pl.BlockSpec(memory_space=pltpu.VMEM)
    scratch = [pltpu.VMEM((6, d, d), BF)] + [pltpu.VMEM((tokens, d), BF)] * 9
    scratch += [pltpu.VMEM((tokens, d), F32), pltpu.VMEM(probs, BF), pltpu.VMEM((d, d), BF)]
    scratch += [pltpu.SemaphoreType.DMA((6,)), pltpu.SemaphoreType.DMA((2,)), pltpu.SemaphoreType.DMA((20,))]
    if remote:
        scratch += [pltpu.SemaphoreType.DMA((6, 31)), pltpu.SemaphoreType.DMA((6, 32))]
    return pl.pallas_call(
        functools.partial(forward_kernel, remote),
        out_shape=outs,
        in_specs=[hbm, hbm, vmem, vmem] + [hbm] * 6,
        out_specs=[hbm] * len(outs),
        scratch_shapes=scratch,
        compiler_params=pltpu.CompilerParams(
            collective_id=0 if remote else None,
            has_side_effects=remote,
            vmem_limit_bytes=62 * 2**20,
        ),
        name="forward",
    )(x, g, allow, vecs, *weights)


def norm_back(values, gain_vec, grad_in):
    factor = inverse_rms(values)
    inner = jnp.mean(grad_in * gain_vec * values, axis=-1, keepdims=True)
    grad_out = factor * gain_vec * grad_in - values * factor * factor * factor * inner
    return (grad_out, jnp.sum(grad_in * values * factor, axis=0))


def prepare(inputs, segment_ids, w_out, w_down, b_query, b_value, b_out, b_up, b_down, dim_scale, gain_attn, gain_mlp):
    tokens = inputs.shape[0] // lax.axis_size("heads")
    heads = inputs.shape[1] // DH
    start = lax.axis_index("heads") * tokens
    segs = lax.dynamic_slice_in_dim(segment_ids, start, tokens, 0).reshape(tokens // SEQ, 8, PATCHES)
    place = jnp.arange(PATCHES)
    allow = (segs[:, None, :, :] == segs.transpose(0, 2, 1)[:, :, :, None]) & (
        place[None, :, None, None] <= place[None, None, None, :]
    )
    allow = allow.astype(F32).reshape(tokens // SEQ, PATCHES, SEQ)
    scale = QUERY_BASE / math.sqrt(DH) * jax.nn.softplus(dim_scale)
    vecs = jnp.stack([gain_attn, gain_mlp, b_query, b_value, b_out, b_up, b_down, jnp.tile(scale, heads)])
    return tokens, start, allow, vecs


def shards(
    inputs, segment_ids, cotangent, w_query, w_key, w_value, w_out, w_up, w_down,
    b_query, b_value, b_out, b_up, b_down, dim_scale, gain_attn, gain_mlp,
):
    tokens, start, allow, vecs = prepare(
        inputs, segment_ids, w_out, w_down, b_query, b_value, b_out, b_up, b_down, dim_scale, gain_attn, gain_mlp
    )
    remote = lax.axis_size("wide") == 16 and lax.axis_size("heads") == 2
    weights = [w_query, w_key, w_value, w_out.T, w_up, w_down.T]
    if not remote:
        weights = [
            lax.all_gather(lax.all_gather(w, "heads", axis=1, tiled=True), "wide", axis=0, tiled=True) for w in weights
        ]
    full, n1, qs, ks, vs, att, n2, gp, res, probs, gwd, output = forward(
        remote, tokens, inputs, cotangent, allow, vecs, weights
    )
    if not remote:
        full = jnp.stack(weights)
    g = lax.dynamic_slice_in_dim(cotangent, start, tokens, 0)
    x = lax.dynamic_slice_in_dim(inputs, start, tokens, 0).astype(F32)
    gf = g.astype(F32)
    dup = (nn(g, full[5]) * gp.astype(F32)).astype(BF)
    gwu = tn(n2, dup)
    gn2 = nt(dup, full[4])
    back_two, gg2 = norm_back(res, gain_mlp, gn2)
    gres = gf + back_two
    branch = gres.astype(BF)
    gwo = tn(branch, att)
    gatt = nn(branch, full[3]).astype(BF)
    tc = tokens // SEQ
    nh = w_query.shape[0] * 0 + inputs.shape[1] // DH
    shp = (tc, SEQ, nh, DH)
    q4, k4, v4, g4 = (a.reshape(shp) for a in (qs, ks, vs, gatt))
    q6, k6, v6, g6 = (a.reshape(tc, 8, PATCHES, nh, DH) for a in (q4, k4, v4, g4))
    ok = allow.reshape(tc, PATCHES, 8, PATCHES).transpose(0, 2, 3, 1)[:, None] > 0.5
    sc = jnp.where(ok, jnp.einsum("tbihe,tbjhe->thbij", q6, k6, preferred_element_type=F32), -1e30)
    pk = jax.nn.softmax(sc, axis=-1)
    gpr = jnp.einsum("tbihe,tbjhe->thbij", g6, v6, preferred_element_type=F32)
    inner = jnp.sum(pk * gpr, axis=-1, keepdims=True)
    gs = (pk * (gpr - inner)).astype(BF)
    gq = jnp.einsum("thbij,tbjhe->tbihe", gs, k6, preferred_element_type=F32)
    gk = jnp.einsum("thbij,tbihe->tbjhe", gs, q6, preferred_element_type=F32).reshape(tokens, -1).astype(BF)
    gv = jnp.einsum("thbij,tbihe->tbjhe", pk.astype(BF), g6, preferred_element_type=F32).reshape(tokens, -1).astype(BF)
    scale = vecs[7]
    gq = gq.reshape(tokens, -1)
    gdim = jnp.sum((gq * qs.astype(F32) / scale).reshape(tokens, nh, DH), axis=(0, 1)) * QUERY_BASE / math.sqrt(DH) * jax.nn.sigmoid(dim_scale)
    gq = (gq * scale).astype(BF)
    gw = [tn(n1, gq), tn(n1, gk), tn(n1, gv), gwo, gwu, gwd]
    gn1 = nt(gq, full[0]) + nt(gk, full[1]) + nt(gv, full[2])
    back_one, gg1 = norm_back(x, gain_attn, gn1)
    input_grad = gres + back_one
    def scatter(a):
        a = lax.psum_scatter(a.astype(BF), "wide", scatter_dimension=0, tiled=True)
        return lax.psum_scatter(a, "heads", scatter_dimension=1, tiled=True).astype(F32)
    gw = [scatter(a) for a in gw]
    small = lax.psum((gg1, gg2, jnp.sum(gres, axis=0), jnp.sum(gf, axis=0), gdim, jnp.sum(gq.astype(F32), axis=0), jnp.sum(gv.astype(F32), axis=0), jnp.sum(dup.astype(F32), axis=0)), ("wide", "heads"))
    gg1, gg2, gbo, gbd, gdim, gbq, gbv, gbu = small
    return (output, input_grad, gw[0], gw[1], gw[2], gw[3].T, gw[4], gw[5].T, gbq, gbv, gbo, gbu, gbd, gdim, gg1, gg2)


def solution(mesh):
    token, both = P("wide", None), P(("wide", "heads"), None)
    tall, flat = P("wide", "heads"), P("heads", "wide")
    return jax.shard_map(
        shards,
        mesh=mesh,
        in_specs=(token, P("wide"), token, tall, tall, tall, flat, tall, flat) + (P(),) * 8,
        out_specs=(both, both, tall, tall, tall, flat, tall, flat) + (P(),) * 8,
        check_vma=False,
    )
```

```python
import functools
import math

import jax
import jax.numpy as jnp
from jax import lax
from jax.experimental import pallas as pl
from jax.experimental.pallas import tpu as pltpu
from jax.sharding import PartitionSpec as P

DH = 80
PATCHES = 16
EPS = 1e-06
QUERY_BASE = 1.442695041
BF = jnp.bfloat16
F32 = jnp.float32
MESH = pl.DeviceIdType.MESH
ROWS = 256
SEQ = 128
GELU_C = math.sqrt(2.0 / math.pi)


def nn(left, right):
    return jnp.dot(left, right, preferred_element_type=F32)


def nt(left, right):
    return lax.dot_general(left, right, (((1,), (1,)), ((), ())), preferred_element_type=F32)


def tn(left, right):
    return lax.dot_general(left, right, (((0,), (0,)), ((), ())), preferred_element_type=F32)


def inverse_rms(values):
    return lax.rsqrt(jnp.mean(values * values, axis=-1, keepdims=True) + EPS)


def tile(index, size):
    return pl.ds(pl.multiple_of(index * size, size), size)


def head_window(pair):
    return (2 * DH * pair) // 128 * 128


def head_masks(pair):
    lanes = head_window(pair) + lax.broadcasted_iota(jnp.int32, (SEQ, 256), 1)
    picks = []
    for head in (2 * pair, 2 * pair + 1):
        inside = (lanes >= DH * head) & (lanes < DH * (head + 1))
        picks.append(jnp.where(inside, 1.0, 0.0).astype(BF))
    return picks


def block_offset():
    row = lax.broadcasted_iota(jnp.int32, (SEQ, SEQ), 0) // PATCHES
    col = lax.broadcasted_iota(jnp.int32, (SEQ, SEQ), 1) // PATCHES
    return row, col


def roll_rows(values, blocks):
    shift = (blocks % 8) * PATCHES
    if shift == 0:
        return values
    return jnp.concatenate([values[SEQ - shift :], values[: SEQ - shift]], axis=0)


def split_heads(window, masks):
    return jnp.concatenate([window * masks[0], window * masks[1]], axis=0)


def split_rolled(window, masks, slots):
    return jnp.concatenate(
        [roll_rows(window, slots[0]) * masks[0], roll_rows(window, slots[1]) * masks[1]], axis=0
    )


def pack_scores(left_ref, right_ref, rows, group):
    row, col = block_offset()
    offset = lax.rem(row - col + 8, 8)
    packed = jnp.zeros((SEQ, SEQ), F32)
    for pair in range(4 * group, 4 * group + 4):
        win = pl.ds(head_window(pair), 256)
        both = nt(left_ref[rows, win], split_heads(right_ref[rows, win], head_masks(pair)))
        for side in range(2):
            slot = (2 * pair + side) % 8
            one = roll_rows(both[:, SEQ * side : SEQ * (side + 1)], slot)
            packed = jnp.where(offset == slot, one, packed)
    return packed


def spread(packed, group, right_ref, rows):
    row, col = block_offset()
    offset = lax.rem(col - row + 8, 8)
    parts = []
    for pair in range(4 * group, 4 * group + 4):
        slots = (2 * pair % 8, (2 * pair + 1) % 8)
        left = jnp.concatenate(
            [packed * jnp.where(offset == s, 1.0, 0.0).astype(BF) for s in slots], axis=1
        )
        win = pl.ds(head_window(pair), 256)
        parts.append(nn(left, split_rolled(right_ref[rows, win], head_masks(pair), slots)))
    return join_windows(parts)


def join_windows(parts):
    tiles = [parts[0][:, :128]]
    for before, after in zip(parts[:-1], parts[1:]):
        tiles.append(before[:, 128:] + after[:, :128])
    tiles.append(parts[-1][:, 128:])
    return jnp.concatenate(tiles, axis=1)


def softmax_packed(packed, allowed):
    scores = jnp.where(allowed > 0.5, packed, -1e30).reshape(8, PATCHES, SEQ)
    exps = jnp.exp(scores - jnp.max(scores, axis=1, keepdims=True))
    return (exps / jnp.sum(exps, axis=1, keepdims=True)).reshape(SEQ, SEQ)


class Peers:
    def __init__(self):
        wide = lax.axis_index("wide")
        self.y = lax.axis_index("heads")
        self.z = wide // 4
        self.x = lax.rem(wide // 2, 2)
        self.c = lax.rem(wide, 2)

    def device(self, z, x, y, c):
        return ((z * 2 + x) * 2 + c, y)

    def across_x(self):
        return self.device(self.z, 1 - self.x, self.y, self.c)

    def across_y(self):
        return self.device(self.z, self.x, 1 - self.y, self.c)

    def across_core(self):
        return self.device(self.z, self.x, self.y, 1 - self.c)

    def along_z(self, step):
        return self.device(lax.rem(self.z + step, 4), self.x, self.y, self.c)

    def enter(self):
        barrier = pltpu.get_barrier_semaphore()
        others = [self.across_x(), self.across_y(), self.across_core()]
        others += [self.along_z(step) for step in (1, 2, 3)]
        for other in others:
            pl.semaphore_signal(barrier, inc=1, device_id=other, device_id_type=MESH)
        pl.semaphore_wait(barrier, len(others))


class Gather:
    def __init__(self, blocks, full, send_sem, recv_sem, own_sem):
        self.blocks, self.full = blocks, full
        self.send_sem, self.recv_sem, self.own_sem = send_sem, recv_sem, own_sem
        self.peers = Peers()
        self.depth, self.width = blocks[0].shape
        self.sent = [0] * len(blocks)

    def at(self, k, z, x, y, c):
        rows = pl.ds(pl.multiple_of((z * 4 + x * 2 + c) * self.depth, 16), self.depth)
        cols = pl.ds(pl.multiple_of(y * self.width, 128), self.width)
        return self.full.at[k, rows, cols]

    def copy(self, k, place, target, slot, source=None):
        z, x, y, c = place
        there = self.at(k, *place)
        return pltpu.make_async_remote_copy(
            src_ref=there if source is None else source,
            dst_ref=there,
            send_sem=self.send_sem.at[k, slot],
            recv_sem=self.recv_sem.at[k, ((z * 2 + x) * 2 + y) * 2 + c],
            device_id=target,
            device_id_type=MESH,
        )

    def send(self, k, place, target, source=None):
        self.copy(k, place, target, self.sent[k], source).start()
        self.sent[k] += 1

    def arrived(self, k, place):
        self.copy(k, place, self.peers.across_core(), 0).wait_recv()

    def own_copy(self, k):
        p = self.peers
        return pltpu.make_async_copy(self.blocks[k], self.at(k, p.z, p.x, p.y, p.c), self.own_sem.at[k])

    def begin(self):
        p = self.peers
        p.enter()
        own = (p.z, p.x, p.y, p.c)
        for k, block in enumerate(self.blocks):
            for step in (1, 2, 3):
                self.send(k, own, p.along_z(step), block)
            self.send(k, own, p.across_x(), block)
            self.send(k, own, p.across_y(), block)
            self.send(k, own, p.across_core(), block)
            self.own_copy(k).start()

    def from_z(self, k):
        if k >= len(self.blocks):
            return
        p = self.peers
        for step in (1, 3, 2):
            place = (lax.rem(p.z + step, 4), p.x, p.y, p.c)
            self.arrived(k, place)
            for target in (p.across_x(), p.across_y(), p.across_core()):
                self.send(k, place, target)

    def from_plane(self, k):
        if k >= len(self.blocks):
            return
        p = self.peers
        for z in range(4):
            place = (z, 1 - p.x, p.y, p.c)
            self.arrived(k, place)
            if z % 2 == 1:
                self.send(k, place, p.across_y())
            self.send(k, place, p.across_core())
            place = (z, p.x, 1 - p.y, p.c)
            self.arrived(k, place)
            if z % 2 == 0:
                self.send(k, place, p.across_x())
            self.send(k, place, p.across_core())

    def from_corner(self, k):
        p = self.peers
        for z in range(4):
            place = (z, 1 - p.x, 1 - p.y, p.c)
            self.arrived(k, place)
            self.send(k, place, p.across_core())

    def ready(self, k):
        p = self.peers
        self.own_copy(k).wait()
        for z in range(4):
            for x in range(2):
                for y in range(2):
                    self.arrived(k, (z, x, y, 1 - p.c))

    def lead(self):
        self.from_z(0)
        self.from_z(1)
        self.from_plane(0)

    def advance(self, k):
        self.from_z(k + 2)
        self.from_plane(k + 1)
        self.from_corner(k)
        self.ready(k)

    def end(self):
        p = self.peers
        for k in range(len(self.blocks)):
            for slot in range(self.sent[k]):
                self.copy(k, (p.z, p.x, p.y, p.c), p.across_core(), slot).wait_send()


class Loaded:
    def __init__(self, blocks, full, own_sem):
        self.blocks, self.full, self.own_sem = blocks, full, own_sem

    def own_copy(self, k):
        return pltpu.make_async_copy(self.blocks[k], self.full.at[k], self.own_sem.at[k])

    def begin(self):
        for k in range(len(self.blocks)):
            self.own_copy(k).start()

    def lead(self):
        pass

    def advance(self, k):
        self.own_copy(k).wait()

    def end(self):
        pass


def forward_kernel(
    remote,
    x_hbm, g_hbm, allow_ref, vec_ref, w0, w1, w2, w3, w4, w5,
    full_out, n1_out, q_out, k_out, v_out, att_out, n2_out, gp_out, res_out, probs_out, gwd_out, y_out,
    full, xs, n1, qs, ks, vs, att, n2, act, gp, res, probs, gwd,
    own_sem, in_sem, out_sem, *remote_sems,
):
    blocks = (w0, w1, w2, w3, w4, w5)
    tokens = xs.shape[0]
    half = lax.axis_index("heads") * tokens
    x_copy = pltpu.make_async_copy(x_hbm.at[pl.ds(pl.multiple_of(half, 16), tokens)], xs, in_sem.at[0])
    g_copy = pltpu.make_async_copy(g_hbm.at[pl.ds(pl.multiple_of(half, 16), tokens)], xs, in_sem.at[1])
    x_copy.start()
    if remote:
        moves = Gather(blocks, full, *remote_sems, own_sem)
    else:
        moves = Loaded(blocks, full, own_sem)
    moves.begin()
    gain_attn, gain_mlp = vec_ref[0:1], vec_ref[1:2]
    bias_q, bias_v, bias_o = vec_ref[2:3], vec_ref[3:4], vec_ref[4:5]
    bias_up, bias_down, scale = vec_ref[5:6], vec_ref[6:7], vec_ref[7:8]
    stores = []

    def store(source, target):
        copy = pltpu.make_async_copy(source, target, out_sem.at[len(stores)])
        copy.start()
        stores.append(copy)
        return copy

    steps = tokens // ROWS
    x_copy.wait()

    @pl.loop(0, steps)
    def _(i):
        rows = tile(i, ROWS)
        values = xs[rows].astype(F32)
        n1[rows] = (values * inverse_rms(values) * gain_attn).astype(BF)

    store(n1, n1_out)
    moves.lead()
    moves.advance(0)

    @pl.loop(0, steps)
    def _(i):
        rows = tile(i, ROWS)
        qs[rows] = ((nn(n1[rows], full[0]) + bias_q) * scale).astype(BF)

    store(qs, q_out)
    moves.advance(1)

    @pl.loop(0, steps)
    def _(i):
        rows = tile(i, ROWS)
        ks[rows] = nn(n1[rows], full[1]).astype(BF)

    store(ks, k_out)
    moves.advance(2)

    @pl.loop(0, steps)
    def _(i):
        rows = tile(i, ROWS)
        vs[rows] = (nn(n1[rows], full[2]) + bias_v).astype(BF)

    v_store = store(vs, v_out)

    @pl.loop(0, tokens // SEQ)
    def _(i):
        rows = tile(i, SEQ)
        allowed = jnp.concatenate([allow_ref[i]] * 8, axis=0)
        for group in range(2):
            part = softmax_packed(pack_scores(ks, qs, rows, group), allowed)
            probs[i, group] = part.astype(BF)
            att[rows, 640 * group : 640 * (group + 1)] = spread(
                part.T.astype(BF), group, vs, rows
            ).astype(BF)

    store(att, att_out)
    store(probs, probs_out)
    moves.advance(3)

    @pl.loop(0, steps)
    def _(i):
        rows = tile(i, ROWS)
        total = xs[rows].astype(F32) + nt(att[rows], full[3]) + bias_o
        res[rows] = total
        n2[rows] = (total * inverse_rms(total) * gain_mlp).astype(BF)

    g_copy.start()
    store(res, res_out)
    store(n2, n2_out)
    moves.advance(4)

    @pl.loop(0, steps)
    def _(i):
        rows = tile(i, ROWS)
        up = nn(n2[rows], full[4]) + bias_up
        square = up * up
        tanh = jnp.tanh(GELU_C * up * (1.0 + 0.044715 * square))
        act[rows] = (0.5 * up * (1.0 + tanh)).astype(BF)
        slope = 0.5 * (1.0 + tanh) + 0.5 * up * (1.0 - tanh * tanh) * (
            GELU_C * (1.0 + 3 * 0.044715 * square)
        )
        gp[rows] = slope.astype(BF)

    store(gp, gp_out)
    g_copy.wait()

    @pl.loop(0, xs.shape[1] // ROWS)
    def _(i):
        cols = tile(i, ROWS)
        gwd[cols] = tn(xs[:, cols], act[...]).astype(BF)

    store(gwd, gwd_out)
    moves.advance(5)
    if remote:
        for k in range(6):
            store(full.at[k], full_out.at[k])

    v_store.wait()

    @pl.loop(0, steps)
    def _(i):
        rows = tile(i, ROWS)
        vs[rows] = (res[rows] + nt(act[rows], full[5]) + bias_down).astype(BF)

    store(vs, y_out)
    for copy in stores:
        if copy is not v_store:
            copy.wait()
    moves.end()


def forward(remote, tokens, x, g, allow, vecs, weights):
    d = x.shape[1]
    big = jax.ShapeDtypeStruct((tokens, d), BF)
    probs = (tokens // SEQ, 2, SEQ, SEQ)
    outs = [jax.ShapeDtypeStruct((6, d, d), BF)] + [big] * 7 + [
        jax.ShapeDtypeStruct((tokens, d), F32),
        jax.ShapeDtypeStruct(probs, BF),
        jax.ShapeDtypeStruct((d, d), BF),
        big,
    ]
    hbm, vmem = pl.BlockSpec(memory_space=pl.ANY), pl.BlockSpec(memory_space=pltpu.VMEM)
    scratch = [pltpu.VMEM((6, d, d), BF)] + [pltpu.VMEM((tokens, d), BF)] * 9
    scratch += [pltpu.VMEM((tokens, d), F32), pltpu.VMEM(probs, BF), pltpu.VMEM((d, d), BF)]
    scratch += [pltpu.SemaphoreType.DMA((6,)), pltpu.SemaphoreType.DMA((2,)), pltpu.SemaphoreType.DMA((20,))]
    if remote:
        scratch += [pltpu.SemaphoreType.DMA((6, 31)), pltpu.SemaphoreType.DMA((6, 32))]
    return pl.pallas_call(
        functools.partial(forward_kernel, remote),
        out_shape=outs,
        in_specs=[hbm, hbm, vmem, vmem] + [hbm] * 6,
        out_specs=[hbm] * len(outs),
        scratch_shapes=scratch,
        compiler_params=pltpu.CompilerParams(
            collective_id=0 if remote else None,
            has_side_effects=remote,
            vmem_limit_bytes=62 * 2**20,
        ),
        name="forward",
    )(x, g, allow, vecs, *weights)


ORDER = (5, 4, 3, 2, 0, 1)


class Scatter:
    def __init__(self, grads, pair, first_x, first_y, last_x, last_y, own, far, out, out_vmem, send_sem, recv_sem, credit, out_sem):
        self.grads, self.pair, self.own, self.far = grads, pair, own, far
        self.first_x, self.first_y, self.last_x, self.last_y = first_x, first_y, last_x, last_y
        self.out, self.out_vmem, self.out_sem = out, out_vmem, out_sem
        self.send_sem, self.recv_sem, self.credit = send_sem, recv_sem, credit
        self.peers = Peers()
        self.depth, self.width = own.shape[2:]
        self.jobs = len(ORDER)

    def begin(self):
        self.peers.enter()

    def remote(self, j, slot, source, there, target):
        return pltpu.make_async_remote_copy(
            src_ref=source,
            dst_ref=there,
            send_sem=self.send_sem.at[j, slot],
            recv_sem=self.recv_sem.at[j, slot],
            device_id=target,
            device_id_type=MESH,
        )

    def grad(self, j):
        return self.grads.at[j % 2].reshape(8, 2, self.depth, 2 * self.width)

    def half(self, which):
        return pl.ds(pl.multiple_of(which * self.width, 128), self.width)

    def cores(self, j):
        return self.remote(j, 0, self.grad(j).at[:, 1 - self.peers.c], self.pair.at[j % 3], self.peers.across_core())

    def outward(self, j):
        p = self.peers
        sums = self.pair.at[j % 3]
        for n in range(2):
            yield self.remote(j, 1 + n, sums.at[4 * n + 1 - p.x], self.first_x.at[j, n], p.across_x())
        for n in range(2):
            yield self.remote(
                j, 3 + n, sums.at[4 * n + 2 : 4 * n + 4, :, self.half(1 - p.y)], self.first_y.at[j, n], p.across_y()
            )

    def second(self, j, to_y):
        p = self.peers
        if to_y:
            return self.remote(j, 5, self.first_x.at[j, :, :, self.half(1 - p.y)], self.last_y.at[j], p.across_y())
        return self.remote(j, 6, self.first_y.at[j, :, 1 - p.x], self.last_x.at[j], p.across_x())

    def depthward(self, j, step):
        p = self.peers
        z = lax.rem(p.z + step, 4)
        return self.remote(j, 6 + step, self.own.at[j, z], self.far.at[j, 3 - step], p.along_z(step))

    def start(self, j):
        if j >= 3:
            pl.semaphore_wait(self.credit, 1)
        self.cores(j).start()

    def pair_sum(self, j):
        if j < 0 or j >= self.jobs:
            return
        p = self.peers
        self.cores(j).wait_recv()
        mine, sums = self.grad(j), self.pair.at[j % 3]

        @pl.loop(0, 8)
        def _(n):
            sums[n] = (mine[n, p.c].astype(F32) + sums[n].astype(F32)).astype(BF)

        for copy in self.outward(j):
            copy.start()
        self.cores(j).wait_send()

    def plane_x(self, j):
        if j < 0 or j >= self.jobs:
            return
        p = self.peers
        sums = self.pair.at[j % 3]
        first = list(self.outward(j))
        for n in range(2):
            first[n].wait_recv()
        for n in range(2):
            self.first_x[j, n] = (self.first_x[j, n].astype(F32) + sums[4 * n + p.x].astype(F32)).astype(BF)
        self.second(j, True).start()

    def plane_y(self, j):
        if j < 0 or j >= self.jobs:
            return
        p = self.peers
        sums = self.pair.at[j % 3]
        first = list(self.outward(j))
        for n in range(2):
            first[2 + n].wait_recv()
        for n in range(2):
            for x in range(2):
                total = self.first_y[j, n, x].astype(F32) + sums[4 * n + 2 + x, :, self.half(p.y)].astype(F32)
                self.first_y[j, n, x] = total.astype(BF)
        self.second(j, False).start()
        for copy in first:
            copy.wait_send()
        if j + 3 < self.jobs:
            pl.semaphore_signal(self.credit, inc=1, device_id=p.across_core(), device_id_type=MESH)

    def plane_last(self, j):
        if j < 0 or j >= self.jobs:
            return
        p = self.peers
        self.second(j, True).wait_recv()
        for n in range(2):
            total = self.first_x[j, n, :, self.half(p.y)].astype(F32) + self.last_y[j, n].astype(F32)
            self.own[j, 2 * n] = total.astype(BF)
        self.second(j, False).wait_recv()
        for n in range(2):
            total = self.first_y[j, n, p.x].astype(F32) + self.last_x[j, n].astype(F32)
            self.own[j, 2 * n + 1] = total.astype(BF)
        for step in (2, 1, 3):
            self.depthward(j, step).start()

    def finish(self, j):
        if j < 0 or j >= self.jobs:
            return
        p = self.peers
        total = self.own[j, p.z].astype(F32)
        for step in (1, 2, 3):
            self.depthward(j, step).wait_recv()
            total += self.far[j, 3 - step].astype(F32)
        self.out_vmem[j % 2] = total
        pltpu.make_async_copy(self.out_vmem.at[j % 2], self.out.at[ORDER[j]], self.out_sem).start()
        pltpu.make_async_copy(self.out_vmem.at[j % 2], self.out.at[ORDER[j]], self.out_sem).wait()

    def end(self):
        for j in range(self.jobs):
            self.second(j, True).wait_send()
            self.second(j, False).wait_send()
            for step in (1, 2, 3):
                self.depthward(j, step).wait_send()


class Kept:
    def __init__(self, grads, out, sems):
        self.grads, self.out, self.sems = grads, out, sems

    def begin(self):
        pass

    def copy(self, j):
        return pltpu.make_async_copy(self.grads.at[j % 2], self.out.at[ORDER[j]], self.sems.at[j])

    def start(self, j):
        self.copy(j).start()
        self.copy(j).wait()

    def pair_sum(self, j):
        pass

    plane_x = plane_y = plane_last = finish = pair_sum

    def end(self):
        pass


class Totals:
    def __init__(self, sums, got, far, send_sem, recv_sem):
        self.sums, self.got, self.far, self.send_sem, self.recv_sem = sums, got, far, send_sem, recv_sem
        self.peers = Peers()

    def copy(self, n, source, there, target):
        return pltpu.make_async_remote_copy(
            src_ref=source, dst_ref=there, send_sem=self.send_sem.at[n], recv_sem=self.recv_sem.at[n],
            device_id=target, device_id_type=MESH,
        )

    def pair(self, n):
        target = (self.peers.across_core, self.peers.across_x, self.peers.across_y)[n]()
        return self.copy(n, self.sums.at[n], self.got.at[n], target)

    def along(self, step):
        z = self.peers.z
        return self.copy(2 + step, self.sums.at[3], self.far.at[z], self.peers.along_z(step))

    def coming(self, step):
        z = lax.rem(self.peers.z - step + 4, 4)
        return self.copy(2 + step, self.sums.at[3], self.far.at[z], self.peers.along_z(step))

    def start(self, n):
        if n < 3:
            self.pair(n).start()
            return
        self.far[self.peers.z] = self.sums[3]
        for step in (1, 2, 3):
            self.along(step).start()

    def take(self, n):
        if n < 3:
            self.pair(n).wait_recv()
            self.sums[n + 1] = self.sums[n] + self.got[n]
            return None
        for step in (1, 2, 3):
            self.coming(step).wait_recv()
        return (self.far[0] + self.far[1]) + (self.far[2] + self.far[3])

    def end(self):
        for n in range(3):
            self.pair(n).wait_send()
        for step in (1, 2, 3):
            self.along(step).wait_send()


def gather_back(packed, group, right_ref, rows):
    row, col = block_offset()
    diagonal = jnp.where(row == col, 1.0, 0.0).astype(BF)
    parts = []
    for pair in range(4 * group, 4 * group + 4):
        left = jnp.concatenate(
            [roll_rows(packed, -(2 * pair + side)) * diagonal for side in range(2)], axis=1
        )
        win = pl.ds(head_window(pair), 256)
        parts.append(nn(left, split_heads(right_ref[rows, win], head_masks(pair))))
    return join_windows(parts)


def norm_back(values, gain, grad_in):
    factor = inverse_rms(values)
    inner = jnp.mean(grad_in * gain * values, axis=-1, keepdims=True)
    grad_out = factor * gain * grad_in - values * (factor * factor * factor * inner)
    return grad_out, jnp.sum(grad_in * values * factor, axis=0, keepdims=True)


def add_to(ref, row, cols, values):
    ref[row : row + 1, cols] = ref[row : row + 1, cols] + values


def backward_kernel(
    remote,
    x_hbm, g_hbm, vec_ref, full_hbm, n1_hbm, q_hbm, k_hbm, v_hbm, att_hbm, n2_hbm, gp_hbm, res_hbm, probs_hbm, gwd_hbm,
    in_grad_out, weight_out, sums_out,
    grads, held, res, gs, ups, n2, att, qs, ks, vs, probs, sums,
    in_sem, out_sem, *rest,
):
    tokens, width = gs.shape
    half = pl.multiple_of(lax.axis_index("heads") * tokens, 16)
    count = [0]

    def load(source, target):
        copy = pltpu.make_async_copy(source, target, in_sem.at[count[0]])
        count[0] += 1
        copy.start()
        return copy

    gwd_in = load(gwd_hbm, grads.at[0])
    g_in = load(g_hbm.at[pl.ds(half, tokens)], gs)
    gp_in = load(gp_hbm, ups)
    down_in = load(full_hbm.at[5], held.at[0])
    n2_in = load(n2_hbm, n2)
    up_in = load(full_hbm.at[4], held.at[1])
    res_in = load(res_hbm, res)
    att_in = load(att_hbm, att)
    out_in = load(full_hbm.at[3], held.at[2])
    v_in = load(v_hbm, vs)
    q_in = load(q_hbm, qs)
    k_in = load(k_hbm, ks)
    probs_in = load(probs_hbm, probs)
    if remote:
        moves = Scatter(grads, *rest[:7], weight_out, *rest[7:12])
        totals = Totals(sums, *rest[12:16])
    else:
        moves, totals = Kept(grads, weight_out, rest[0]), None
    moves.begin()
    gain_attn, gain_mlp, scale = vec_ref[0:1], vec_ref[1:2], vec_ref[7:8]
    steps = tokens // ROWS
    every = slice(None)
    sums[...] = jnp.zeros_like(sums)
    small = sums.at[0]
    gwd_in.wait()
    moves.start(0)
    g_in.wait()
    gp_in.wait()
    down_in.wait()

    @pl.loop(0, steps)
    def _(i):
        rows = tile(i, ROWS)
        grad_up = (nn(gs[rows], held[0]) * ups[rows].astype(F32)).astype(BF)
        ups[rows] = grad_up
        add_to(small, 7, every, jnp.sum(grad_up.astype(F32), axis=0, keepdims=True))
        add_to(small, 3, every, jnp.sum(gs[rows].astype(F32), axis=0, keepdims=True))

    moves.pair_sum(0)
    query_in = load(full_hbm.at[0], held.at[0])
    n2_in.wait()

    @pl.loop(0, width // ROWS)
    def _(i):
        cols = tile(i, ROWS)
        grads[1, cols] = tn(n2[:, cols], ups[...]).astype(BF)

    moves.start(1)
    up_in.wait()
    res_in.wait()

    @pl.loop(0, steps)
    def _(i):
        rows = tile(i, ROWS)
        values = res[rows]
        back, gain_sum = norm_back(values, gain_mlp, nt(ups[rows], held[1]))
        total = gs[rows].astype(F32) + back
        res[rows] = total
        n2[rows] = total.astype(BF)
        add_to(small, 1, every, gain_sum)
        add_to(small, 2, every, jnp.sum(total, axis=0, keepdims=True))

    moves.pair_sum(1)
    key_in = load(full_hbm.at[1], held.at[1])
    n1_in = load(n1_hbm, ups)
    att_in.wait()

    @pl.loop(0, width // ROWS)
    def _(i):
        cols = tile(i, ROWS)
        grads[0, cols] = tn(n2[:, cols], att[...]).astype(BF)

    moves.start(2)
    moves.plane_x(0)
    moves.plane_y(0)
    out_in.wait()

    @pl.loop(0, steps)
    def _(i):
        rows = tile(i, ROWS)
        gs[rows] = nn(n2[rows], held[2]).astype(BF)

    value_in = load(full_hbm.at[2], held.at[2])
    x_in = load(x_hbm.at[pl.ds(half, tokens)], att)
    moves.pair_sum(2)
    v_in.wait()
    q_in.wait()
    k_in.wait()
    probs_in.wait()

    def attention(first, last):
        @pl.loop(first, last)
        def _(i):
            rows = tile(i, SEQ)
            for group in range(2):
                cols = slice(640 * group, 640 * (group + 1))
                soft = probs[i, group]
                grad_soft = pack_scores(vs, gs, rows, group).reshape(8, PATCHES, SEQ)
                soft_f = soft.astype(F32).reshape(8, PATCHES, SEQ)
                inner = jnp.sum(soft_f * grad_soft, axis=1, keepdims=True)
                grad_scores = (soft_f * (grad_soft - inner)).reshape(SEQ, SEQ)
                by_query = grad_scores.T.astype(BF)
                by_key = grad_scores.astype(BF)
                grad_q = spread(by_query, group, ks, rows)
                grad_k = gather_back(by_key, group, qs, rows).astype(BF)
                grad_v = gather_back(soft, group, gs, rows).astype(BF)
                add_to(small, 4, cols, jnp.sum(grad_q * qs[rows, cols].astype(F32), axis=0, keepdims=True))
                grad_q = (grad_q * scale[:, cols]).astype(BF)
                add_to(small, 5, cols, jnp.sum(grad_q.astype(F32), axis=0, keepdims=True))
                add_to(small, 6, cols, jnp.sum(grad_v.astype(F32), axis=0, keepdims=True))
                qs[rows, cols] = grad_q
                ks[rows, cols] = grad_k
                vs[rows, cols] = grad_v

    tiles = tokens // SEQ
    attention(0, tiles // 4)
    moves.plane_last(0)
    moves.plane_x(1)
    moves.plane_y(1)
    attention(tiles // 4, tiles // 2)
    moves.plane_last(1)
    attention(tiles // 2, 3 * tiles // 4)
    moves.plane_x(2)
    moves.plane_y(2)
    attention(3 * tiles // 4, tiles)
    moves.finish(0)
    n1_in.wait()

    def project(slot, values):
        @pl.loop(0, width // ROWS)
        def _(i):
            cols = tile(i, ROWS)
            grads[slot, cols] = tn(ups[:, cols], values[...]).astype(BF)

    project(1, vs)
    moves.start(3)
    moves.plane_last(2)
    moves.finish(1)
    project(0, qs)
    moves.start(4)
    moves.pair_sum(3)
    moves.pair_sum(4)
    project(1, ks)
    moves.start(5)
    moves.plane_x(3)
    moves.plane_y(3)
    moves.pair_sum(5)
    moves.finish(2)
    query_in.wait()
    key_in.wait()
    value_in.wait()
    x_in.wait()

    def enter(first, last):
        @pl.loop(first, last)
        def _(i):
            rows = tile(i, ROWS)
            grad_norm = nt(qs[rows], held[0]) + nt(ks[rows], held[1]) + nt(vs[rows], held[2])
            back, gain_sum = norm_back(att[rows].astype(F32), gain_attn, grad_norm)
            res[rows] = res[rows] + back
            add_to(small, 0, every, gain_sum)

    enter(0, steps // 2)
    moves.plane_last(3)
    moves.plane_x(4)
    moves.plane_y(4)
    enter(steps // 2, steps)
    in_grad = pltpu.make_async_copy(res, in_grad_out, out_sem.at[0])
    in_grad.start()
    if remote:
        totals.start(0)
    moves.plane_x(5)
    moves.plane_y(5)
    if remote:
        totals.take(0)
        totals.start(1)
    moves.plane_last(4)
    moves.finish(3)
    if remote:
        totals.take(1)
        totals.start(2)
    moves.plane_last(5)
    moves.finish(4)
    if remote:
        totals.take(2)
        totals.start(3)
    moves.finish(5)
    if remote:
        sums_out[...] = totals.take(3)
    else:
        sums_out[...] = sums[0]
    in_grad.wait()
    moves.end()
    if remote:
        totals.end()


def backward(remote, tokens, x, g, vecs, full, n1, qs, ks, vs, att, n2, gp, res, probs, gwd):
    d = x.shape[1]
    hbm, vmem = pl.BlockSpec(memory_space=pl.ANY), pl.BlockSpec(memory_space=pltpu.VMEM)
    depth, width = (d // lax.axis_size("wide"), d // lax.axis_size("heads")) if remote else (d, d)
    big = pltpu.VMEM((tokens, d), BF)
    jobs = len(ORDER)
    dma, regular = pltpu.SemaphoreType.DMA, pltpu.SemaphoreType.REGULAR
    scratch = [
        pltpu.VMEM((2, d, d), BF), pltpu.VMEM((3, d, d), BF), pltpu.VMEM((tokens, d), F32),
        big, big, big, big, big, big, big, pltpu.VMEM(probs.shape, BF), pltpu.VMEM((4, 8, d), F32),
        dma((20,)), dma((1,)),
    ]
    if remote:
        block = (depth, width)
        scratch += [
            pltpu.VMEM((3, 8, depth, d), BF),
            pltpu.VMEM((jobs, 2, depth, d), BF), pltpu.VMEM((jobs, 2, 2) + block, BF),
            pltpu.VMEM((jobs, 2) + block, BF), pltpu.VMEM((jobs, 2) + block, BF),
            pltpu.VMEM((jobs, 4) + block, BF), pltpu.VMEM((jobs, 3) + block, BF),
            pltpu.VMEM((2,) + block, F32),
            dma((jobs, 10)), dma((jobs, 10)), regular, dma,
            pltpu.VMEM((3, 8, d), F32), pltpu.VMEM((4, 8, d), F32), dma((6,)), dma((6,)),
        ]
    else:
        scratch += [dma((jobs,))]
    weights = jax.ShapeDtypeStruct((jobs, depth, width), F32 if remote else BF)
    return pl.pallas_call(
        functools.partial(backward_kernel, remote),
        out_shape=[jax.ShapeDtypeStruct((tokens, d), F32), weights, jax.ShapeDtypeStruct((8, d), F32)],
        in_specs=[hbm, hbm, vmem] + [hbm] * 11,
        out_specs=[hbm, hbm, vmem],
        scratch_shapes=scratch,
        compiler_params=pltpu.CompilerParams(
            collective_id=1 if remote else None,
            has_side_effects=remote,
            vmem_limit_bytes=63 * 2**20,
        ),
        name="backward",
    )(x, g, vecs, full, n1, qs, ks, vs, att, n2, gp, res, probs, gwd)


def prepare(inputs, segment_ids, w_out, w_down, b_query, b_value, b_out, b_up, b_down, dim_scale, gain_attn, gain_mlp):
    tokens = inputs.shape[0] // lax.axis_size("heads")
    heads = inputs.shape[1] // DH
    start = lax.axis_index("heads") * tokens
    segs = lax.dynamic_slice_in_dim(segment_ids, start, tokens, 0).reshape(tokens // SEQ, 8, PATCHES)
    place = jnp.arange(PATCHES)
    allow = (segs[:, None, :, :] == segs.transpose(0, 2, 1)[:, :, :, None]) & (
        place[None, :, None, None] <= place[None, None, None, :]
    )
    allow = allow.astype(F32).reshape(tokens // SEQ, PATCHES, SEQ)
    scale = QUERY_BASE / math.sqrt(DH) * jax.nn.softplus(dim_scale)
    vecs = jnp.stack([gain_attn, gain_mlp, b_query, b_value, b_out, b_up, b_down, jnp.tile(scale, heads)])
    return tokens, start, allow, vecs


def shards(
    inputs, segment_ids, cotangent, w_query, w_key, w_value, w_out, w_up, w_down,
    b_query, b_value, b_out, b_up, b_down, dim_scale, gain_attn, gain_mlp,
):
    tokens, start, allow, vecs = prepare(
        inputs, segment_ids, w_out, w_down, b_query, b_value, b_out, b_up, b_down, dim_scale, gain_attn, gain_mlp
    )
    remote = lax.axis_size("wide") == 16 and lax.axis_size("heads") == 2
    weights = [w_query, w_key, w_value, w_out.T, w_up, w_down.T]
    if not remote:
        weights = [
            lax.all_gather(lax.all_gather(w, "heads", axis=1, tiled=True), "wide", axis=0, tiled=True) for w in weights
        ]
    full, n1, qs, ks, vs, att, n2, gp, res, probs, gwd, output = forward(
        remote, tokens, inputs, cotangent, allow, vecs, weights
    )
    if not remote:
        full = jnp.stack(weights)
    input_grad, grads, sums = backward(
        remote, tokens, inputs, cotangent, vecs, full, n1, qs, ks, vs, att, n2, gp, res, probs, gwd
    )
    if not remote:
        grads = lax.psum_scatter(grads, "wide", scatter_dimension=1, tiled=True)
        grads = lax.psum_scatter(grads, "heads", scatter_dimension=2, tiled=True).astype(F32)
        sums = lax.psum(sums, ("wide", "heads"))
    scaled = jnp.sum((sums[4] / vecs[7]).reshape(-1, DH), axis=0)
    grad_dim = scaled * (QUERY_BASE / math.sqrt(DH)) * jax.nn.sigmoid(dim_scale)
    return (
        output, input_grad, grads[0], grads[1], grads[2], grads[3].T, grads[4], grads[5].T,
        sums[5], sums[6], sums[2], sums[7], sums[3], grad_dim, sums[0], sums[1],
    )


def solution(mesh):
    token, both = P("wide", None), P(("wide", "heads"), None)
    tall, flat = P("wide", "heads"), P("heads", "wide")
    return jax.shard_map(
        shards,
        mesh=mesh,
        in_specs=(token, P("wide"), token, tall, tall, tall, flat, tall, flat) + (P(),) * 8,
        out_specs=(both, both, tall, tall, tall, flat, tall, flat) + (P(),) * 8,
        check_vma=False,
    )
```

```python
import functools
import math

import jax
import jax.numpy as jnp
from jax import lax
from jax.experimental import pallas as pl
from jax.experimental.pallas import tpu as pltpu
from jax.sharding import PartitionSpec as P

DH = 80
PATCHES = 16
EPS = 1e-06
QUERY_BASE = 1.442695041
BF = jnp.bfloat16
F32 = jnp.float32
MESH = pl.DeviceIdType.MESH
ROWS = 256
SEQ = 128
GELU_C = math.sqrt(2.0 / math.pi)


def nn(left, right):
    return jnp.dot(left, right, preferred_element_type=F32)


def nt(left, right):
    return lax.dot_general(left, right, (((1,), (1,)), ((), ())), preferred_element_type=F32)


def tn(left, right):
    return lax.dot_general(left, right, (((0,), (0,)), ((), ())), preferred_element_type=F32)


def inverse_rms(values):
    return lax.rsqrt(jnp.mean(values * values, axis=-1, keepdims=True) + EPS)


def tile(index, size):
    return pl.ds(pl.multiple_of(index * size, size), size)


def head_window(pair):
    return (2 * DH * pair) // 128 * 128


def head_masks(pair):
    lanes = head_window(pair) + lax.broadcasted_iota(jnp.int32, (SEQ, 256), 1)
    picks = []
    for head in (2 * pair, 2 * pair + 1):
        inside = (lanes >= DH * head) & (lanes < DH * (head + 1))
        picks.append(jnp.where(inside, 1.0, 0.0).astype(BF))
    return picks


def block_offset():
    row = lax.broadcasted_iota(jnp.int32, (SEQ, SEQ), 0) // PATCHES
    col = lax.broadcasted_iota(jnp.int32, (SEQ, SEQ), 1) // PATCHES
    return row, col


def roll_rows(values, blocks):
    shift = (blocks % 8) * PATCHES
    if shift == 0:
        return values
    return jnp.concatenate([values[SEQ - shift :], values[: SEQ - shift]], axis=0)


def split_heads(window, masks):
    return jnp.concatenate([window * masks[0], window * masks[1]], axis=0)


def split_rolled(window, masks, slots):
    return jnp.concatenate(
        [roll_rows(window, slots[0]) * masks[0], roll_rows(window, slots[1]) * masks[1]], axis=0
    )


def pack_scores(left_ref, right_ref, rows, group):
    row, col = block_offset()
    offset = lax.rem(row - col + 8, 8)
    packed = jnp.zeros((SEQ, SEQ), F32)
    for pair in range(4 * group, 4 * group + 4):
        win = pl.ds(head_window(pair), 256)
        both = nt(left_ref[rows, win], split_heads(right_ref[rows, win], head_masks(pair)))
        for side in range(2):
            slot = (2 * pair + side) % 8
            one = roll_rows(both[:, SEQ * side : SEQ * (side + 1)], slot)
            packed = jnp.where(offset == slot, one, packed)
    return packed


def spread(packed, group, right_ref, rows):
    row, col = block_offset()
    offset = lax.rem(col - row + 8, 8)
    parts = []
    for pair in range(4 * group, 4 * group + 4):
        slots = (2 * pair % 8, (2 * pair + 1) % 8)
        left = jnp.concatenate(
            [packed * jnp.where(offset == s, 1.0, 0.0).astype(BF) for s in slots], axis=1
        )
        win = pl.ds(head_window(pair), 256)
        parts.append(nn(left, split_rolled(right_ref[rows, win], head_masks(pair), slots)))
    return join_windows(parts)


def join_windows(parts):
    tiles = [parts[0][:, :128]]
    for before, after in zip(parts[:-1], parts[1:]):
        tiles.append(before[:, 128:] + after[:, :128])
    tiles.append(parts[-1][:, 128:])
    return jnp.concatenate(tiles, axis=1)


def softmax_packed(packed, allowed):
    scores = jnp.where(allowed > 0.5, packed, -1e30).reshape(8, PATCHES, SEQ)
    exps = jnp.exp(scores - jnp.max(scores, axis=1, keepdims=True))
    return (exps / jnp.sum(exps, axis=1, keepdims=True)).reshape(SEQ, SEQ)


class Peers:
    def __init__(self):
        wide = lax.axis_index("wide")
        self.y = lax.axis_index("heads")
        self.z = wide // 4
        self.x = lax.rem(wide // 2, 2)
        self.c = lax.rem(wide, 2)

    def device(self, z, x, y, c):
        return ((z * 2 + x) * 2 + c, y)

    def across_x(self):
        return self.device(self.z, 1 - self.x, self.y, self.c)

    def across_y(self):
        return self.device(self.z, self.x, 1 - self.y, self.c)

    def across_core(self):
        return self.device(self.z, self.x, self.y, 1 - self.c)

    def along_z(self, step):
        return self.device(lax.rem(self.z + step, 4), self.x, self.y, self.c)

    def enter(self):
        barrier = pltpu.get_barrier_semaphore()
        others = [self.across_x(), self.across_y(), self.across_core()]
        others += [self.along_z(step) for step in (1, 2, 3)]
        for other in others:
            pl.semaphore_signal(barrier, inc=1, device_id=other, device_id_type=MESH)
        pl.semaphore_wait(barrier, len(others))


class Gather:
    SLOTS = 37

    def __init__(self, blocks, full, send_sem, recv_sem, own_sem):
        self.blocks, self.full = blocks, full
        self.send_sem, self.recv_sem, self.own_sem = send_sem, recv_sem, own_sem
        self.peers = Peers()
        self.depth, self.width = blocks[0].shape
        self.closed = set()

    def at(self, k, z, x, y, c):
        rows = pl.ds(pl.multiple_of((z * 4 + x * 2 + c) * self.depth, 16), self.depth)
        cols = pl.ds(pl.multiple_of(y * self.width, 128), self.width)
        return self.full.at[k, rows, cols]

    def copy(self, k, place, target, slot, source=None):
        z, x, y, c = place
        there = self.at(k, *place)
        return pltpu.make_async_remote_copy(
            src_ref=there if source is None else source,
            dst_ref=there,
            send_sem=self.send_sem.at[k, slot],
            recv_sem=self.recv_sem.at[k, ((z * 2 + x) * 2 + y) * 2 + c],
            device_id=target,
            device_id_type=MESH,
        )

    def send(self, k, place, target, slot, source=None):
        self.copy(k, place, target, slot, source).start()

    def arrived(self, k, place):
        self.copy(k, place, self.peers.across_core(), 0).wait_recv()

    def own_copy(self, k):
        p = self.peers
        return pltpu.make_async_copy(self.blocks[k], self.at(k, p.z, p.x, p.y, p.c), self.own_sem.at[k])

    def launch(self, k):
        p, block = self.peers, self.blocks[k]
        own = (p.z, p.x, p.y, p.c)
        for side in (1, -1):
            @pl.when(self.inside(p.z + side))
            def _():
                self.send(k, own, p.device(p.z + side, p.x, p.y, p.c), self.z_slot(0, side), block)
        self.send(k, own, p.across_x(), 0, block)
        self.send(k, own, p.across_y(), 1, block)
        self.send(k, own, p.across_core(), 2, block)
        self.own_copy(k).start()

    def inside(self, z):
        return (z >= 0) & (z < 4)

    def z_slot(self, hop, side):
        return 3 + 2 * hop + (1 if side > 0 else 0)

    def from_z(self, k, hop):
        p = self.peers
        for side in (1, -1):
            z = p.z - side * hop
            place = (z, p.x, p.y, p.c)

            @pl.when(self.inside(z))
            def _():
                self.arrived(k, place)
                if hop < 3:
                    @pl.when(self.inside(p.z + side))
                    def _():
                        self.send(k, place, p.device(p.z + side, p.x, p.y, p.c), self.z_slot(hop, side))
                self.send(k, place, p.across_x(), 9 + z)
                self.send(k, place, p.across_y(), 13 + z)
                self.send(k, place, p.across_core(), 17 + z)

    def from_plane(self, k):
        p = self.peers
        for z in range(4):
            place = (z, 1 - p.x, p.y, p.c)
            self.arrived(k, place)
            if z % 2 == 1:
                self.send(k, place, p.across_y(), 29 + z)
            self.send(k, place, p.across_core(), 21 + z)
            place = (z, p.x, 1 - p.y, p.c)
            self.arrived(k, place)
            if z % 2 == 0:
                self.send(k, place, p.across_x(), 29 + z)
            self.send(k, place, p.across_core(), 25 + z)

    def from_corner(self, k):
        p = self.peers
        for z in range(4):
            place = (z, 1 - p.x, 1 - p.y, p.c)
            self.arrived(k, place)
            self.send(k, place, p.across_core(), 33 + z)

    def ready(self, k):
        p = self.peers
        self.own_copy(k).wait()
        for z in range(4):
            for x in range(2):
                for y in range(2):
                    self.arrived(k, (z, x, y, 1 - p.c))

    def close(self, k):
        if k in self.closed:
            return
        self.closed.add(k)
        p = self.peers
        own = (p.z, p.x, p.y, p.c)

        def sent(slot):
            self.copy(k, own, p.across_core(), slot).wait_send()

        for slot in (0, 1, 2) + tuple(range(21, 37)):
            sent(slot)
        for step in (1, 2, 3):
            z = lax.rem(p.z + step, 4)
            for base in (9, 13, 17):
                sent(base + z)
        for hop in range(3):
            for side in (1, -1):
                @pl.when(self.inside(p.z - side * hop) & self.inside(p.z + side))
                def _():
                    sent(self.z_slot(hop, side))


class Loaded:
    def __init__(self, blocks, full, own_sem):
        self.blocks, self.full, self.own_sem = blocks, full, own_sem

    def own_copy(self, k):
        return pltpu.make_async_copy(self.blocks[k], self.full.at[k], self.own_sem.at[k])

    def launch(self, k):
        self.own_copy(k).start()

    def from_z(self, *_):
        pass

    from_plane = from_corner = close = from_z

    def ready(self, k):
        self.own_copy(k).wait()


ORDER = (5, 4, 3, 2, 0, 1)
JOBS = len(ORDER)


class Scatter:
    def __init__(self, full, outs, first_x, first_y, last_x, last_y, own, far, out_vmem, send_sem, recv_sem, credit, out_sem):
        self.full, self.own, self.far, self.outs = full, own, far, outs
        self.first_x, self.first_y, self.last_x, self.last_y = first_x, first_y, last_x, last_y
        self.out_vmem, self.out_sem = out_vmem, out_sem
        self.send_sem, self.recv_sem, self.credit = send_sem, recv_sem, credit
        self.peers = Peers()
        self.depth, self.width = own.shape[2:]
        self.left = [4] * JOBS
        self.sent = set()

    def remote(self, j, slot, source, there, target):
        return pltpu.make_async_remote_copy(
            src_ref=source,
            dst_ref=there,
            send_sem=self.send_sem.at[j, slot],
            recv_sem=self.recv_sem.at[j, slot],
            device_id=target,
            device_id_type=MESH,
        )

    def grad(self, j):
        return self.full.at[j % 2].reshape(8, 2, self.depth, 2 * self.width)

    def pair(self, j):
        return self.full.at[2].reshape(2, 8, self.depth, 2 * self.width).at[j % 2]

    def half(self, which):
        return pl.ds(pl.multiple_of(which * self.width, 128), self.width)

    def cores(self, j):
        return self.remote(j, 0, self.grad(j).at[:, 1 - self.peers.c], self.pair(j), self.peers.across_core())

    def out_x(self, j, n):
        p = self.peers
        return self.remote(j, 1 + n, self.pair(j).at[2 * n + 1 - p.x], self.first_x.at[j, n], p.across_x())

    def out_y(self, j, n):
        p = self.peers
        z = 3 - n
        return self.remote(
            j, 3 + n, self.pair(j).at[2 * z : 2 * z + 2, :, self.half(1 - p.y)], self.first_y.at[j, n], p.across_y()
        )

    def then_y(self, j, n):
        p = self.peers
        return self.remote(j, 5 + n, self.first_x.at[j, n, :, self.half(1 - p.y)], self.last_y.at[j, n], p.across_y())

    def then_x(self, j, n):
        p = self.peers
        return self.remote(j, 7 + n, self.first_y.at[j, n, 1 - p.x], self.last_x.at[j, n], p.across_x())

    def along(self, j, z):
        p = self.peers
        place = lax.rem(p.z - z + 4, 4) - 1
        return self.remote(j, 9 + place, self.own.at[j % 3, z], self.far.at[j, place], p.device(z, p.x, p.y, p.c))

    def open(self):
        pl.semaphore_signal(self.credit, inc=2, device_id=self.peers.across_core(), device_id_type=MESH)

    def start(self, j):
        pl.semaphore_wait(self.credit, 1)
        self.cores(j).start()

    def pair_sum(self, j):
        p = self.peers
        self.cores(j).wait_recv()
        mine, sums = self.grad(j), self.pair(j)

        @pl.loop(0, 8)
        def _(n):
            sums[n] = (mine[n, p.c].astype(F32) + sums[n].astype(F32)).astype(BF)

        for n in range(2):
            self.out_x(j, n).start()
            self.out_y(j, n).start()
        self.cores(j).wait_send()

    def used(self, j):
        self.left[j] -= 1
        if self.left[j] == 0:
            for n in range(2):
                self.out_x(j, n).wait_send()
                self.out_y(j, n).wait_send()
            if j + 2 < JOBS:
                pl.semaphore_signal(self.credit, inc=1, device_id=self.peers.across_core(), device_id_type=MESH)

    def plane_x(self, j, n):
        p = self.peers
        self.out_x(j, n).wait_recv()
        total = self.first_x[j, n].astype(F32) + self.pair(j)[2 * n + p.x].astype(F32)
        self.first_x[j, n] = total.astype(BF)
        self.then_y(j, n).start()
        self.used(j)

    def plane_y(self, j, n):
        p = self.peers
        self.out_y(j, n).wait_recv()
        for x in range(2):
            mine = self.pair(j)[2 * (3 - n) + x, :, self.half(p.y)]
            self.first_y[j, n, x] = (self.first_y[j, n, x].astype(F32) + mine.astype(F32)).astype(BF)
        self.then_x(j, n).start()
        self.used(j)

    def all_sent(self, j):
        if j >= 0 and j not in self.sent:
            self.sent.add(j)
            for step in (1, 2, 3):
                self.along(j, lax.rem(self.peers.z + step, 4)).wait_send()

    def plane_last(self, j, n):
        p = self.peers
        self.all_sent(j - 3)
        self.then_y(j, n).wait_recv()
        total = self.first_x[j, n, :, self.half(p.y)].astype(F32) + self.last_y[j, n].astype(F32)
        self.own[j % 3, n] = total.astype(BF)
        self.then_x(j, n).wait_recv()
        total = self.first_y[j, n, p.x].astype(F32) + self.last_x[j, n].astype(F32)
        self.own[j % 3, 3 - n] = total.astype(BF)
        for z in (n, 3 - n):
            @pl.when(p.z != z)
            def _():
                self.along(j, z).start()

    def out_copy(self, j):
        return pltpu.make_async_copy(self.out_vmem.at[j], self.outs[ORDER[j]], self.out_sem.at[j])

    def finish(self, j):
        p = self.peers
        total = self.own[j % 3, p.z].astype(F32)
        for step in (1, 2, 3):
            self.along(j, lax.rem(p.z + 4 - step, 4)).wait_recv()
        for place in range(3):
            total += self.far[j, place].astype(F32)
        self.out_vmem[j] = total
        self.out_copy(j).start()

    def end(self):
        p = self.peers
        for j in range(JOBS):
            for n in range(2):
                self.then_y(j, n).wait_send()
                self.then_x(j, n).wait_send()
            self.all_sent(j)
            self.out_copy(j).wait()


class Kept:
    def __init__(self, full, outs, sems):
        self.full, self.outs, self.sems = full, outs, sems

    def copy(self, j):
        return pltpu.make_async_copy(self.full.at[j % 2], self.outs[ORDER[j]], self.sems.at[j])

    def start(self, j):
        self.copy(j).start()

    def pair_sum(self, j):
        self.copy(j).wait()

    def open(self, *_):
        pass

    plane_x = plane_y = plane_last = finish = end = open


class Totals:
    def __init__(self, sums, got, far, send_sem, recv_sem):
        self.sums, self.got, self.far, self.send_sem, self.recv_sem = sums, got, far, send_sem, recv_sem
        self.peers = Peers()

    def copy(self, n, source, there, target):
        return pltpu.make_async_remote_copy(
            src_ref=source, dst_ref=there, send_sem=self.send_sem.at[n], recv_sem=self.recv_sem.at[n],
            device_id=target, device_id_type=MESH,
        )

    def pair(self, n):
        target = (self.peers.across_core, self.peers.across_x, self.peers.across_y)[n]()
        return self.copy(n, self.sums.at[n], self.got.at[n], target)

    def along(self, step):
        z = self.peers.z
        return self.copy(2 + step, self.sums.at[3], self.far.at[z], self.peers.along_z(step))

    def coming(self, step):
        z = lax.rem(self.peers.z - step + 4, 4)
        return self.copy(2 + step, self.sums.at[3], self.far.at[z], self.peers.along_z(step))

    def start(self, n):
        if n < 3:
            self.pair(n).start()
            return
        self.far[self.peers.z] = self.sums[3]
        for step in (1, 2, 3):
            self.along(step).start()

    def take(self, n):
        if n < 3:
            self.pair(n).wait_recv()
            self.sums[n + 1] = self.sums[n] + self.got[n]
            return None
        for step in (1, 2, 3):
            self.coming(step).wait_recv()
        return (self.far[0] + self.far[1]) + (self.far[2] + self.far[3])

    def end(self):
        for n in range(3):
            self.pair(n).wait_send()
        for step in (1, 2, 3):
            self.along(step).wait_send()


def gather_back(packed, group, right_ref, rows):
    row, col = block_offset()
    diagonal = jnp.where(row == col, 1.0, 0.0).astype(BF)
    parts = []
    for pair in range(4 * group, 4 * group + 4):
        left = jnp.concatenate(
            [roll_rows(packed, -(2 * pair + side)) * diagonal for side in range(2)], axis=1
        )
        win = pl.ds(head_window(pair), 256)
        parts.append(nn(left, split_heads(right_ref[rows, win], head_masks(pair))))
    return join_windows(parts)


def norm_back(values, gain, grad_in):
    factor = inverse_rms(values)
    inner = jnp.mean(grad_in * gain * values, axis=-1, keepdims=True)
    grad_out = factor * gain * grad_in - values * (factor * factor * factor * inner)
    return grad_out, jnp.sum(grad_in * values * factor, axis=0, keepdims=True)


def allowed_keys(segments):
    query = jnp.broadcast_to(segments.astype(F32), (SEQ, SEQ))
    row, col = block_offset()
    key_at = lax.broadcasted_iota(jnp.int32, (SEQ, SEQ), 0)
    query_at = lax.broadcasted_iota(jnp.int32, (SEQ, SEQ), 1)
    seen = (query.T == query) & (row == col) & (key_at <= query_at)
    return jnp.sum(jnp.where(seen, 1.0, 0.0).reshape(8, PATCHES, SEQ), axis=0)


SCHEDULE = (
    ("launch", 0), ("launch", 1), ("n1", 0, 4), ("launch", 2), ("Z", 0, 1), ("Z", 0, 2), ("Z", 0, 3), ("launch", 3),
    ("Z", 1, 1), ("Z", 1, 2), ("Z", 1, 3), ("launch", 4), ("Z", 2, 1), ("Z", 2, 2), ("Z", 2, 3), ("P", 0), ("P", 1),
    ("C", 0), ("R", 0), ("launch", 5), ("Z", 3, 1), ("q", 0, 4), ("Z", 3, 2), ("Z", 3, 3), ("P", 2), ("C", 1),
    ("R", 1), ("Z", 4, 1), ("k", 0, 4), ("Z", 4, 2), ("Z", 4, 3), ("P", 3), ("C", 2), ("R", 2), ("Z", 5, 1),
    ("v", 0, 4), ("Z", 5, 2), ("af", 0, 3), ("Z", 5, 3), ("P", 4), ("C", 3), ("af", 3, 6), ("R", 3), ("af", 6, 8),
    ("o", 0, 1), ("P", 5), ("o", 1, 4), ("C", 4), ("R", 4), ("u", 0, 3), ("C", 5), ("u", 3, 4), ("gwd", 0, 1),
    ("R", 5), ("gwd", 1, 5), ("s", 0), ("ga", 0, 4), ("p", 0), ("gwu", 0, 5), ("s", 1), ("y", 0, 1), ("X", 0, 0),
    ("Y", 0, 0), ("y", 1, 3), ("p", 1), ("y", 3, 4), ("X", 0, 1), ("Y", 0, 1), ("gn2", 0, 2), ("L", 0, 0),
    ("gn2", 2, 4), ("gwo", 0, 2), ("X", 1, 0), ("Y", 1, 0), ("gwo", 2, 5), ("s", 2), ("gatt", 0, 1), ("X", 1, 1),
    ("Y", 1, 1), ("gatt", 1, 3), ("L", 0, 1), ("p", 2), ("gatt", 3, 4), ("L", 1, 0), ("ab", 0, 2), ("L", 1, 1),
    ("ab", 2, 5), ("F", 0), ("X", 2, 0), ("Y", 2, 0), ("ab", 5, 7), ("X", 2, 1), ("Y", 2, 1), ("ab", 7, 8),
    ("gwv", 0, 1), ("L", 2, 0), ("gwv", 1, 3), ("L", 2, 1), ("F", 1), ("gwv", 3, 5), ("s", 3), ("gwq", 0, 4),
    ("p", 3), ("gwq", 4, 5), ("s", 4), ("gwk", 0, 4), ("p", 4), ("F", 2), ("X", 3, 0), ("Y", 3, 0), ("gwk", 4, 5),
    ("gn1", 0, 1), ("X", 3, 1), ("Y", 3, 1), ("s", 5), ("gn1", 1, 3), ("X", 4, 0), ("Y", 4, 0), ("p", 5),
    ("gn1", 3, 4), ("t", 0), ("X", 4, 1), ("Y", 4, 1), ("L", 3, 0), ("T", 0), ("t", 1), ("L", 3, 1), ("L", 4, 0),
    ("X", 5, 0), ("T", 1), ("t", 2), ("Y", 5, 0), ("X", 5, 1), ("F", 3), ("T", 2), ("t", 3), ("Y", 5, 1),
    ("L", 4, 1), ("L", 5, 0), ("T", 3), ("L", 5, 1), ("F", 4), ("F", 5),
)


def layer_kernel(
    remote,
    x_hbm, g_hbm, seg_ref, dim_ref, gain_attn_in, gain_mlp_in, bias_q_in, bias_v_in, bias_o_in, bias_up_in, bias_down_in,
    w0, w1, w2, w3, w4, w5,
    y_out, in_grad_out, g0, g1, g2, g3, g4, g5,
    s_query, s_value, s_out, s_up, s_down, s_dim, s_gain_attn, s_gain_mlp, spill, n1_spill,
    full, b0, b1, b2, b3, b4, b5, b6, b7, res, probs, sums, vecs,
    own_sem, load_sem, *rest,
):
    tokens, width = b0.shape
    half = pl.multiple_of(lax.axis_index("heads") * tokens, SEQ)
    outs = (g0, g1, g2, g3, g4, g5)
    loads, stores = {}, {}

    def move(name, source, target):
        copy = pltpu.make_async_copy(source, target, load_sem.at[len(loads) + len(stores)])
        copy.start()
        return copy

    def load(name, source, target):
        loads[name] = move(name, source, target)

    def store(name, source, target):
        stores[name] = move(name, source, target)

    def loaded(*names):
        for name in names:
            if name in loads and name not in waited:
                loads[name].wait()
                waited.add(name)

    def stored(*names):
        for name in names:
            if name not in waited:
                stores[name].wait()
                waited.add(name)

    waited = set()
    load("x", x_hbm.at[pl.ds(half, tokens)], b0)
    if remote:
        Peers().enter()
        gather = Gather((w0, w1, w2, w3, w4, w5), full, rest[0], rest[1], own_sem)
        scatter = Scatter(full, outs, *rest[2:13])
        totals = Totals(sums, *rest[13:17])
    else:
        gather = Loaded((w0, w1, w2, w3, w4, w5), full, own_sem)
        scatter, totals = Kept(full, outs, rest[0]), None
    sums[0] = jnp.zeros(sums.shape[1:], F32)
    inputs = (gain_attn_in, gain_mlp_in, bias_q_in, bias_v_in, bias_o_in, bias_up_in, bias_down_in)
    for n, vector in enumerate(inputs):
        vecs[n : n + 1] = vector[...].reshape(1, width)
    factor = QUERY_BASE / math.sqrt(DH)
    dims = dim_ref[...].reshape(1, DH)
    softplus = jnp.maximum(dims, 0.0) + jnp.log(1.0 + jnp.exp(-jnp.abs(dims)))
    vecs[7:8] = jnp.concatenate([factor * softplus] * (width // DH), axis=1)
    gain_attn_ref, gain_mlp_ref, bias_q_ref, bias_v_ref = (vecs.at[n : n + 1] for n in range(4))
    bias_o_ref, bias_up_ref, bias_down_ref, scale_ref = (vecs.at[n : n + 1] for n in range(4, 8))
    small = sums.at[0]
    every = slice(None)

    def add_to(row, cols, values):
        small[row : row + 1, cols] = small[row : row + 1, cols] + values

    def over(first, last, size, body):
        if last - first == 1:
            body(pl.ds(first * size, size), first)
            return

        @pl.loop(first, last)
        def _(i):
            body(tile(i, size), i)

    def normed_one(first, last):
        loaded("x")

        def body(rows, i):
            values = b0[rows].astype(F32)
            b1[rows] = (values * inverse_rms(values) * gain_attn_ref[...]).astype(BF)

        over(first, last, ROWS, body)
        if last * ROWS == tokens:
            store("n1_out", b1, n1_spill)

    def query(first, last):
        def body(rows, i):
            b4[rows] = ((nn(b1[rows], full[0]) + bias_q_ref[...]) * scale_ref[...]).astype(BF)

        over(first, last, ROWS, body)

    def key(first, last):
        def body(rows, i):
            b5[rows] = nn(b1[rows], full[1]).astype(BF)

        over(first, last, ROWS, body)

    def value(first, last):
        def body(rows, i):
            b6[rows] = (nn(b1[rows], full[2]) + bias_v_ref[...]).astype(BF)

        over(first, last, ROWS, body)
        if last * ROWS == tokens:
            if remote:
                stored("w2")
            gather.close(2)
            scatter.open()

    def attend(first, last):
        stored("n1_out")

        def body(rows, i):
            allowed = jnp.concatenate([allowed_keys(seg_ref[pl.ds(lax.axis_index("heads") * (tokens // SEQ) + i, 1)])] * 8, axis=0)
            for group in range(2):
                part = softmax_packed(pack_scores(b5, b4, rows, group), allowed)
                probs[i, group] = part.astype(BF)
                b1[rows, 640 * group : 640 * (group + 1)] = spread(part.T.astype(BF), group, b6, rows).astype(BF)

        over(first, last, SEQ, body)

    def attend_out(first, last):
        def body(rows, i):
            total = b0[rows].astype(F32) + nt(b1[rows], full[3]) + bias_o_ref[...]
            res[rows] = total
            b2[rows] = (total * inverse_rms(total) * gain_mlp_ref[...]).astype(BF)

        over(first, last, ROWS, body)
        if last * ROWS == tokens:
            load("g", g_hbm.at[pl.ds(half, tokens)], b0)

    def up(first, last):
        def body(rows, i):
            up_proj = nn(b2[rows], full[4]) + bias_up_ref[...]
            square = up_proj * up_proj
            tanh = jnp.tanh(GELU_C * up_proj * (1.0 + 0.044715 * square))
            b7[rows] = (0.5 * up_proj * (1.0 + tanh)).astype(BF)
            slope = 0.5 * (1.0 + tanh) + 0.5 * up_proj * (1.0 - tanh * tanh) * (
                GELU_C * (1.0 + 3 * 0.044715 * square)
            )
            b3[rows] = slope.astype(BF)

        over(first, last, ROWS, body)

    def weight_grad(slot, left, right):
        def run(first, last):
            def body(cols, i):
                full[slot, cols] = tn(left[:, cols], right[...]).astype(BF)

            over(first, last, ROWS, body)

        return run

    down_grad = weight_grad(0, b0, b7)

    def grad_down(first, last):
        loaded("g")
        if remote:
            stored("w0")
        gather.close(0)
        down_grad(first, last)

    def down(first, last):
        def body(rows, i):
            b7[rows] = (res[rows] + nt(b7[rows], full[5]) + bias_down_ref[...]).astype(BF)

        over(first, last, ROWS, body)
        rows = pl.ds(first * ROWS, (last - first) * ROWS)
        store(f"y{first}", b7.at[rows], y_out.at[rows])

    def grad_act(first, last):
        def body(rows, i):
            grad_up = (nn(b0[rows], full[5]) * b3[rows].astype(F32)).astype(BF)
            b3[rows] = grad_up
            add_to(7, every, jnp.sum(grad_up.astype(F32), axis=0, keepdims=True))
            add_to(3, every, jnp.sum(b0[rows].astype(F32), axis=0, keepdims=True))

        over(first, last, ROWS, body)

    up_grad = weight_grad(1, b2, b3)

    def grad_up(first, last):
        if remote:
            stored("w1")
        gather.close(1)
        up_grad(first, last)

    def reload(k, slot):
        gather.close(slot)
        load(f"again{k}", spill.at[k] if remote else (w0, w1, w2)[k], full.at[slot])

    def norm_two_back(first, last):
        if first == 0:
            reload(0, 5)

        def body(rows, i):
            back, gain_sum = norm_back(res[rows], gain_mlp_ref[...], nt(b3[rows], full[4]))
            total = b0[rows].astype(F32) + back
            res[rows] = total
            b2[rows] = total.astype(BF)
            add_to(1, every, gain_sum)
            add_to(2, every, jnp.sum(total, axis=0, keepdims=True))

        over(first, last, ROWS, body)
        if last * ROWS == tokens:
            reload(1, 4)
            load("n1", n1_spill, b3)

    grad_out = weight_grad(0, b2, b1)

    def attended_grad(first, last):
        if first == 0:
            load("x2", x_hbm.at[pl.ds(half, tokens)], b1)

        def body(rows, i):
            b0[rows] = nn(b2[rows], full[3]).astype(BF)

        over(first, last, ROWS, body)
        if last * ROWS == tokens:
            reload(2, 3)

    def attend_back(first, last):
        def body(rows, i):
            for group in range(2):
                cols = slice(640 * group, 640 * (group + 1))
                soft = probs[i, group]
                grad_soft = pack_scores(b6, b0, rows, group).reshape(8, PATCHES, SEQ)
                soft_f = soft.astype(F32).reshape(8, PATCHES, SEQ)
                inner = jnp.sum(soft_f * grad_soft, axis=1, keepdims=True)
                grad_scores = (soft_f * (grad_soft - inner)).reshape(SEQ, SEQ)
                grad_q = spread(grad_scores.T.astype(BF), group, b5, rows)
                grad_k = gather_back(grad_scores.astype(BF), group, b4, rows).astype(BF)
                grad_v = gather_back(soft, group, b0, rows).astype(BF)
                add_to(4, cols, jnp.sum(grad_q * b4[rows, cols].astype(F32), axis=0, keepdims=True))
                grad_q = (grad_q * scale_ref[:, cols]).astype(BF)
                add_to(5, cols, jnp.sum(grad_q.astype(F32), axis=0, keepdims=True))
                add_to(6, cols, jnp.sum(grad_v.astype(F32), axis=0, keepdims=True))
                b4[rows, cols] = grad_q
                b5[rows, cols] = grad_k
                b6[rows, cols] = grad_v

        over(first, last, SEQ, body)

    value_grad = weight_grad(1, b3, b6)

    def grad_value(first, last):
        loaded("n1")
        value_grad(first, last)

    def norm_one_back(first, last):
        loaded("again0", "again1", "again2", "x2")

        def body(rows, i):
            grad_norm = nt(b4[rows], full[5]) + nt(b5[rows], full[4]) + nt(b6[rows], full[3])
            back, gain_sum = norm_back(b1[rows].astype(F32), gain_attn_ref[...], grad_norm)
            res[rows] = res[rows] + back
            add_to(0, every, gain_sum)

        over(first, last, ROWS, body)
        rows = pl.ds(first * ROWS, (last - first) * ROWS)
        store(f"dx{first}", res.at[rows], in_grad_out.at[rows])

    def arrived(k):
        gather.ready(k)
        if remote and k < 3:
            store(f"w{k}", full.at[k], spill.at[k])

    def total_start(n):
        if remote:
            totals.start(n)

    def total_take(n):
        done = totals.take(n) if remote else sums[0]
        if n < 3:
            return
        by_lane = done[4:5] / scale_ref[...]
        by_dim = by_lane[:, :DH]
        for head in range(1, width // DH):
            by_dim = by_dim + by_lane[:, DH * head : DH * (head + 1)]
        s_dim[...] = (by_dim * (factor / (1.0 + jnp.exp(-dims)))).reshape(DH)
        rows = ((s_query, 5), (s_value, 6), (s_out, 2), (s_up, 7), (s_down, 3), (s_gain_attn, 0), (s_gain_mlp, 1))
        for target, row in rows:
            target[...] = done[row : row + 1].reshape(width)

    steps = {
        "launch": gather.launch, "Z": gather.from_z, "P": gather.from_plane, "C": gather.from_corner, "R": arrived,
        "n1": normed_one, "q": query, "k": key, "v": value, "af": attend, "o": attend_out, "u": up, "gwd": grad_down,
        "y": down, "ga": grad_act, "gwu": grad_up, "gn2": norm_two_back, "gwo": grad_out, "gatt": attended_grad,
        "ab": attend_back, "gwv": grad_value, "gwq": weight_grad(0, b3, b4), "gwk": weight_grad(1, b3, b5),
        "gn1": norm_one_back, "s": scatter.start, "p": scatter.pair_sum, "X": scatter.plane_x, "Y": scatter.plane_y,
        "L": scatter.plane_last, "F": scatter.finish, "t": total_start, "T": total_take,
    }
    for name, *numbers in SCHEDULE:
        steps[name](*numbers)
    for name, copy in list(stores.items()):
        if name not in waited:
            copy.wait()
    scatter.end()
    if remote:
        totals.end()


def layer(remote, tokens, x, g, segments, vectors, weights):
    d = x.shape[1]
    hbm, vmem = pl.BlockSpec(memory_space=pl.ANY), pl.BlockSpec(memory_space=pltpu.VMEM)
    dma, regular = pltpu.SemaphoreType.DMA, pltpu.SemaphoreType.REGULAR
    big = pltpu.VMEM((tokens, d), BF)
    sums = pltpu.VMEM((4 if remote else 1, 8, d), F32)
    scratch = [pltpu.VMEM((6, d, d), BF)] + [big] * 8
    scratch += [pltpu.VMEM((tokens, d), F32), pltpu.VMEM((tokens // SEQ, 2, SEQ, SEQ), BF), sums, pltpu.VMEM((8, d), F32), dma((6,)), dma((24,))]
    if remote:
        depth, width = d // lax.axis_size("wide"), d // lax.axis_size("heads")
        block = (depth, width)
        scratch += [
            dma((6, Gather.SLOTS)), dma((6, 32)),
            pltpu.VMEM((JOBS, 2, depth, d), BF), pltpu.VMEM((JOBS, 2, 2) + block, BF),
            pltpu.VMEM((JOBS, 2) + block, BF), pltpu.VMEM((JOBS, 2) + block, BF),
            pltpu.VMEM((3, 4) + block, BF), pltpu.VMEM((JOBS, 3) + block, BF),
            pltpu.VMEM((JOBS,) + block, F32),
            dma((JOBS, 12)), dma((JOBS, 12)), regular, dma((JOBS,)),
            pltpu.VMEM((3, 8, d), F32), pltpu.VMEM((4, 8, d), F32), dma((6,)), dma((6,)),
        ]
        grads = [jax.ShapeDtypeStruct(block, F32)] * 6
    else:
        scratch += [dma((JOBS,))]
        grads = [jax.ShapeDtypeStruct((d, d), BF)] * 6
    outs = [
        jax.ShapeDtypeStruct((tokens, d), BF), jax.ShapeDtypeStruct((tokens, d), F32), *grads,
        *[jax.ShapeDtypeStruct((DH if n == 5 else d,), F32) for n in range(8)], jax.ShapeDtypeStruct((3, d, d), BF), jax.ShapeDtypeStruct((tokens, d), BF),
    ]
    return pl.pallas_call(
        functools.partial(layer_kernel, remote),
        out_shape=outs,
        in_specs=[hbm, hbm] + [vmem] * 9 + [hbm] * 6,
        out_specs=[hbm] * 8 + [vmem] * 8 + [hbm] * 2,
        scratch_shapes=scratch,
        compiler_params=pltpu.CompilerParams(
            collective_id=0 if remote else None,
            has_side_effects=remote,
            vmem_limit_bytes=63 * 2**20,
        ),
        name="layer",
    )(x, g, segments, *vectors, *weights)


def shards(
    inputs, segment_ids, cotangent, w_query, w_key, w_value, w_out, w_up, w_down,
    b_query, b_value, b_out, b_up, b_down, dim_scale, gain_attn, gain_mlp,
):
    tokens = inputs.shape[0] // lax.axis_size("heads")
    remote = lax.axis_size("wide") == 16 and lax.axis_size("heads") == 2
    vectors = (dim_scale, gain_attn, gain_mlp, b_query, b_value, b_out, b_up, b_down)
    weights = [w_query, w_key, w_value, w_out.T, w_up, w_down.T]
    if not remote:
        weights = [
            lax.all_gather(lax.all_gather(w, "heads", axis=1, tiled=True), "wide", axis=0, tiled=True) for w in weights
        ]
    output, input_grad, *rest = layer(remote, tokens, inputs, cotangent, segment_ids.reshape(-1, SEQ), vectors, weights)
    grads, sums = rest[:6], rest[6:14]
    if not remote:
        grads = [lax.psum_scatter(grad, "wide", scatter_dimension=0, tiled=True) for grad in grads]
        grads = [lax.psum_scatter(grad, "heads", scatter_dimension=1, tiled=True).astype(F32) for grad in grads]
        sums = lax.psum(sums, ("wide", "heads"))
    grads[3], grads[5] = grads[3].T, grads[5].T
    return (output, input_grad, *grads, *sums)


def solution(mesh):
    token, both = P("wide", None), P(("wide", "heads"), None)
    tall, flat = P("wide", "heads"), P("heads", "wide")
    return jax.shard_map(
        shards,
        mesh=mesh,
        in_specs=(token, P("wide"), token, tall, tall, tall, flat, tall, flat) + (P(),) * 8,
        out_specs=(both, both, tall, tall, tall, flat, tall, flat) + (P(),) * 8,
        check_vma=False,
    )
```

```python
import functools
import math

import jax
import jax.numpy as jnp
from jax import lax
from jax.experimental import pallas as pl
from jax.experimental.pallas import tpu as pltpu
from jax.sharding import PartitionSpec as P

DH = 80
PATCHES = 16
EPS = 1e-06
QUERY_BASE = 1.442695041
BF = jnp.bfloat16
F32 = jnp.float32
MESH = pl.DeviceIdType.MESH
ROWS = 256
SEQ = 128
GELU_C = math.sqrt(2.0 / math.pi)


def nn(left, right):
    return jnp.dot(left, right, preferred_element_type=F32)


def nt(left, right):
    return lax.dot_general(left, right, (((1,), (1,)), ((), ())), preferred_element_type=F32)


def tn(left, right):
    return lax.dot_general(left, right, (((0,), (0,)), ((), ())), preferred_element_type=F32)


def inverse_rms(values):
    return lax.rsqrt(jnp.mean(values * values, axis=-1, keepdims=True) + EPS)


def tile(index, size):
    return pl.ds(pl.multiple_of(index * size, size), size)


def head_window(pair):
    return (2 * DH * pair) // 128 * 128


def head_masks(pair):
    lanes = head_window(pair) + lax.broadcasted_iota(jnp.int32, (SEQ, 256), 1)
    picks = []
    for head in (2 * pair, 2 * pair + 1):
        inside = (lanes >= DH * head) & (lanes < DH * (head + 1))
        picks.append(jnp.where(inside, 1.0, 0.0).astype(BF))
    return picks


def block_offset():
    row = lax.broadcasted_iota(jnp.int32, (SEQ, SEQ), 0) // PATCHES
    col = lax.broadcasted_iota(jnp.int32, (SEQ, SEQ), 1) // PATCHES
    return row, col


def roll_rows(values, blocks):
    shift = (blocks % 8) * PATCHES
    if shift == 0:
        return values
    return jnp.concatenate([values[SEQ - shift :], values[: SEQ - shift]], axis=0)


def split_heads(window, masks):
    return jnp.concatenate([window * masks[0], window * masks[1]], axis=0)


def split_rolled(window, masks, slots):
    return jnp.concatenate(
        [roll_rows(window, slots[0]) * masks[0], roll_rows(window, slots[1]) * masks[1]], axis=0
    )


def pack_scores(left_ref, right_ref, rows, group):
    row, col = block_offset()
    offset = lax.rem(row - col + 8, 8)
    packed = jnp.zeros((SEQ, SEQ), F32)
    for pair in range(4 * group, 4 * group + 4):
        win = pl.ds(head_window(pair), 256)
        both = nt(left_ref[rows, win], split_heads(right_ref[rows, win], head_masks(pair)))
        for side in range(2):
            slot = (2 * pair + side) % 8
            one = roll_rows(both[:, SEQ * side : SEQ * (side + 1)], slot)
            packed = jnp.where(offset == slot, one, packed)
    return packed


def spread(packed, group, right_ref, rows):
    row, col = block_offset()
    offset = lax.rem(col - row + 8, 8)
    parts = []
    for pair in range(4 * group, 4 * group + 4):
        slots = (2 * pair % 8, (2 * pair + 1) % 8)
        left = jnp.concatenate(
            [packed * jnp.where(offset == s, 1.0, 0.0).astype(BF) for s in slots], axis=1
        )
        win = pl.ds(head_window(pair), 256)
        parts.append(nn(left, split_rolled(right_ref[rows, win], head_masks(pair), slots)))
    return join_windows(parts)


def join_windows(parts):
    tiles = [parts[0][:, :128]]
    for before, after in zip(parts[:-1], parts[1:]):
        tiles.append(before[:, 128:] + after[:, :128])
    tiles.append(parts[-1][:, 128:])
    return jnp.concatenate(tiles, axis=1)


def softmax_packed(packed, allowed):
    scores = jnp.where(allowed > 0.5, packed, -1e30).reshape(8, PATCHES, SEQ)
    exps = jnp.exp(scores - jnp.max(scores, axis=1, keepdims=True))
    return (exps / jnp.sum(exps, axis=1, keepdims=True)).reshape(SEQ, SEQ)


class Peers:
    def __init__(self):
        wide = lax.axis_index("wide")
        self.y = lax.axis_index("heads")
        self.z = wide // 4
        self.x = lax.rem(wide // 2, 2)
        self.c = lax.rem(wide, 2)

    def device(self, z, x, y, c):
        return ((z * 2 + x) * 2 + c, y)

    def across_x(self):
        return self.device(self.z, 1 - self.x, self.y, self.c)

    def across_y(self):
        return self.device(self.z, self.x, 1 - self.y, self.c)

    def across_core(self):
        return self.device(self.z, self.x, self.y, 1 - self.c)

    def along_z(self, step):
        return self.device(lax.rem(self.z + step, 4), self.x, self.y, self.c)

    def enter(self):
        barrier = pltpu.get_barrier_semaphore()
        others = [self.across_x(), self.across_y(), self.across_core()]
        others += [self.along_z(step) for step in (1, 2, 3)]
        for other in others:
            pl.semaphore_signal(barrier, inc=1, device_id=other, device_id_type=MESH)
        pl.semaphore_wait(barrier, len(others))


DOUBLED = 3


class Gather:
    SLOTS = 37

    def __init__(self, blocks, full, send_sem, recv_sem, own_sem):
        self.blocks, self.full = blocks, full
        self.send_sem, self.recv_sem, self.own_sem = send_sem, recv_sem, own_sem
        self.peers = Peers()
        self.depth, self.width = blocks[0].shape
        self.closed = set()

    def at(self, k, z, x, y, c):
        rows = pl.ds(pl.multiple_of((z * 4 + x * 2 + c) * self.depth, 16), self.depth)
        cols = pl.ds(pl.multiple_of(y * self.width, 128), self.width)
        return self.full.at[k, rows, cols]

    def copy(self, k, place, target, slot, source=None):
        z, x, y, c = place
        there = self.at(k, *place)
        return pltpu.make_async_remote_copy(
            src_ref=there if source is None else source,
            dst_ref=there,
            send_sem=self.send_sem.at[k, slot],
            recv_sem=self.recv_sem.at[k, ((z * 2 + x) * 2 + y) * 2 + c],
            device_id=target,
            device_id_type=MESH,
        )

    def send(self, k, place, target, slot, source=None):
        self.copy(k, place, target, slot, source).start()

    def arrived(self, k, place):
        self.copy(k, place, self.peers.across_core(), 0).wait_recv()

    def own_copy(self, k):
        p = self.peers
        return pltpu.make_async_copy(self.blocks[k], self.at(k, p.z, p.x, p.y, p.c), self.own_sem.at[k])

    def launch(self, k):
        p, block = self.peers, self.blocks[k]
        own = (p.z, p.x, p.y, p.c)
        if k == DOUBLED:
            self.pass_on(k, 0, 0, self.at(k, *own), p.across_y(), block).start()
            self.own_copy(k).start()
            return
        for side in (1, -1):
            @pl.when(self.inside(p.z + side))
            def _():
                self.send(k, own, p.device(p.z + side, p.x, p.y, p.c), self.z_slot(0, side), block)
        self.send(k, own, p.across_x(), 0, block)
        self.send(k, own, p.across_y(), 1, block)
        self.send(k, own, p.across_core(), 2, block)
        self.own_copy(k).start()

    def inside(self, z):
        return (z >= 0) & (z < 4)

    def z_slot(self, hop, side):
        return 3 + 2 * hop + (1 if side > 0 else 0)

    def block(self, k, z, x):
        rows = pl.ds(pl.multiple_of((z * 4 + x * 2 + self.peers.c) * self.depth, 16), self.depth)
        return self.full.at[k, rows]

    def cores(self, k, c):
        return self.full.at[k].reshape(8, 2, self.depth, 2 * self.width).at[:, c]

    def pass_on(self, k, slot, place, there, target, source=None):
        return pltpu.make_async_remote_copy(
            src_ref=there if source is None else source,
            dst_ref=there,
            send_sem=self.send_sem.at[k, slot],
            recv_sem=self.recv_sem.at[k, place],
            device_id=target,
            device_id_type=MESH,
        )

    def from_block(self, k, z, x):
        self.pass_on(k, 0, 1 + 2 * z + x, self.block(k, z, x), self.peers.across_core()).wait_recv()

    def to_block(self, k, slot, z, x, target):
        self.pass_on(k, slot, 1 + 2 * z + x, self.block(k, z, x), target).start()

    def doubling(self, k, step):
        p = self.peers
        far, near = lax.rem(p.z + 2, 4), p.z + 1 - 2 * lax.rem(p.z, 2)
        to_far, to_near = p.device(far, p.x, p.y, p.c), p.device(near, p.x, p.y, p.c)
        if step == 0:
            self.own_copy(k).wait()
            self.pass_on(k, 0, 0, self.at(k, p.z, p.x, 1 - p.y, p.c), p.across_y()).wait_recv()
            self.to_block(k, 1, p.z, p.x, p.across_x())
        elif step == 1:
            self.from_block(k, p.z, 1 - p.x)
        elif step in (2, 3):
            self.to_block(k, step, p.z, p.x if step == 2 else 1 - p.x, to_far)
        elif step in (4, 5):
            self.to_block(k, step, p.z, p.x if step == 4 else 1 - p.x, to_near)
        elif step in (6, 7):
            x = p.x if step == 6 else 1 - p.x
            self.from_block(k, far, x)
            self.to_block(k, step, far, x, to_near)
        else:
            for z in (near, lax.rem(near + 2, 4)):
                for x in range(2):
                    self.from_block(k, z, x)
            self.pass_on(k, 8, 9, self.cores(k, p.c), p.across_core()).start()

    def from_z(self, k, hop):
        p = self.peers
        for side in (1, -1):
            z = p.z - side * hop
            place = (z, p.x, p.y, p.c)

            @pl.when(self.inside(z))
            def _():
                self.arrived(k, place)
                if hop < 3:
                    @pl.when(self.inside(p.z + side))
                    def _():
                        self.send(k, place, p.device(p.z + side, p.x, p.y, p.c), self.z_slot(hop, side))
                self.send(k, place, p.across_x(), 9 + z)
                self.send(k, place, p.across_y(), 13 + z)
                self.send(k, place, p.across_core(), 17 + z)

    def from_plane(self, k):
        p = self.peers
        for z in range(4):
            place = (z, 1 - p.x, p.y, p.c)
            self.arrived(k, place)
            if z % 2 == 1:
                self.send(k, place, p.across_y(), 29 + z)
            self.send(k, place, p.across_core(), 21 + z)
            place = (z, p.x, 1 - p.y, p.c)
            self.arrived(k, place)
            if z % 2 == 0:
                self.send(k, place, p.across_x(), 29 + z)
            self.send(k, place, p.across_core(), 25 + z)

    def from_corner(self, k):
        p = self.peers
        for z in range(4):
            place = (z, 1 - p.x, 1 - p.y, p.c)
            self.arrived(k, place)
            self.send(k, place, p.across_core(), 33 + z)

    def ready(self, k):
        p = self.peers
        if k == DOUBLED:
            self.pass_on(k, 0, 9, self.cores(k, 1 - p.c), p.across_core()).wait_recv()
            return
        self.own_copy(k).wait()
        for z in range(4):
            for x in range(2):
                for y in range(2):
                    self.arrived(k, (z, x, y, 1 - p.c))

    def close(self, k):
        if k in self.closed:
            return
        self.closed.add(k)
        p = self.peers
        own = (p.z, p.x, p.y, p.c)

        if k == DOUBLED:
            self.pass_on(k, 0, 0, self.at(k, *own), p.across_y()).wait_send()
            for slot in range(1, 8):
                self.pass_on(k, slot, 0, self.block(k, p.z, p.x), p.across_x()).wait_send()
            self.pass_on(k, 8, 9, self.cores(k, p.c), p.across_core()).wait_send()
            return

        def sent(slot):
            self.copy(k, own, p.across_core(), slot).wait_send()

        for slot in (0, 1, 2) + tuple(range(21, 37)):
            sent(slot)
        for step in (1, 2, 3):
            z = lax.rem(p.z + step, 4)
            for base in (9, 13, 17):
                sent(base + z)
        for hop in range(3):
            for side in (1, -1):
                @pl.when(self.inside(p.z - side * hop) & self.inside(p.z + side))
                def _():
                    sent(self.z_slot(hop, side))


class Loaded:
    def __init__(self, blocks, full, own_sem):
        self.blocks, self.full, self.own_sem = blocks, full, own_sem

    def own_copy(self, k):
        return pltpu.make_async_copy(self.blocks[k], self.full.at[k], self.own_sem.at[k])

    def launch(self, k):
        self.own_copy(k).start()

    def from_z(self, *_):
        pass

    from_plane = from_corner = close = doubling = from_z

    def ready(self, k):
        self.own_copy(k).wait()


ORDER = (5, 4, 3, 2, 0, 1)
JOBS = len(ORDER)


class Scatter:
    def __init__(self, full, outs, first_x, first_y, last_x, last_y, own, far, out_vmem, send_sem, recv_sem, credit, out_sem):
        self.full, self.own, self.far, self.outs = full, own, far, outs
        self.first_x, self.first_y, self.last_x, self.last_y = first_x, first_y, last_x, last_y
        self.out_vmem, self.out_sem = out_vmem, out_sem
        self.send_sem, self.recv_sem, self.credit = send_sem, recv_sem, credit
        self.peers = Peers()
        self.depth, self.width = own.shape[2:]
        self.left = [4] * JOBS
        self.sent = set()

    def remote(self, j, slot, source, there, target):
        return pltpu.make_async_remote_copy(
            src_ref=source,
            dst_ref=there,
            send_sem=self.send_sem.at[j, slot],
            recv_sem=self.recv_sem.at[j, slot],
            device_id=target,
            device_id_type=MESH,
        )

    def grad(self, j):
        return self.full.at[j % 2].reshape(8, 2, self.depth, 2 * self.width)

    def pair(self, j):
        return self.full.at[2].reshape(2, 8, self.depth, 2 * self.width).at[j % 2]

    def half(self, which):
        return pl.ds(pl.multiple_of(which * self.width, 128), self.width)

    def cores(self, j):
        return self.remote(j, 0, self.grad(j).at[:, 1 - self.peers.c], self.pair(j), self.peers.across_core())

    def out_x(self, j, n):
        p = self.peers
        return self.remote(j, 1 + n, self.pair(j).at[2 * n + 1 - p.x], self.first_x.at[j, n], p.across_x())

    def out_y(self, j, n):
        p = self.peers
        z = 3 - n
        return self.remote(
            j, 3 + n, self.pair(j).at[2 * z : 2 * z + 2, :, self.half(1 - p.y)], self.first_y.at[j, n], p.across_y()
        )

    def then_y(self, j, n):
        p = self.peers
        return self.remote(j, 5 + n, self.first_x.at[j, n, :, self.half(1 - p.y)], self.last_y.at[j, n], p.across_y())

    def then_x(self, j, n):
        p = self.peers
        return self.remote(j, 7 + n, self.first_y.at[j, n, 1 - p.x], self.last_x.at[j, n], p.across_x())

    def along(self, j, z):
        p = self.peers
        place = lax.rem(p.z - z + 4, 4) - 1
        return self.remote(j, 9 + place, self.own.at[j % 3, z], self.far.at[j, place], p.device(z, p.x, p.y, p.c))

    def open(self):
        pl.semaphore_signal(self.credit, inc=2, device_id=self.peers.across_core(), device_id_type=MESH)

    def start(self, j):
        pl.semaphore_wait(self.credit, 1)
        self.cores(j).start()

    def pair_sum(self, j):
        p = self.peers
        self.cores(j).wait_recv()
        mine, sums = self.grad(j), self.pair(j)

        @pl.loop(0, 8)
        def _(n):
            sums[n] = (mine[n, p.c].astype(F32) + sums[n].astype(F32)).astype(BF)

        for n in range(2):
            self.out_x(j, n).start()
            self.out_y(j, n).start()
        self.cores(j).wait_send()

    def used(self, j):
        self.left[j] -= 1
        if self.left[j] == 0:
            for n in range(2):
                self.out_x(j, n).wait_send()
                self.out_y(j, n).wait_send()
            if j + 2 < JOBS:
                pl.semaphore_signal(self.credit, inc=1, device_id=self.peers.across_core(), device_id_type=MESH)

    def plane_x(self, j, n):
        p = self.peers
        self.out_x(j, n).wait_recv()
        total = self.first_x[j, n].astype(F32) + self.pair(j)[2 * n + p.x].astype(F32)
        self.first_x[j, n] = total.astype(BF)
        self.then_y(j, n).start()
        self.used(j)

    def plane_y(self, j, n):
        p = self.peers
        self.out_y(j, n).wait_recv()
        for x in range(2):
            mine = self.pair(j)[2 * (3 - n) + x, :, self.half(p.y)]
            self.first_y[j, n, x] = (self.first_y[j, n, x].astype(F32) + mine.astype(F32)).astype(BF)
        self.then_x(j, n).start()
        self.used(j)

    def all_sent(self, j):
        if j >= 0 and j not in self.sent:
            self.sent.add(j)
            for step in (1, 2, 3):
                self.along(j, lax.rem(self.peers.z + step, 4)).wait_send()

    def plane_last(self, j, n):
        p = self.peers
        self.all_sent(j - 3)
        self.then_y(j, n).wait_recv()
        total = self.first_x[j, n, :, self.half(p.y)].astype(F32) + self.last_y[j, n].astype(F32)
        self.own[j % 3, n] = total.astype(BF)
        self.then_x(j, n).wait_recv()
        total = self.first_y[j, n, p.x].astype(F32) + self.last_x[j, n].astype(F32)
        self.own[j % 3, 3 - n] = total.astype(BF)
        for z in (n, 3 - n):
            @pl.when(p.z != z)
            def _():
                self.along(j, z).start()

    def out_copy(self, j):
        return pltpu.make_async_copy(self.out_vmem.at[j], self.outs[ORDER[j]], self.out_sem.at[j])

    def finish(self, j):
        p = self.peers
        total = self.own[j % 3, p.z].astype(F32)
        for step in (1, 2, 3):
            self.along(j, lax.rem(p.z + 4 - step, 4)).wait_recv()
        for place in range(3):
            total += self.far[j, place].astype(F32)
        self.out_vmem[j] = total
        self.out_copy(j).start()

    def end(self):
        p = self.peers
        for j in range(JOBS):
            for n in range(2):
                self.then_y(j, n).wait_send()
                self.then_x(j, n).wait_send()
            self.all_sent(j)
            self.out_copy(j).wait()


class Kept:
    def __init__(self, full, outs, sems):
        self.full, self.outs, self.sems = full, outs, sems

    def copy(self, j):
        return pltpu.make_async_copy(self.full.at[j % 2], self.outs[ORDER[j]], self.sems.at[j])

    def start(self, j):
        self.copy(j).start()

    def pair_sum(self, j):
        self.copy(j).wait()

    def open(self, *_):
        pass

    plane_x = plane_y = plane_last = finish = end = open


class Totals:
    def __init__(self, sums, got, far, send_sem, recv_sem):
        self.sums, self.got, self.far, self.send_sem, self.recv_sem = sums, got, far, send_sem, recv_sem
        self.peers = Peers()

    def copy(self, n, source, there, target):
        return pltpu.make_async_remote_copy(
            src_ref=source, dst_ref=there, send_sem=self.send_sem.at[n], recv_sem=self.recv_sem.at[n],
            device_id=target, device_id_type=MESH,
        )

    def pair(self, n):
        target = (self.peers.across_core, self.peers.across_x, self.peers.across_y)[n]()
        return self.copy(n, self.sums.at[n], self.got.at[n], target)

    def along(self, step):
        z = self.peers.z
        return self.copy(2 + step, self.sums.at[3], self.far.at[z], self.peers.along_z(step))

    def coming(self, step):
        z = lax.rem(self.peers.z - step + 4, 4)
        return self.copy(2 + step, self.sums.at[3], self.far.at[z], self.peers.along_z(step))

    def start(self, n):
        if n < 3:
            self.pair(n).start()
            return
        self.far[self.peers.z] = self.sums[3]
        for step in (1, 2, 3):
            self.along(step).start()

    def take(self, n):
        if n < 3:
            self.pair(n).wait_recv()
            self.sums[n + 1] = self.sums[n] + self.got[n]
            return None
        for step in (1, 2, 3):
            self.coming(step).wait_recv()
        return (self.far[0] + self.far[1]) + (self.far[2] + self.far[3])

    def end(self):
        for n in range(3):
            self.pair(n).wait_send()
        for step in (1, 2, 3):
            self.along(step).wait_send()


def gather_back(packed, group, right_ref, rows):
    row, col = block_offset()
    diagonal = jnp.where(row == col, 1.0, 0.0).astype(BF)
    parts = []
    for pair in range(4 * group, 4 * group + 4):
        left = jnp.concatenate(
            [roll_rows(packed, -(2 * pair + side)) * diagonal for side in range(2)], axis=1
        )
        win = pl.ds(head_window(pair), 256)
        parts.append(nn(left, split_heads(right_ref[rows, win], head_masks(pair))))
    return join_windows(parts)


def norm_back(values, gain, grad_in):
    factor = inverse_rms(values)
    inner = jnp.mean(grad_in * gain * values, axis=-1, keepdims=True)
    grad_out = factor * gain * grad_in - values * (factor * factor * factor * inner)
    return grad_out, jnp.sum(grad_in * values * factor, axis=0, keepdims=True)


def allowed_keys(segments):
    query = jnp.broadcast_to(segments.astype(F32), (SEQ, SEQ))
    row, col = block_offset()
    key_at = lax.broadcasted_iota(jnp.int32, (SEQ, SEQ), 0)
    query_at = lax.broadcasted_iota(jnp.int32, (SEQ, SEQ), 1)
    seen = (query.T == query) & (row == col) & (key_at <= query_at)
    return jnp.sum(jnp.where(seen, 1.0, 0.0).reshape(8, PATCHES, SEQ), axis=0)


SCHEDULE = (
    ("launch", 2), ("launch", 3), ("launch", 0), ("Z", 2, 1), ("n1", 0, 1), ("D", 3, 0), ("launch", 1), ("Z", 0, 1),
    ("Z", 1, 1), ("n1", 1, 2), ("Z", 2, 2), ("D", 3, 4), ("Z", 0, 2), ("Z", 2, 3), ("D", 3, 2), ("Z", 1, 2),
    ("D", 3, 1), ("P", 2), ("D", 3, 5), ("Z", 1, 3), ("D", 3, 3), ("C", 2), ("n1", 2, 3), ("Z", 0, 3), ("n1", 3, 4),
    ("R", 2), ("P", 1), ("P", 0), ("launch", 4), ("v", 0, 3), ("launch", 5), ("C", 1), ("Z", 4, 1), ("v", 3, 4),
    ("D", 3, 7), ("R", 1), ("k", 0, 3), ("C", 0), ("k", 3, 4), ("Z", 4, 2), ("D", 3, 6), ("R", 0), ("q", 0, 4),
    ("af", 0, 2), ("Z", 4, 3), ("af", 2, 3), ("Z", 5, 1), ("af", 3, 5), ("D", 3, 8), ("P", 4), ("af", 5, 7),
    ("Z", 5, 2), ("af", 7, 8), ("R", 3), ("o", 0, 2), ("C", 4), ("Z", 5, 3), ("o", 2, 4), ("R", 4), ("u", 0, 2),
    ("P", 5), ("u", 2, 4), ("gwd", 0, 3), ("C", 5), ("gwd", 3, 5), ("R", 5), ("y", 0, 1), ("s", 0), ("ga", 0, 2),
    ("y", 1, 2), ("ga", 2, 4), ("p", 0), ("y", 2, 3), ("gwu", 0, 5), ("s", 1), ("X", 0, 0), ("y", 3, 4), ("Y", 0, 0),
    ("gn2", 0, 3), ("p", 1), ("Y", 0, 1), ("gn2", 3, 4), ("gwo", 0, 2), ("X", 0, 1), ("gwo", 2, 5), ("s", 2),
    ("gatt", 0, 3), ("X", 1, 0), ("gatt", 3, 4), ("ab", 0, 3), ("p", 2), ("ab", 3, 4), ("X", 1, 1), ("ab", 4, 5),
    ("Y", 1, 0), ("ab", 5, 7), ("L", 0, 1), ("X", 2, 0), ("Y", 1, 1), ("ab", 7, 8), ("gwv", 0, 2), ("Y", 2, 1),
    ("L", 0, 0), ("gwv", 2, 5), ("s", 3), ("X", 2, 1), ("gwq", 0, 1), ("Y", 2, 0), ("gwq", 1, 3), ("p", 3),
    ("L", 1, 0), ("F", 0), ("L", 2, 0), ("gn1", 0, 1), ("gwq", 3, 5), ("Y", 3, 0), ("X", 3, 0), ("s", 4),
    ("L", 2, 1), ("gwk", 0, 4), ("Y", 3, 1), ("X", 3, 1), ("p", 4), ("L", 1, 1), ("L", 3, 0), ("gn1", 1, 3),
    ("L", 3, 1), ("Y", 4, 0), ("X", 4, 0), ("gn1", 3, 4), ("t", 0), ("gwk", 4, 5), ("s", 5), ("T", 0), ("t", 1),
    ("F", 1), ("X", 4, 1), ("Y", 4, 1), ("L", 4, 0), ("T", 1), ("t", 2), ("p", 5), ("L", 4, 1), ("Y", 5, 0),
    ("X", 5, 0), ("T", 2), ("F", 3), ("F", 2), ("t", 3), ("L", 5, 0), ("X", 5, 1), ("Y", 5, 1), ("L", 5, 1),
    ("T", 3), ("F", 4), ("F", 5),
)


def layer_kernel(
    remote,
    x_hbm, g_hbm, seg_ref, dim_ref, gain_attn_in, gain_mlp_in, bias_q_in, bias_v_in, bias_o_in, bias_up_in, bias_down_in,
    w0, w1, w2, w3, w4, w5,
    y_out, in_grad_out, g0, g1, g2, g3, g4, g5,
    s_query, s_value, s_out, s_up, s_down, s_dim, s_gain_attn, s_gain_mlp, spill, n1_spill,
    full, b0, b1, b2, b3, b4, b5, b6, b7, res, probs, sums, vecs,
    own_sem, load_sem, *rest,
):
    tokens, width = b0.shape
    half = pl.multiple_of(lax.axis_index("heads") * tokens, SEQ)
    outs = (g0, g1, g2, g3, g4, g5)
    loads, stores = {}, {}

    def move(name, source, target):
        copy = pltpu.make_async_copy(source, target, load_sem.at[len(loads) + len(stores)])
        copy.start()
        return copy

    def load(name, source, target):
        loads[name] = move(name, source, target)

    def store(name, source, target):
        stores[name] = move(name, source, target)

    def loaded(*names):
        for name in names:
            if name in loads and name not in waited:
                loads[name].wait()
                waited.add(name)

    def stored(*names):
        for name in names:
            if name not in waited:
                stores[name].wait()
                waited.add(name)

    waited = set()
    load("x", x_hbm.at[pl.ds(half, tokens)], b0)
    if remote:
        Peers().enter()
        gather = Gather((w0, w1, w2, w3, w4, w5), full, rest[0], rest[1], own_sem)
        scatter = Scatter(full, outs, *rest[2:13])
        totals = Totals(sums, *rest[13:17])
    else:
        gather = Loaded((w0, w1, w2, w3, w4, w5), full, own_sem)
        scatter, totals = Kept(full, outs, rest[0]), None
    sums[0] = jnp.zeros(sums.shape[1:], F32)
    inputs = (gain_attn_in, gain_mlp_in, bias_q_in, bias_v_in, bias_o_in, bias_up_in, bias_down_in)
    for n, vector in enumerate(inputs):
        vecs[n : n + 1] = vector[...].reshape(1, width)
    factor = QUERY_BASE / math.sqrt(DH)
    dims = dim_ref[...].reshape(1, DH)
    softplus = jnp.maximum(dims, 0.0) + jnp.log(1.0 + jnp.exp(-jnp.abs(dims)))
    vecs[7:8] = jnp.concatenate([factor * softplus] * (width // DH), axis=1)
    gain_attn_ref, gain_mlp_ref, bias_q_ref, bias_v_ref = (vecs.at[n : n + 1] for n in range(4))
    bias_o_ref, bias_up_ref, bias_down_ref, scale_ref = (vecs.at[n : n + 1] for n in range(4, 8))
    small = sums.at[0]
    every = slice(None)

    def add_to(row, cols, values):
        small[row : row + 1, cols] = small[row : row + 1, cols] + values

    def over(first, last, size, body):
        if last - first == 1:
            body(pl.ds(first * size, size), first)
            return

        @pl.loop(first, last)
        def _(i):
            body(tile(i, size), i)

    def normed_one(first, last):
        loaded("x")

        def body(rows, i):
            values = b0[rows].astype(F32)
            b1[rows] = (values * inverse_rms(values) * gain_attn_ref[...]).astype(BF)

        over(first, last, ROWS, body)
        if last * ROWS == tokens:
            store("n1_out", b1, n1_spill)

    def query(first, last):
        def body(rows, i):
            b4[rows] = ((nn(b1[rows], full[0]) + bias_q_ref[...]) * scale_ref[...]).astype(BF)

        over(first, last, ROWS, body)

    def key(first, last):
        def body(rows, i):
            b5[rows] = nn(b1[rows], full[1]).astype(BF)

        over(first, last, ROWS, body)

    def value(first, last):
        def body(rows, i):
            b6[rows] = (nn(b1[rows], full[2]) + bias_v_ref[...]).astype(BF)

        over(first, last, ROWS, body)

    def attend(first, last):
        stored("n1_out")

        def body(rows, i):
            allowed = jnp.concatenate([allowed_keys(seg_ref[pl.ds(lax.axis_index("heads") * (tokens // SEQ) + i, 1)])] * 8, axis=0)
            for group in range(2):
                part = softmax_packed(pack_scores(b5, b4, rows, group), allowed)
                probs[i, group] = part.astype(BF)
                b1[rows, 640 * group : 640 * (group + 1)] = spread(part.T.astype(BF), group, b6, rows).astype(BF)

        over(first, last, SEQ, body)

    def attend_out(first, last):
        def body(rows, i):
            total = b0[rows].astype(F32) + nt(b1[rows], full[3]) + bias_o_ref[...]
            res[rows] = total
            b2[rows] = (total * inverse_rms(total) * gain_mlp_ref[...]).astype(BF)

        over(first, last, ROWS, body)
        if last * ROWS == tokens:
            load("g", g_hbm.at[pl.ds(half, tokens)], b0)

    def up(first, last):
        def body(rows, i):
            up_proj = nn(b2[rows], full[4]) + bias_up_ref[...]
            square = up_proj * up_proj
            tanh = jnp.tanh(GELU_C * up_proj * (1.0 + 0.044715 * square))
            b7[rows] = (0.5 * up_proj * (1.0 + tanh)).astype(BF)
            slope = 0.5 * (1.0 + tanh) + 0.5 * up_proj * (1.0 - tanh * tanh) * (
                GELU_C * (1.0 + 3 * 0.044715 * square)
            )
            b3[rows] = slope.astype(BF)

        over(first, last, ROWS, body)

    def weight_grad(slot, left, right):
        def run(first, last):
            def body(cols, i):
                full[slot, cols] = tn(left[:, cols], right[...]).astype(BF)

            over(first, last, ROWS, body)

        return run

    down_grad = weight_grad(0, b0, b7)

    def grad_down(first, last):
        loaded("g")
        if remote:
            stored("w0", "w2")
        gather.close(0)
        if first == 0:
            gather.close(2)
            scatter.open()
        down_grad(first, last)

    def down(first, last):
        def body(rows, i):
            b7[rows] = (res[rows] + nt(b7[rows], full[5]) + bias_down_ref[...]).astype(BF)

        over(first, last, ROWS, body)
        rows = pl.ds(first * ROWS, (last - first) * ROWS)
        store(f"y{first}", b7.at[rows], y_out.at[rows])

    def grad_act(first, last):
        def body(rows, i):
            grad_up = (nn(b0[rows], full[5]) * b3[rows].astype(F32)).astype(BF)
            b3[rows] = grad_up
            add_to(7, every, jnp.sum(grad_up.astype(F32), axis=0, keepdims=True))
            add_to(3, every, jnp.sum(b0[rows].astype(F32), axis=0, keepdims=True))

        over(first, last, ROWS, body)

    up_grad = weight_grad(1, b2, b3)

    def grad_up(first, last):
        if remote:
            stored("w1")
        gather.close(1)
        up_grad(first, last)

    def reload(k, slot):
        gather.close(slot)
        load(f"again{k}", spill.at[k] if remote else (w0, w1, w2)[k], full.at[slot])

    def norm_two_back(first, last):
        if first == 0:
            reload(0, 5)

        def body(rows, i):
            back, gain_sum = norm_back(res[rows], gain_mlp_ref[...], nt(b3[rows], full[4]))
            total = b0[rows].astype(F32) + back
            res[rows] = total
            b2[rows] = total.astype(BF)
            add_to(1, every, gain_sum)
            add_to(2, every, jnp.sum(total, axis=0, keepdims=True))

        over(first, last, ROWS, body)
        if last * ROWS == tokens:
            reload(1, 4)
            load("n1", n1_spill, b3)

    grad_out = weight_grad(0, b2, b1)

    def attended_grad(first, last):
        if first == 0:
            load("x2", x_hbm.at[pl.ds(half, tokens)], b1)

        def body(rows, i):
            b0[rows] = nn(b2[rows], full[3]).astype(BF)

        over(first, last, ROWS, body)
        if last * ROWS == tokens:
            reload(2, 3)

    def attend_back(first, last):
        def body(rows, i):
            for group in range(2):
                cols = slice(640 * group, 640 * (group + 1))
                soft = probs[i, group]
                grad_soft = pack_scores(b6, b0, rows, group).reshape(8, PATCHES, SEQ)
                soft_f = soft.astype(F32).reshape(8, PATCHES, SEQ)
                inner = jnp.sum(soft_f * grad_soft, axis=1, keepdims=True)
                grad_scores = (soft_f * (grad_soft - inner)).reshape(SEQ, SEQ)
                grad_q = spread(grad_scores.T.astype(BF), group, b5, rows)
                grad_k = gather_back(grad_scores.astype(BF), group, b4, rows).astype(BF)
                grad_v = gather_back(soft, group, b0, rows).astype(BF)
                add_to(4, cols, jnp.sum(grad_q * b4[rows, cols].astype(F32), axis=0, keepdims=True))
                grad_q = (grad_q * scale_ref[:, cols]).astype(BF)
                add_to(5, cols, jnp.sum(grad_q.astype(F32), axis=0, keepdims=True))
                add_to(6, cols, jnp.sum(grad_v.astype(F32), axis=0, keepdims=True))
                b4[rows, cols] = grad_q
                b5[rows, cols] = grad_k
                b6[rows, cols] = grad_v

        over(first, last, SEQ, body)

    value_grad = weight_grad(1, b3, b6)

    def grad_value(first, last):
        loaded("n1")
        value_grad(first, last)

    def norm_one_back(first, last):
        loaded("again0", "again1", "again2", "x2")

        def body(rows, i):
            grad_norm = nt(b4[rows], full[5]) + nt(b5[rows], full[4]) + nt(b6[rows], full[3])
            back, gain_sum = norm_back(b1[rows].astype(F32), gain_attn_ref[...], grad_norm)
            res[rows] = res[rows] + back
            add_to(0, every, gain_sum)

        over(first, last, ROWS, body)
        rows = pl.ds(first * ROWS, (last - first) * ROWS)
        store(f"dx{first}", res.at[rows], in_grad_out.at[rows])

    def arrived(k):
        gather.ready(k)
        if remote and k < 3:
            store(f"w{k}", full.at[k], spill.at[k])

    def total_start(n):
        if remote:
            totals.start(n)

    def total_take(n):
        done = totals.take(n) if remote else sums[0]
        if n < 3:
            return
        by_lane = done[4:5] / scale_ref[...]
        by_dim = by_lane[:, :DH]
        for head in range(1, width // DH):
            by_dim = by_dim + by_lane[:, DH * head : DH * (head + 1)]
        s_dim[...] = (by_dim * (factor / (1.0 + jnp.exp(-dims)))).reshape(DH)
        rows = ((s_query, 5), (s_value, 6), (s_out, 2), (s_up, 7), (s_down, 3), (s_gain_attn, 0), (s_gain_mlp, 1))
        for target, row in rows:
            target[...] = done[row : row + 1].reshape(width)

    steps = {
        "launch": gather.launch, "Z": gather.from_z, "P": gather.from_plane, "C": gather.from_corner, "R": arrived, "D": gather.doubling,
        "n1": normed_one, "q": query, "k": key, "v": value, "af": attend, "o": attend_out, "u": up, "gwd": grad_down,
        "y": down, "ga": grad_act, "gwu": grad_up, "gn2": norm_two_back, "gwo": grad_out, "gatt": attended_grad,
        "ab": attend_back, "gwv": grad_value, "gwq": weight_grad(0, b3, b4), "gwk": weight_grad(1, b3, b5),
        "gn1": norm_one_back, "s": scatter.start, "p": scatter.pair_sum, "X": scatter.plane_x, "Y": scatter.plane_y,
        "L": scatter.plane_last, "F": scatter.finish, "t": total_start, "T": total_take,
    }
    for name, *numbers in SCHEDULE:
        steps[name](*numbers)
    for name, copy in list(stores.items()):
        if name not in waited:
            copy.wait()
    scatter.end()
    if remote:
        totals.end()


def layer(remote, tokens, x, g, segments, vectors, weights):
    d = x.shape[1]
    hbm, vmem = pl.BlockSpec(memory_space=pl.ANY), pl.BlockSpec(memory_space=pltpu.VMEM)
    dma, regular = pltpu.SemaphoreType.DMA, pltpu.SemaphoreType.REGULAR
    big = pltpu.VMEM((tokens, d), BF)
    sums = pltpu.VMEM((4 if remote else 1, 8, d), F32)
    scratch = [pltpu.VMEM((6, d, d), BF)] + [big] * 8
    scratch += [pltpu.VMEM((tokens, d), F32), pltpu.VMEM((tokens // SEQ, 2, SEQ, SEQ), BF), sums, pltpu.VMEM((8, d), F32), dma((6,)), dma((24,))]
    if remote:
        depth, width = d // lax.axis_size("wide"), d // lax.axis_size("heads")
        block = (depth, width)
        scratch += [
            dma((6, Gather.SLOTS)), dma((6, 32)),
            pltpu.VMEM((JOBS, 2, depth, d), BF), pltpu.VMEM((JOBS, 2, 2) + block, BF),
            pltpu.VMEM((JOBS, 2) + block, BF), pltpu.VMEM((JOBS, 2) + block, BF),
            pltpu.VMEM((3, 4) + block, BF), pltpu.VMEM((JOBS, 3) + block, BF),
            pltpu.VMEM((JOBS,) + block, F32),
            dma((JOBS, 12)), dma((JOBS, 12)), regular, dma((JOBS,)),
            pltpu.VMEM((3, 8, d), F32), pltpu.VMEM((4, 8, d), F32), dma((6,)), dma((6,)),
        ]
        grads = [jax.ShapeDtypeStruct(block, F32)] * 6
    else:
        scratch += [dma((JOBS,))]
        grads = [jax.ShapeDtypeStruct((d, d), BF)] * 6
    outs = [
        jax.ShapeDtypeStruct((tokens, d), BF), jax.ShapeDtypeStruct((tokens, d), F32), *grads,
        *[jax.ShapeDtypeStruct((DH if n == 5 else d,), F32) for n in range(8)], jax.ShapeDtypeStruct((3, d, d), BF), jax.ShapeDtypeStruct((tokens, d), BF),
    ]
    return pl.pallas_call(
        functools.partial(layer_kernel, remote),
        out_shape=outs,
        in_specs=[hbm, hbm] + [vmem] * 9 + [hbm] * 6,
        out_specs=[hbm] * 8 + [vmem] * 8 + [hbm] * 2,
        scratch_shapes=scratch,
        compiler_params=pltpu.CompilerParams(
            collective_id=0 if remote else None,
            has_side_effects=remote,
            vmem_limit_bytes=63 * 2**20,
        ),
        name="layer",
    )(x, g, segments, *vectors, *weights)


def deliver_kernel(parts, *refs):
    count = len(parts)
    sources, targets, held, sems = refs[:count], refs[count : 2 * count], refs[2 * count : 3 * count], refs[3 * count]
    steps = []
    for source, target, middle, cut in zip(sources, targets, held, parts):
        depth = source.shape[0] // cut
        for n in range(cut):
            rows = pl.ds(n * depth, depth)
            first = pltpu.make_async_copy(source.at[rows], middle.at[rows], sems.at[0, len(steps)])
            first.start()
            steps.append((first, pltpu.make_async_copy(middle.at[rows], target.at[rows], sems.at[1, len(steps)])))
    for first, second in steps:
        first.wait()
        second.start()
    for first, second in steps:
        second.wait()


def deliver(arrays):
    parts = [8 if a.size >= 2**20 else 1 for a in arrays]
    hbm = pl.BlockSpec(memory_space=pl.ANY)
    return pl.pallas_call(
        functools.partial(deliver_kernel, parts),
        out_shape=[jax.ShapeDtypeStruct(a.shape, a.dtype) for a in arrays],
        in_specs=[hbm] * len(arrays),
        out_specs=[hbm] * len(arrays),
        scratch_shapes=[pltpu.VMEM(a.shape, a.dtype) for a in arrays] + [pltpu.SemaphoreType.DMA((2, sum(parts)))],
        compiler_params=pltpu.CompilerParams(vmem_limit_bytes=62 * 2**20),
        name="deliver",
    )(*arrays)


def shards(
    inputs, segment_ids, cotangent, w_query, w_key, w_value, w_out, w_up, w_down,
    b_query, b_value, b_out, b_up, b_down, dim_scale, gain_attn, gain_mlp,
):
    tokens = inputs.shape[0] // lax.axis_size("heads")
    remote = lax.axis_size("wide") == 16 and lax.axis_size("heads") == 2
    vectors = (dim_scale, gain_attn, gain_mlp, b_query, b_value, b_out, b_up, b_down)
    weights = [w_query, w_key, w_value, w_out.T, w_up, w_down.T]
    if not remote:
        weights = [
            lax.all_gather(lax.all_gather(w, "heads", axis=1, tiled=True), "wide", axis=0, tiled=True) for w in weights
        ]
    output, input_grad, *rest = layer(remote, tokens, inputs, cotangent, segment_ids.reshape(-1, SEQ), vectors, weights)
    rest = rest[:14]
    if remote:
        output, input_grad, *rest = deliver([output, input_grad, *rest])
    grads, sums = rest[:6], rest[6:]
    if not remote:
        grads = [lax.psum_scatter(grad, "wide", scatter_dimension=0, tiled=True) for grad in grads]
        grads = [lax.psum_scatter(grad, "heads", scatter_dimension=1, tiled=True).astype(F32) for grad in grads]
        sums = lax.psum(sums, ("wide", "heads"))
    grads[3], grads[5] = grads[3].T, grads[5].T
    return (output, input_grad, *grads, *sums)


def solution(mesh):
    token, both = P("wide", None), P(("wide", "heads"), None)
    tall, flat = P("wide", "heads"), P("heads", "wide")
    return jax.shard_map(
        shards,
        mesh=mesh,
        in_specs=(token, P("wide"), token, tall, tall, tall, flat, tall, flat) + (P(),) * 8,
        out_specs=(both, both, tall, tall, tall, flat, tall, flat) + (P(),) * 8,
        check_vma=False,
    )
```

```python
import functools
import math

import jax
import jax.numpy as jnp
from jax import lax
from jax.experimental import pallas as pl
from jax.experimental.pallas import tpu as pltpu
from jax.sharding import PartitionSpec as P

DH = 80
PATCHES = 16
EPS = 1e-06
QUERY_BASE = 1.442695041
BF = jnp.bfloat16
F32 = jnp.float32
MESH = pl.DeviceIdType.MESH
ROWS = 256
SEQ = 128
GELU_C = math.sqrt(2.0 / math.pi)


def nn(left, right):
    return jnp.dot(left, right, preferred_element_type=F32)


def nt(left, right):
    return lax.dot_general(left, right, (((1,), (1,)), ((), ())), preferred_element_type=F32)


def tn(left, right):
    return lax.dot_general(left, right, (((0,), (0,)), ((), ())), preferred_element_type=F32)


def inverse_rms(values):
    return lax.rsqrt(jnp.mean(values * values, axis=-1, keepdims=True) + EPS)


def tile(index, size):
    return pl.ds(pl.multiple_of(index * size, size), size)


def head_window(pair):
    return (2 * DH * pair) // 128 * 128


def head_masks(pair):
    lanes = head_window(pair) + lax.broadcasted_iota(jnp.int32, (SEQ, 256), 1)
    picks = []
    for head in (2 * pair, 2 * pair + 1):
        inside = (lanes >= DH * head) & (lanes < DH * (head + 1))
        picks.append(jnp.where(inside, 1.0, 0.0).astype(BF))
    return picks


def block_offset():
    row = lax.broadcasted_iota(jnp.int32, (SEQ, SEQ), 0) // PATCHES
    col = lax.broadcasted_iota(jnp.int32, (SEQ, SEQ), 1) // PATCHES
    return row, col


def roll_rows(values, blocks):
    shift = (blocks % 8) * PATCHES
    if shift == 0:
        return values
    return jnp.concatenate([values[SEQ - shift :], values[: SEQ - shift]], axis=0)


def split_heads(window, masks):
    return jnp.concatenate([window * masks[0], window * masks[1]], axis=0)


def split_rolled(window, masks, slots):
    return jnp.concatenate(
        [roll_rows(window, slots[0]) * masks[0], roll_rows(window, slots[1]) * masks[1]], axis=0
    )


def pack_scores(left_ref, right_ref, rows, group):
    row, col = block_offset()
    offset = lax.rem(row - col + 8, 8)
    packed = jnp.zeros((SEQ, SEQ), F32)
    for pair in range(4 * group, 4 * group + 4):
        win = pl.ds(head_window(pair), 256)
        both = nt(left_ref[rows, win], split_heads(right_ref[rows, win], head_masks(pair)))
        for side in range(2):
            slot = (2 * pair + side) % 8
            one = roll_rows(both[:, SEQ * side : SEQ * (side + 1)], slot)
            packed = jnp.where(offset == slot, one, packed)
    return packed


def spread(packed, group, right_ref, rows):
    row, col = block_offset()
    offset = lax.rem(col - row + 8, 8)
    parts = []
    for pair in range(4 * group, 4 * group + 4):
        slots = (2 * pair % 8, (2 * pair + 1) % 8)
        left = jnp.concatenate(
            [packed * jnp.where(offset == s, 1.0, 0.0).astype(BF) for s in slots], axis=1
        )
        win = pl.ds(head_window(pair), 256)
        parts.append(nn(left, split_rolled(right_ref[rows, win], head_masks(pair), slots)))
    return join_windows(parts)


def join_windows(parts):
    tiles = [parts[0][:, :128]]
    for before, after in zip(parts[:-1], parts[1:]):
        tiles.append(before[:, 128:] + after[:, :128])
    tiles.append(parts[-1][:, 128:])
    return jnp.concatenate(tiles, axis=1)


def softmax_packed(packed, allowed):
    scores = jnp.where(allowed > 0.5, packed, -1e30).reshape(8, PATCHES, SEQ)
    exps = jnp.exp(scores - jnp.max(scores, axis=1, keepdims=True))
    return (exps / jnp.sum(exps, axis=1, keepdims=True)).reshape(SEQ, SEQ)


class Peers:
    def __init__(self):
        wide = lax.axis_index("wide")
        self.y = lax.axis_index("heads")
        self.z = wide // 4
        self.x = lax.rem(wide // 2, 2)
        self.c = lax.rem(wide, 2)

    def device(self, z, x, y, c):
        return ((z * 2 + x) * 2 + c, y)

    def across_x(self):
        return self.device(self.z, 1 - self.x, self.y, self.c)

    def across_y(self):
        return self.device(self.z, self.x, 1 - self.y, self.c)

    def across_core(self):
        return self.device(self.z, self.x, self.y, 1 - self.c)

    def along_z(self, step):
        return self.device(lax.rem(self.z + step, 4), self.x, self.y, self.c)

    def enter(self):
        barrier = pltpu.get_barrier_semaphore()
        others = [self.across_x(), self.across_y(), self.across_core()]
        others += [self.along_z(step) for step in (1, 2, 3)]
        for other in others:
            pl.semaphore_signal(barrier, inc=1, device_id=other, device_id_type=MESH)
        pl.semaphore_wait(barrier, len(others))


DOUBLED = 3


class Gather:
    SLOTS = 37

    def __init__(self, blocks, full, send_sem, recv_sem, own_sem):
        self.blocks, self.full = blocks, full
        self.send_sem, self.recv_sem, self.own_sem = send_sem, recv_sem, own_sem
        self.peers = Peers()
        self.depth, self.width = blocks[0].shape
        self.closed = set()

    def at(self, k, z, x, y, c):
        rows = pl.ds(pl.multiple_of((z * 4 + x * 2 + c) * self.depth, 16), self.depth)
        cols = pl.ds(pl.multiple_of(y * self.width, 128), self.width)
        return self.full.at[k, rows, cols]

    def copy(self, k, place, target, slot, source=None):
        z, x, y, c = place
        there = self.at(k, *place)
        return pltpu.make_async_remote_copy(
            src_ref=there if source is None else source,
            dst_ref=there,
            send_sem=self.send_sem.at[k, slot],
            recv_sem=self.recv_sem.at[k, ((z * 2 + x) * 2 + y) * 2 + c],
            device_id=target,
            device_id_type=MESH,
        )

    def send(self, k, place, target, slot, source=None):
        self.copy(k, place, target, slot, source).start()

    def arrived(self, k, place):
        self.copy(k, place, self.peers.across_core(), 0).wait_recv()

    def own_copy(self, k):
        p = self.peers
        return pltpu.make_async_copy(self.blocks[k], self.at(k, p.z, p.x, p.y, p.c), self.own_sem.at[k])

    def launch(self, k):
        p, block = self.peers, self.blocks[k]
        own = (p.z, p.x, p.y, p.c)
        if k == DOUBLED:
            self.pass_on(k, 0, 0, self.at(k, *own), p.across_y(), block).start()
            self.own_copy(k).start()
            return
        for side in (1, -1):
            @pl.when(self.inside(p.z + side))
            def _():
                self.send(k, own, p.device(p.z + side, p.x, p.y, p.c), self.z_slot(0, side), block)
        self.send(k, own, p.across_x(), 0, block)
        self.send(k, own, p.across_y(), 1, block)
        self.send(k, own, p.across_core(), 2, block)
        self.own_copy(k).start()

    def inside(self, z):
        return (z >= 0) & (z < 4)

    def z_slot(self, hop, side):
        return 3 + 2 * hop + (1 if side > 0 else 0)

    def block(self, k, z, x):
        rows = pl.ds(pl.multiple_of((z * 4 + x * 2 + self.peers.c) * self.depth, 16), self.depth)
        return self.full.at[k, rows]

    def cores(self, k, c):
        return self.full.at[k].reshape(8, 2, self.depth, 2 * self.width).at[:, c]

    def pass_on(self, k, slot, place, there, target, source=None):
        return pltpu.make_async_remote_copy(
            src_ref=there if source is None else source,
            dst_ref=there,
            send_sem=self.send_sem.at[k, slot],
            recv_sem=self.recv_sem.at[k, place],
            device_id=target,
            device_id_type=MESH,
        )

    def from_block(self, k, z, x):
        self.pass_on(k, 0, 1 + 2 * z + x, self.block(k, z, x), self.peers.across_core()).wait_recv()

    def to_block(self, k, slot, z, x, target):
        self.pass_on(k, slot, 1 + 2 * z + x, self.block(k, z, x), target).start()

    def doubling(self, k, step):
        p = self.peers
        far, near = lax.rem(p.z + 2, 4), p.z + 1 - 2 * lax.rem(p.z, 2)
        to_far, to_near = p.device(far, p.x, p.y, p.c), p.device(near, p.x, p.y, p.c)
        if step == 0:
            self.own_copy(k).wait()
            self.pass_on(k, 0, 0, self.at(k, p.z, p.x, 1 - p.y, p.c), p.across_y()).wait_recv()
            self.to_block(k, 1, p.z, p.x, p.across_x())
        elif step == 1:
            self.from_block(k, p.z, 1 - p.x)
        elif step in (2, 3):
            self.to_block(k, step, p.z, p.x if step == 2 else 1 - p.x, to_far)
        elif step in (4, 5):
            self.to_block(k, step, p.z, p.x if step == 4 else 1 - p.x, to_near)
        elif step in (6, 7):
            x = p.x if step == 6 else 1 - p.x
            self.from_block(k, far, x)
            self.to_block(k, step, far, x, to_near)
        else:
            for z in (near, lax.rem(near + 2, 4)):
                for x in range(2):
                    self.from_block(k, z, x)
            self.pass_on(k, 8, 9, self.cores(k, p.c), p.across_core()).start()

    def from_z(self, k, hop):
        p = self.peers
        for side in (1, -1):
            z = p.z - side * hop
            place = (z, p.x, p.y, p.c)

            @pl.when(self.inside(z))
            def _():
                self.arrived(k, place)
                if hop < 3:
                    @pl.when(self.inside(p.z + side))
                    def _():
                        self.send(k, place, p.device(p.z + side, p.x, p.y, p.c), self.z_slot(hop, side))
                self.send(k, place, p.across_x(), 9 + z)
                self.send(k, place, p.across_y(), 13 + z)
                self.send(k, place, p.across_core(), 17 + z)

    def from_plane(self, k):
        p = self.peers
        for z in range(4):
            place = (z, 1 - p.x, p.y, p.c)
            self.arrived(k, place)
            if z % 2 == 1:
                self.send(k, place, p.across_y(), 29 + z)
            self.send(k, place, p.across_core(), 21 + z)
            place = (z, p.x, 1 - p.y, p.c)
            self.arrived(k, place)
            if z % 2 == 0:
                self.send(k, place, p.across_x(), 29 + z)
            self.send(k, place, p.across_core(), 25 + z)

    def from_corner(self, k):
        p = self.peers
        for z in range(4):
            place = (z, 1 - p.x, 1 - p.y, p.c)
            self.arrived(k, place)
            self.send(k, place, p.across_core(), 33 + z)

    def ready(self, k):
        p = self.peers
        if k == DOUBLED:
            self.pass_on(k, 0, 9, self.cores(k, 1 - p.c), p.across_core()).wait_recv()
            return
        self.own_copy(k).wait()
        for z in range(4):
            for x in range(2):
                for y in range(2):
                    self.arrived(k, (z, x, y, 1 - p.c))

    def close(self, k):
        if k in self.closed:
            return
        self.closed.add(k)
        p = self.peers
        own = (p.z, p.x, p.y, p.c)

        if k == DOUBLED:
            self.pass_on(k, 0, 0, self.at(k, *own), p.across_y()).wait_send()
            for slot in range(1, 8):
                self.pass_on(k, slot, 0, self.block(k, p.z, p.x), p.across_x()).wait_send()
            self.pass_on(k, 8, 9, self.cores(k, p.c), p.across_core()).wait_send()
            return

        def sent(slot):
            self.copy(k, own, p.across_core(), slot).wait_send()

        for slot in (0, 1, 2) + tuple(range(21, 37)):
            sent(slot)
        for step in (1, 2, 3):
            z = lax.rem(p.z + step, 4)
            for base in (9, 13, 17):
                sent(base + z)
        for hop in range(3):
            for side in (1, -1):
                @pl.when(self.inside(p.z - side * hop) & self.inside(p.z + side))
                def _():
                    sent(self.z_slot(hop, side))


class Loaded:
    def __init__(self, blocks, full, own_sem):
        self.blocks, self.full, self.own_sem = blocks, full, own_sem

    def own_copy(self, k):
        return pltpu.make_async_copy(self.blocks[k], self.full.at[k], self.own_sem.at[k])

    def launch(self, k):
        self.own_copy(k).start()

    def from_z(self, *_):
        pass

    from_plane = from_corner = close = doubling = from_z

    def ready(self, k):
        self.own_copy(k).wait()


ORDER = (5, 4, 3, 2, 0, 1)
JOBS = len(ORDER)


class Scatter:
    def __init__(self, full, outs, first_x, first_y, last_x, last_y, own, far, out_vmem, send_sem, recv_sem, credit, out_sem):
        self.full, self.own, self.far, self.outs = full, own, far, outs
        self.first_x, self.first_y, self.last_x, self.last_y = first_x, first_y, last_x, last_y
        self.out_vmem, self.out_sem = out_vmem, out_sem
        self.send_sem, self.recv_sem, self.credit = send_sem, recv_sem, credit
        self.peers = Peers()
        self.depth, self.width = own.shape[2:]
        self.left = [4] * JOBS
        self.sent = set()

    def remote(self, j, slot, source, there, target):
        return pltpu.make_async_remote_copy(
            src_ref=source,
            dst_ref=there,
            send_sem=self.send_sem.at[j, slot],
            recv_sem=self.recv_sem.at[j, slot],
            device_id=target,
            device_id_type=MESH,
        )

    def grad(self, j):
        return self.full.at[j % 2].reshape(8, 2, self.depth, 2 * self.width)

    def pair(self, j):
        return self.full.at[2].reshape(2, 8, self.depth, 2 * self.width).at[j % 2]

    def half(self, which):
        return pl.ds(pl.multiple_of(which * self.width, 128), self.width)

    def cores(self, j):
        return self.remote(j, 0, self.grad(j).at[:, 1 - self.peers.c], self.pair(j), self.peers.across_core())

    def out_x(self, j, n):
        p = self.peers
        return self.remote(j, 1 + n, self.pair(j).at[2 * n + 1 - p.x], self.first_x.at[j, n], p.across_x())

    def out_y(self, j, n):
        p = self.peers
        z = 3 - n
        return self.remote(
            j, 3 + n, self.pair(j).at[2 * z : 2 * z + 2, :, self.half(1 - p.y)], self.first_y.at[j, n], p.across_y()
        )

    def then_y(self, j, n):
        p = self.peers
        return self.remote(j, 5 + n, self.first_x.at[j, n, :, self.half(1 - p.y)], self.last_y.at[j, n], p.across_y())

    def then_x(self, j, n):
        p = self.peers
        return self.remote(j, 7 + n, self.first_y.at[j, n, 1 - p.x], self.last_x.at[j, n], p.across_x())

    def along(self, j, z):
        p = self.peers
        place = lax.rem(p.z - z + 4, 4) - 1
        return self.remote(j, 9 + place, self.own.at[j % 3, z], self.far.at[j, place], p.device(z, p.x, p.y, p.c))

    def open(self):
        pl.semaphore_signal(self.credit, inc=2, device_id=self.peers.across_core(), device_id_type=MESH)

    def start(self, j):
        pl.semaphore_wait(self.credit, 1)
        self.cores(j).start()

    def pair_sum(self, j):
        p = self.peers
        self.cores(j).wait_recv()
        mine, sums = self.grad(j), self.pair(j)

        @pl.loop(0, 8)
        def _(n):
            sums[n] = mine[n, p.c] + sums[n]

        for n in range(2):
            self.out_x(j, n).start()
            self.out_y(j, n).start()
        self.cores(j).wait_send()

    def used(self, j):
        self.left[j] -= 1
        if self.left[j] == 0:
            for n in range(2):
                self.out_x(j, n).wait_send()
                self.out_y(j, n).wait_send()
            if j + 2 < JOBS:
                pl.semaphore_signal(self.credit, inc=1, device_id=self.peers.across_core(), device_id_type=MESH)

    def plane_x(self, j, n):
        p = self.peers
        self.out_x(j, n).wait_recv()
        self.first_x[j, n] = self.first_x[j, n] + self.pair(j)[2 * n + p.x]
        self.then_y(j, n).start()
        self.used(j)

    def plane_y(self, j, n):
        p = self.peers
        self.out_y(j, n).wait_recv()
        for x in range(2):
            mine = self.pair(j)[2 * (3 - n) + x, :, self.half(p.y)]
            self.first_y[j, n, x] = self.first_y[j, n, x] + mine
        self.then_x(j, n).start()
        self.used(j)

    def all_sent(self, j):
        if j >= 0 and j not in self.sent:
            self.sent.add(j)
            for step in (1, 2, 3):
                self.along(j, lax.rem(self.peers.z + step, 4)).wait_send()

    def plane_last(self, j, n):
        p = self.peers
        self.all_sent(j - 3)
        self.then_y(j, n).wait_recv()
        self.own[j % 3, n] = self.first_x[j, n, :, self.half(p.y)] + self.last_y[j, n]
        self.then_x(j, n).wait_recv()
        self.own[j % 3, 3 - n] = self.first_y[j, n, p.x] + self.last_x[j, n]
        for z in (n, 3 - n):
            @pl.when(p.z != z)
            def _():
                self.along(j, z).start()

    def out_copy(self, j):
        return pltpu.make_async_copy(self.out_vmem.at[j], self.outs[ORDER[j]], self.out_sem.at[j])

    def finish(self, j):
        p = self.peers
        total = self.own[j % 3, p.z].astype(F32)
        for step in (1, 2, 3):
            self.along(j, lax.rem(p.z + 4 - step, 4)).wait_recv()
        for place in range(3):
            total += self.far[j, place].astype(F32)
        self.out_vmem[j] = total
        self.out_copy(j).start()

    def end(self):
        p = self.peers
        for j in range(JOBS):
            for n in range(2):
                self.then_y(j, n).wait_send()
                self.then_x(j, n).wait_send()
            self.all_sent(j)
            self.out_copy(j).wait()


class Kept:
    def __init__(self, full, outs, sems):
        self.full, self.outs, self.sems = full, outs, sems

    def copy(self, j):
        return pltpu.make_async_copy(self.full.at[j % 2], self.outs[ORDER[j]], self.sems.at[j])

    def start(self, j):
        self.copy(j).start()

    def pair_sum(self, j):
        self.copy(j).wait()

    def open(self, *_):
        pass

    plane_x = plane_y = plane_last = finish = end = open


class Totals:
    def __init__(self, sums, got, far, send_sem, recv_sem):
        self.sums, self.got, self.far, self.send_sem, self.recv_sem = sums, got, far, send_sem, recv_sem
        self.peers = Peers()

    def copy(self, n, source, there, target):
        return pltpu.make_async_remote_copy(
            src_ref=source, dst_ref=there, send_sem=self.send_sem.at[n], recv_sem=self.recv_sem.at[n],
            device_id=target, device_id_type=MESH,
        )

    def pair(self, n):
        target = (self.peers.across_core, self.peers.across_x, self.peers.across_y)[n]()
        return self.copy(n, self.sums.at[n], self.got.at[n], target)

    def along(self, step):
        z = self.peers.z
        return self.copy(2 + step, self.sums.at[3], self.far.at[z], self.peers.along_z(step))

    def coming(self, step):
        z = lax.rem(self.peers.z - step + 4, 4)
        return self.copy(2 + step, self.sums.at[3], self.far.at[z], self.peers.along_z(step))

    def start(self, n):
        if n < 3:
            self.pair(n).start()
            return
        self.far[self.peers.z] = self.sums[3]
        for step in (1, 2, 3):
            self.along(step).start()

    def take(self, n):
        if n < 3:
            self.pair(n).wait_recv()
            self.sums[n + 1] = self.sums[n] + self.got[n]
            return None
        for step in (1, 2, 3):
            self.coming(step).wait_recv()
        return (self.far[0] + self.far[1]) + (self.far[2] + self.far[3])

    def end(self):
        for n in range(3):
            self.pair(n).wait_send()
        for step in (1, 2, 3):
            self.along(step).wait_send()


def gather_back(packed, group, right_ref, rows):
    row, col = block_offset()
    diagonal = jnp.where(row == col, 1.0, 0.0).astype(BF)
    parts = []
    for pair in range(4 * group, 4 * group + 4):
        left = jnp.concatenate(
            [roll_rows(packed, -(2 * pair + side)) * diagonal for side in range(2)], axis=1
        )
        win = pl.ds(head_window(pair), 256)
        parts.append(nn(left, split_heads(right_ref[rows, win], head_masks(pair))))
    return join_windows(parts)


def norm_back(values, gain, grad_in):
    factor = inverse_rms(values)
    inner = jnp.mean(grad_in * gain * values, axis=-1, keepdims=True)
    grad_out = factor * gain * grad_in - values * (factor * factor * factor * inner)
    return grad_out, jnp.sum(grad_in * values * factor, axis=0, keepdims=True)


def allowed_keys(segments):
    query = jnp.broadcast_to(segments.astype(F32), (SEQ, SEQ))
    row, col = block_offset()
    key_at = lax.broadcasted_iota(jnp.int32, (SEQ, SEQ), 0)
    query_at = lax.broadcasted_iota(jnp.int32, (SEQ, SEQ), 1)
    seen = (query.T == query) & (row == col) & (key_at <= query_at)
    return jnp.sum(jnp.where(seen, 1.0, 0.0).reshape(8, PATCHES, SEQ), axis=0)


SCHEDULE = (
    ("launch", 0), ("launch", 3), ("launch", 2), ("launch", 1), ("Z", 2, 1), ("n1", 0, 1), ("Z", 1, 1), ("n1", 1, 4),
    ("tr", 0, 1), ("D", 3, 0), ("Z", 1, 2), ("D", 3, 2), ("D", 3, 4), ("Z", 1, 3), ("Z", 0, 1), ("P", 1),
    ("Z", 2, 2), ("Z", 0, 2), ("C", 1), ("D", 3, 1), ("Z", 2, 3), ("tr", 1, 2), ("D", 3, 5), ("D", 3, 3),
    ("tr", 2, 3), ("Z", 0, 3), ("R", 1), ("tr", 3, 4), ("k", 0, 2), ("P", 2), ("P", 0), ("k", 2, 3), ("launch", 4),
    ("k", 3, 4), ("launch", 5), ("C", 2), ("Z", 4, 1), ("D", 3, 6), ("R", 2), ("v", 0, 3), ("C", 0), ("v", 3, 4),
    ("Z", 4, 2), ("Z", 5, 1), ("R", 0), ("D", 3, 7), ("q", 0, 4), ("af", 0, 3), ("Z", 4, 3), ("af", 3, 4),
    ("Z", 5, 2), ("af", 4, 6), ("D", 3, 8), ("P", 4), ("af", 6, 8), ("Z", 5, 3), ("R", 3), ("o", 0, 2), ("C", 4),
    ("o", 2, 4), ("R", 4), ("P", 5), ("u", 0, 4), ("C", 5), ("gwd", 0, 3), ("R", 5), ("ga", 0, 1), ("gwd", 3, 4),
    ("ga", 1, 4), ("gwu", 0, 1), ("gwd", 4, 5), ("s", 0), ("gwu", 1, 5), ("p", 0), ("y", 0, 4), ("gn2", 0, 1),
    ("Y", 0, 0), ("s", 1), ("gn2", 1, 3), ("X", 0, 0), ("gn2", 3, 4), ("p", 1), ("gwo", 0, 4), ("X", 0, 1),
    ("Y", 0, 1), ("gwo", 4, 5), ("s", 2), ("gatt", 0, 1), ("X", 1, 0), ("gatt", 1, 4), ("p", 2), ("Y", 1, 1),
    ("ab", 0, 2), ("Y", 1, 0), ("ab", 2, 6), ("Y", 2, 0), ("ab", 6, 8), ("L", 0, 0), ("X", 1, 1), ("gwv", 0, 1),
    ("X", 2, 1), ("gwv", 1, 5), ("s", 3), ("L", 0, 1), ("X", 2, 0), ("gwq", 0, 1), ("Y", 2, 1), ("gwq", 1, 2),
    ("L", 1, 1), ("gwq", 2, 3), ("p", 3), ("gn1", 0, 1), ("F", 0), ("L", 2, 1), ("gwq", 3, 5), ("Y", 3, 0),
    ("X", 3, 0), ("gwk", 0, 1), ("L", 1, 0), ("s", 4), ("gn1", 1, 2), ("Y", 3, 1), ("X", 3, 1), ("gwk", 1, 2),
    ("L", 2, 0), ("p", 4), ("L", 3, 0), ("gwk", 2, 3), ("gn1", 2, 4), ("X", 4, 0), ("Y", 4, 0), ("L", 3, 1),
    ("t", 0), ("gwk", 3, 5), ("s", 5), ("T", 0), ("t", 1), ("X", 4, 1), ("Y", 4, 1), ("F", 1), ("F", 2), ("T", 1),
    ("t", 2), ("L", 4, 0), ("p", 5), ("T", 2), ("t", 3), ("Y", 5, 0), ("X", 5, 0), ("L", 4, 1), ("Y", 5, 1),
    ("L", 5, 0), ("F", 4), ("X", 5, 1), ("T", 3), ("F", 3), ("L", 5, 1), ("F", 5),
)


def layer_kernel(
    remote,
    x_hbm, g_hbm, seg_ref, dim_ref, gain_attn_in, gain_mlp_in, bias_q_in, bias_v_in, bias_o_in, bias_up_in, bias_down_in,
    w0, w1, w2, w3, w4, w5,
    y_out, in_grad_out, g0, g1, g2, g3, g4, g5,
    s_query, s_value, s_out, s_up, s_down, s_dim, s_gain_attn, s_gain_mlp, spill, n1_spill,
    full, b0, b1, b2, b3, b4, b5, b6, b7, res, probs, sums, vecs,
    own_sem, load_sem, *rest,
):
    tokens, width = b0.shape
    half = pl.multiple_of(lax.axis_index("heads") * tokens, SEQ)
    outs = (g0, g1, g2, g3, g4, g5)
    loads, stores = {}, {}

    def move(name, source, target):
        copy = pltpu.make_async_copy(source, target, load_sem.at[len(loads) + len(stores)])
        copy.start()
        return copy

    def load(name, source, target):
        loads[name] = move(name, source, target)

    def store(name, source, target):
        stores[name] = move(name, source, target)

    def loaded(*names):
        for name in names:
            if name in loads and name not in waited:
                loads[name].wait()
                waited.add(name)

    def stored(*names):
        for name in names:
            if name not in waited:
                stores[name].wait()
                waited.add(name)

    waited = set()
    load("x", x_hbm.at[pl.ds(half, tokens)], b0)
    if remote:
        Peers().enter()
        gather = Gather((w0, w1, w2, w3, w4, w5), full, rest[0], rest[1], own_sem)
        scatter = Scatter(full, outs, *rest[2:13])
        totals = Totals(sums, *rest[13:17])
    else:
        gather = Loaded((w0, w1, w2, w3, w4, w5), full, own_sem)
        scatter, totals = Kept(full, outs, rest[0]), None
    sums[0] = jnp.zeros(sums.shape[1:], F32)
    inputs = (gain_attn_in, gain_mlp_in, bias_q_in, bias_v_in, bias_o_in, bias_up_in, bias_down_in)
    for n, vector in enumerate(inputs):
        vecs[n : n + 1] = vector[...].reshape(1, width)
    factor = QUERY_BASE / math.sqrt(DH)
    dims = dim_ref[...].reshape(1, DH)
    softplus = jnp.maximum(dims, 0.0) + jnp.log(1.0 + jnp.exp(-jnp.abs(dims)))
    vecs[7:8] = jnp.concatenate([factor * softplus] * (width // DH), axis=1)
    gain_attn_ref, gain_mlp_ref, bias_q_ref, bias_v_ref = (vecs.at[n : n + 1] for n in range(4))
    bias_o_ref, bias_up_ref, bias_down_ref, scale_ref = (vecs.at[n : n + 1] for n in range(4, 8))
    small = sums.at[0]
    every = slice(None)

    def add_to(row, cols, values):
        small[row : row + 1, cols] = small[row : row + 1, cols] + values

    def over(first, last, size, body):
        if last - first == 1:
            body(pl.ds(first * size, size), first)
            return

        @pl.loop(first, last)
        def _(i):
            body(tile(i, size), i)

    def normed_one(first, last):
        loaded("x")

        def body(rows, i):
            values = b0[rows].astype(F32)
            b1[rows] = (values * inverse_rms(values) * gain_attn_ref[...]).astype(BF)

        over(first, last, ROWS, body)

    split = width // ROWS - 1

    def turn(first, last):
        for i in range(first, last):
            rows = pl.ds(i * ROWS, ROWS)
            for n in range(split + 1):
                piece = b1[rows, n * ROWS : (n + 1) * ROWS].T
                if n < split:
                    b3[n * ROWS : (n + 1) * ROWS, rows] = piece
                else:
                    b3[rows, n * ROWS :] = piece
        if last * ROWS == tokens:
            store("n1_out", b3, n1_spill)

    def query(first, last):
        def body(rows, i):
            b4[rows] = ((nn(b1[rows], full[0]) + bias_q_ref[...]) * scale_ref[...]).astype(BF)

        over(first, last, ROWS, body)

    def key(first, last):
        def body(rows, i):
            b5[rows] = nn(b1[rows], full[1]).astype(BF)

        over(first, last, ROWS, body)

    def value(first, last):
        def body(rows, i):
            b6[rows] = (nn(b1[rows], full[2]) + bias_v_ref[...]).astype(BF)

        over(first, last, ROWS, body)

    def attend(first, last):
        def body(rows, i):
            allowed = jnp.concatenate([allowed_keys(seg_ref[pl.ds(lax.axis_index("heads") * (tokens // SEQ) + i, 1)])] * 8, axis=0)
            for group in range(2):
                part = softmax_packed(pack_scores(b5, b4, rows, group), allowed)
                probs[i, group] = part.astype(BF)
                b1[rows, 640 * group : 640 * (group + 1)] = spread(part.T.astype(BF), group, b6, rows).astype(BF)

        over(first, last, SEQ, body)

    def attend_out(first, last):
        def body(rows, i):
            total = b0[rows].astype(F32) + nt(b1[rows], full[3]) + bias_o_ref[...]
            res[rows] = total
            b2[rows] = (total * inverse_rms(total) * gain_mlp_ref[...]).astype(BF)

        over(first, last, ROWS, body)
        if last * ROWS == tokens:
            load("g", g_hbm.at[pl.ds(half, tokens)], b0)

    def up(first, last):
        stored("n1_out")

        def body(rows, i):
            up_proj = nn(b2[rows], full[4]) + bias_up_ref[...]
            square = up_proj * up_proj
            tanh = jnp.tanh(GELU_C * up_proj * (1.0 + 0.044715 * square))
            b7[rows] = (0.5 * up_proj * (1.0 + tanh)).astype(BF)
            slope = 0.5 * (1.0 + tanh) + 0.5 * up_proj * (1.0 - tanh * tanh) * (
                GELU_C * (1.0 + 3 * 0.044715 * square)
            )
            b3[rows] = slope.astype(BF)

        over(first, last, ROWS, body)

    def weight_grad(slot, left, right):
        def run(first, last):
            def body(cols, i):
                full[slot, cols] = tn(left[:, cols], right[...]).astype(BF)

            over(first, last, ROWS, body)

        return run

    down_grad = weight_grad(0, b0, b7)

    def grad_down(first, last):
        loaded("g")
        if remote:
            stored("w0", "w2")
        gather.close(0)
        if first == 0:
            gather.close(2)
            scatter.open()
        down_grad(first, last)

    def down(first, last):
        def body(rows, i):
            b7[rows] = (res[rows] + nt(b7[rows], full[5]) + bias_down_ref[...]).astype(BF)

        over(first, last, ROWS, body)
        rows = pl.ds(first * ROWS, (last - first) * ROWS)
        store(f"y{first}", b7.at[rows], y_out.at[rows])

    def grad_act(first, last):
        def body(rows, i):
            grad_up = (nn(b0[rows], full[5]) * b3[rows].astype(F32)).astype(BF)
            b3[rows] = grad_up
            add_to(7, every, jnp.sum(grad_up.astype(F32), axis=0, keepdims=True))
            add_to(3, every, jnp.sum(b0[rows].astype(F32), axis=0, keepdims=True))

        over(first, last, ROWS, body)

    up_grad = weight_grad(1, b2, b3)

    def grad_up(first, last):
        if remote:
            stored("w1")
        gather.close(1)
        up_grad(first, last)

    def reload(k, slot):
        gather.close(slot)
        load(f"again{k}", spill.at[k] if remote else (w0, w1, w2)[k], full.at[slot])

    def norm_two_back(first, last):
        if first == 0:
            reload(0, 5)

        def body(rows, i):
            back, gain_sum = norm_back(res[rows], gain_mlp_ref[...], nt(b3[rows], full[4]))
            total = b0[rows].astype(F32) + back
            res[rows] = total
            b2[rows] = total.astype(BF)
            add_to(1, every, gain_sum)
            add_to(2, every, jnp.sum(total, axis=0, keepdims=True))

        over(first, last, ROWS, body)
        if last * ROWS == tokens:
            reload(1, 4)
            load("n1", n1_spill, b3)

    grad_out = weight_grad(0, b2, b1)

    def attended_grad(first, last):
        if first == 0:
            load("x2", x_hbm.at[pl.ds(half, tokens)], b1)

        def body(rows, i):
            b0[rows] = nn(b2[rows], full[3]).astype(BF)

        over(first, last, ROWS, body)
        if last * ROWS == tokens:
            reload(2, 3)

    def attend_back(first, last):
        def body(rows, i):
            for group in range(2):
                cols = slice(640 * group, 640 * (group + 1))
                soft = probs[i, group]
                grad_soft = pack_scores(b6, b0, rows, group).reshape(8, PATCHES, SEQ)
                soft_f = soft.astype(F32).reshape(8, PATCHES, SEQ)
                inner = jnp.sum(soft_f * grad_soft, axis=1, keepdims=True)
                grad_scores = (soft_f * (grad_soft - inner)).reshape(SEQ, SEQ)
                grad_q = spread(grad_scores.T.astype(BF), group, b5, rows)
                grad_k = gather_back(grad_scores.astype(BF), group, b4, rows).astype(BF)
                grad_v = gather_back(soft, group, b0, rows).astype(BF)
                add_to(4, cols, jnp.sum(grad_q * b4[rows, cols].astype(F32), axis=0, keepdims=True))
                grad_q = (grad_q * scale_ref[:, cols]).astype(BF)
                add_to(5, cols, jnp.sum(grad_q.astype(F32), axis=0, keepdims=True))
                add_to(6, cols, jnp.sum(grad_v.astype(F32), axis=0, keepdims=True))
                b4[rows, cols] = grad_q
                b5[rows, cols] = grad_k
                b6[rows, cols] = grad_v

        over(first, last, SEQ, body)

    def inward_grad(slot, right):
        def run(first, last):
            loaded("n1")

            def body(cols, i):
                full[slot, cols] = nn(b3[cols, : split * ROWS], right[...]).astype(BF)

            if first < min(last, split):
                over(first, min(last, split), ROWS, body)
            if last > split:
                left = jnp.concatenate([b3[n * ROWS : (n + 1) * ROWS, split * ROWS :] for n in range(split)], axis=1)
                full[slot, split * ROWS :] = nn(left, right[...]).astype(BF)

        return run

    def norm_one_back(first, last):
        loaded("again0", "again1", "again2", "x2")

        def body(rows, i):
            grad_norm = nt(b4[rows], full[5]) + nt(b5[rows], full[4]) + nt(b6[rows], full[3])
            back, gain_sum = norm_back(b1[rows].astype(F32), gain_attn_ref[...], grad_norm)
            res[rows] = res[rows] + back
            add_to(0, every, gain_sum)

        over(first, last, ROWS, body)
        rows = pl.ds(first * ROWS, (last - first) * ROWS)
        store(f"dx{first}", res.at[rows], in_grad_out.at[rows])

    def arrived(k):
        gather.ready(k)
        if remote and k < 3:
            store(f"w{k}", full.at[k], spill.at[k])

    def total_start(n):
        if remote:
            totals.start(n)

    def total_take(n):
        done = totals.take(n) if remote else sums[0]
        if n < 3:
            return
        by_lane = done[4:5] / scale_ref[...]
        by_dim = by_lane[:, :DH]
        for head in range(1, width // DH):
            by_dim = by_dim + by_lane[:, DH * head : DH * (head + 1)]
        s_dim[...] = (by_dim * (factor / (1.0 + jnp.exp(-dims)))).reshape(DH)
        rows = ((s_query, 5), (s_value, 6), (s_out, 2), (s_up, 7), (s_down, 3), (s_gain_attn, 0), (s_gain_mlp, 1))
        for target, row in rows:
            target[...] = done[row : row + 1].reshape(width)

    steps = {
        "launch": gather.launch, "Z": gather.from_z, "P": gather.from_plane, "C": gather.from_corner, "R": arrived, "D": gather.doubling,
        "n1": normed_one, "q": query, "k": key, "v": value, "af": attend, "o": attend_out, "u": up, "gwd": grad_down,
        "y": down, "ga": grad_act, "gwu": grad_up, "gn2": norm_two_back, "gwo": grad_out, "gatt": attended_grad,
        "ab": attend_back, "gwv": inward_grad(1, b6), "gwq": inward_grad(0, b4), "gwk": inward_grad(1, b5), "tr": turn,
        "gn1": norm_one_back, "s": scatter.start, "p": scatter.pair_sum, "X": scatter.plane_x, "Y": scatter.plane_y,
        "L": scatter.plane_last, "F": scatter.finish, "t": total_start, "T": total_take,
    }
    for name, *numbers in SCHEDULE:
        steps[name](*numbers)
    for name, copy in list(stores.items()):
        if name not in waited:
            copy.wait()
    scatter.end()
    if remote:
        totals.end()


def layer(remote, tokens, x, g, segments, vectors, weights):
    d = x.shape[1]
    hbm, vmem = pl.BlockSpec(memory_space=pl.ANY), pl.BlockSpec(memory_space=pltpu.VMEM)
    dma, regular = pltpu.SemaphoreType.DMA, pltpu.SemaphoreType.REGULAR
    big = pltpu.VMEM((tokens, d), BF)
    sums = pltpu.VMEM((4 if remote else 1, 8, d), F32)
    scratch = [pltpu.VMEM((6, d, d), BF)] + [big] * 8
    scratch += [pltpu.VMEM((tokens, d), F32), pltpu.VMEM((tokens // SEQ, 2, SEQ, SEQ), BF), sums, pltpu.VMEM((8, d), F32), dma((6,)), dma((24,))]
    if remote:
        depth, width = d // lax.axis_size("wide"), d // lax.axis_size("heads")
        block = (depth, width)
        scratch += [
            dma((6, Gather.SLOTS)), dma((6, 32)),
            pltpu.VMEM((JOBS, 2, depth, d), BF), pltpu.VMEM((JOBS, 2, 2) + block, BF),
            pltpu.VMEM((JOBS, 2) + block, BF), pltpu.VMEM((JOBS, 2) + block, BF),
            pltpu.VMEM((3, 4) + block, BF), pltpu.VMEM((JOBS, 3) + block, BF),
            pltpu.VMEM((JOBS,) + block, F32),
            dma((JOBS, 12)), dma((JOBS, 12)), regular, dma((JOBS,)),
            pltpu.VMEM((3, 8, d), F32), pltpu.VMEM((4, 8, d), F32), dma((6,)), dma((6,)),
        ]
        grads = [jax.ShapeDtypeStruct(block, F32)] * 6
    else:
        scratch += [dma((JOBS,))]
        grads = [jax.ShapeDtypeStruct((d, d), BF)] * 6
    outs = [
        jax.ShapeDtypeStruct((tokens, d), BF), jax.ShapeDtypeStruct((tokens, d), F32), *grads,
        *[jax.ShapeDtypeStruct((DH if n == 5 else d,), F32) for n in range(8)], jax.ShapeDtypeStruct((3, d, d), BF), jax.ShapeDtypeStruct((tokens, d), BF),
    ]
    return pl.pallas_call(
        functools.partial(layer_kernel, remote),
        out_shape=outs,
        in_specs=[hbm, hbm] + [vmem] * 9 + [hbm] * 6,
        out_specs=[hbm] * 8 + [vmem] * 8 + [hbm] * 2,
        scratch_shapes=scratch,
        compiler_params=pltpu.CompilerParams(
            collective_id=0 if remote else None,
            has_side_effects=remote,
            vmem_limit_bytes=63 * 2**20,
        ),
        name="layer",
    )(x, g, segments, *vectors, *weights)


def deliver_kernel(parts, *refs):
    count = len(parts)
    sources, targets, held, sems = refs[:count], refs[count : 2 * count], refs[2 * count : 3 * count], refs[3 * count]
    steps = []
    for source, target, middle, cut in zip(sources, targets, held, parts):
        depth = source.shape[0] // cut
        for n in range(cut):
            rows = pl.ds(n * depth, depth)
            first = pltpu.make_async_copy(source.at[rows], middle.at[rows], sems.at[0, len(steps)])
            first.start()
            steps.append((first, pltpu.make_async_copy(middle.at[rows], target.at[rows], sems.at[1, len(steps)])))
    for first, second in steps:
        first.wait()
        second.start()
    for first, second in steps:
        second.wait()


def deliver(arrays):
    parts = [8 if a.size >= 2**20 else 1 for a in arrays]
    hbm = pl.BlockSpec(memory_space=pl.ANY)
    return pl.pallas_call(
        functools.partial(deliver_kernel, parts),
        out_shape=[jax.ShapeDtypeStruct(a.shape, a.dtype) for a in arrays],
        in_specs=[hbm] * len(arrays),
        out_specs=[hbm] * len(arrays),
        scratch_shapes=[pltpu.VMEM(a.shape, a.dtype) for a in arrays] + [pltpu.SemaphoreType.DMA((2, sum(parts)))],
        compiler_params=pltpu.CompilerParams(vmem_limit_bytes=62 * 2**20),
        name="deliver",
    )(*arrays)


def shards(
    inputs, segment_ids, cotangent, w_query, w_key, w_value, w_out, w_up, w_down,
    b_query, b_value, b_out, b_up, b_down, dim_scale, gain_attn, gain_mlp,
):
    tokens = inputs.shape[0] // lax.axis_size("heads")
    remote = lax.axis_size("wide") == 16 and lax.axis_size("heads") == 2
    vectors = (dim_scale, gain_attn, gain_mlp, b_query, b_value, b_out, b_up, b_down)
    weights = [w_query, w_key, w_value, w_out.T, w_up, w_down.T]
    if not remote:
        weights = [
            lax.all_gather(lax.all_gather(w, "heads", axis=1, tiled=True), "wide", axis=0, tiled=True) for w in weights
        ]
    output, input_grad, *rest = layer(remote, tokens, inputs, cotangent, segment_ids.reshape(-1, SEQ), vectors, weights)
    rest = rest[:14]
    if remote:
        output, input_grad, *rest = deliver([output, input_grad, *rest])
    grads, sums = rest[:6], rest[6:]
    if not remote:
        grads = [lax.psum_scatter(grad, "wide", scatter_dimension=0, tiled=True) for grad in grads]
        grads = [lax.psum_scatter(grad, "heads", scatter_dimension=1, tiled=True).astype(F32) for grad in grads]
        sums = lax.psum(sums, ("wide", "heads"))
    grads[3], grads[5] = grads[3].T, grads[5].T
    return (output, input_grad, *grads, *sums)


def solution(mesh):
    token, both = P("wide", None), P(("wide", "heads"), None)
    tall, flat = P("wide", "heads"), P("heads", "wide")
    return jax.shard_map(
        shards,
        mesh=mesh,
        in_specs=(token, P("wide"), token, tall, tall, tall, flat, tall, flat) + (P(),) * 8,
        out_specs=(both, both, tall, tall, tall, flat, tall, flat) + (P(),) * 8,
        check_vma=False,
    )
```

```python
import functools
import math

import jax
import jax.numpy as jnp
from jax import lax
from jax.experimental import pallas as pl
from jax.experimental.pallas import tpu as pltpu
from jax.sharding import PartitionSpec as P

DH = 80
PATCHES = 16
EPS = 1e-06
QUERY_BASE = 1.442695041
BF = jnp.bfloat16
F32 = jnp.float32
MESH = pl.DeviceIdType.MESH
ROWS = 256
SEQ = 128
GELU_C = math.sqrt(2.0 / math.pi)


def nn(left, right):
    return jnp.dot(left, right, preferred_element_type=F32)


def nt(left, right):
    return lax.dot_general(left, right, (((1,), (1,)), ((), ())), preferred_element_type=F32)


def tn(left, right):
    return lax.dot_general(left, right, (((0,), (0,)), ((), ())), preferred_element_type=F32)


def inverse_rms(values):
    return lax.rsqrt(jnp.mean(values * values, axis=-1, keepdims=True) + EPS)


def tile(index, size):
    return pl.ds(pl.multiple_of(index * size, size), size)


def head_window(pair):
    return (2 * DH * pair) // 128 * 128


def head_masks(pair):
    lanes = head_window(pair) + lax.broadcasted_iota(jnp.int32, (SEQ, 256), 1)
    picks = []
    for head in (2 * pair, 2 * pair + 1):
        inside = (lanes >= DH * head) & (lanes < DH * (head + 1))
        picks.append(jnp.where(inside, 1.0, 0.0).astype(BF))
    return picks


def block_offset():
    row = lax.broadcasted_iota(jnp.int32, (SEQ, SEQ), 0) // PATCHES
    col = lax.broadcasted_iota(jnp.int32, (SEQ, SEQ), 1) // PATCHES
    return row, col


def roll_rows(values, blocks):
    shift = (blocks % 8) * PATCHES
    if shift == 0:
        return values
    return jnp.concatenate([values[SEQ - shift :], values[: SEQ - shift]], axis=0)


def split_heads(window, masks):
    return jnp.concatenate([window * masks[0], window * masks[1]], axis=0)


def split_rolled(window, masks, slots):
    return jnp.concatenate(
        [roll_rows(window, slots[0]) * masks[0], roll_rows(window, slots[1]) * masks[1]], axis=0
    )


def pack_scores(left_ref, right_ref, rows, group):
    row, col = block_offset()
    offset = lax.rem(row - col + 8, 8)
    packed = jnp.zeros((SEQ, SEQ), F32)
    for pair in range(4 * group, 4 * group + 4):
        win = pl.ds(head_window(pair), 256)
        both = nt(left_ref[rows, win], split_heads(right_ref[rows, win], head_masks(pair)))
        for side in range(2):
            slot = (2 * pair + side) % 8
            one = roll_rows(both[:, SEQ * side : SEQ * (side + 1)], slot)
            packed = jnp.where(offset == slot, one, packed)
    return packed


def spread(packed, group, right_ref, rows):
    row, col = block_offset()
    offset = lax.rem(col - row + 8, 8)
    parts = []
    for pair in range(4 * group, 4 * group + 4):
        slots = (2 * pair % 8, (2 * pair + 1) % 8)
        left = jnp.concatenate(
            [packed * jnp.where(offset == s, 1.0, 0.0).astype(BF) for s in slots], axis=1
        )
        win = pl.ds(head_window(pair), 256)
        parts.append(nn(left, split_rolled(right_ref[rows, win], head_masks(pair), slots)))
    return join_windows(parts)


def join_windows(parts):
    tiles = [parts[0][:, :128]]
    for before, after in zip(parts[:-1], parts[1:]):
        tiles.append(before[:, 128:] + after[:, :128])
    tiles.append(parts[-1][:, 128:])
    return jnp.concatenate(tiles, axis=1)


def softmax_packed(packed, allowed):
    scores = jnp.where(allowed > 0.5, packed, -1e30).reshape(8, PATCHES, SEQ)
    exps = jnp.exp(scores - jnp.max(scores, axis=1, keepdims=True))
    return (exps / jnp.sum(exps, axis=1, keepdims=True)).reshape(SEQ, SEQ)


class Peers:
    def __init__(self):
        wide = lax.axis_index("wide")
        self.y = lax.axis_index("heads")
        self.z = wide // 4
        self.x = lax.rem(wide // 2, 2)
        self.c = lax.rem(wide, 2)

    def device(self, z, x, y, c):
        return ((z * 2 + x) * 2 + c, y)

    def across_x(self):
        return self.device(self.z, 1 - self.x, self.y, self.c)

    def across_y(self):
        return self.device(self.z, self.x, 1 - self.y, self.c)

    def across_core(self):
        return self.device(self.z, self.x, self.y, 1 - self.c)

    def along_z(self, step):
        return self.device(lax.rem(self.z + step, 4), self.x, self.y, self.c)

    def enter(self):
        barrier = pltpu.get_barrier_semaphore()
        others = [self.across_x(), self.across_y(), self.across_core()]
        others += [self.along_z(step) for step in (1, 2, 3)]
        for other in others:
            pl.semaphore_signal(barrier, inc=1, device_id=other, device_id_type=MESH)
        pl.semaphore_wait(barrier, len(others))


DOUBLED = 3


class Gather:
    SLOTS = 37

    def __init__(self, blocks, full, send_sem, recv_sem, own_sem):
        self.blocks, self.full = blocks, full
        self.send_sem, self.recv_sem, self.own_sem = send_sem, recv_sem, own_sem
        self.peers = Peers()
        self.depth, self.width = blocks[0].shape
        self.closed = set()

    def at(self, k, z, x, y, c):
        rows = pl.ds(pl.multiple_of((z * 4 + x * 2 + c) * self.depth, 16), self.depth)
        cols = pl.ds(pl.multiple_of(y * self.width, 128), self.width)
        return self.full.at[k, rows, cols]

    def copy(self, k, place, target, slot, source=None):
        z, x, y, c = place
        there = self.at(k, *place)
        return pltpu.make_async_remote_copy(
            src_ref=there if source is None else source,
            dst_ref=there,
            send_sem=self.send_sem.at[k, slot],
            recv_sem=self.recv_sem.at[k, ((z * 2 + x) * 2 + y) * 2 + c],
            device_id=target,
            device_id_type=MESH,
        )

    def send(self, k, place, target, slot, source=None):
        self.copy(k, place, target, slot, source).start()

    def arrived(self, k, place):
        self.copy(k, place, self.peers.across_core(), 0).wait_recv()

    def own_copy(self, k):
        p = self.peers
        return pltpu.make_async_copy(self.blocks[k], self.at(k, p.z, p.x, p.y, p.c), self.own_sem.at[k])

    def launch(self, k):
        p, block = self.peers, self.blocks[k]
        own = (p.z, p.x, p.y, p.c)
        if k == DOUBLED:
            self.pass_on(k, 0, 0, self.at(k, *own), p.across_y(), block).start()
            self.own_copy(k).start()
            return
        for side in (1, -1):
            @pl.when(self.inside(p.z + side))
            def _():
                self.send(k, own, p.device(p.z + side, p.x, p.y, p.c), self.z_slot(0, side), block)
        self.send(k, own, p.across_x(), 0, block)
        self.send(k, own, p.across_y(), 1, block)
        self.send(k, own, p.across_core(), 2, block)
        self.own_copy(k).start()

    def inside(self, z):
        return (z >= 0) & (z < 4)

    def z_slot(self, hop, side):
        return 3 + 2 * hop + (1 if side > 0 else 0)

    def block(self, k, z, x):
        rows = pl.ds(pl.multiple_of((z * 4 + x * 2 + self.peers.c) * self.depth, 16), self.depth)
        return self.full.at[k, rows]

    def cores(self, k, c):
        return self.full.at[k].reshape(8, 2, self.depth, 2 * self.width).at[:, c]

    def pass_on(self, k, slot, place, there, target, source=None):
        return pltpu.make_async_remote_copy(
            src_ref=there if source is None else source,
            dst_ref=there,
            send_sem=self.send_sem.at[k, slot],
            recv_sem=self.recv_sem.at[k, place],
            device_id=target,
            device_id_type=MESH,
        )

    def from_block(self, k, z, x):
        self.pass_on(k, 0, 1 + 2 * z + x, self.block(k, z, x), self.peers.across_core()).wait_recv()

    def to_block(self, k, slot, z, x, target):
        self.pass_on(k, slot, 1 + 2 * z + x, self.block(k, z, x), target).start()

    def doubling(self, k, step):
        p = self.peers
        far, near = lax.rem(p.z + 2, 4), p.z + 1 - 2 * lax.rem(p.z, 2)
        to_far, to_near = p.device(far, p.x, p.y, p.c), p.device(near, p.x, p.y, p.c)
        if step == 0:
            self.own_copy(k).wait()
            self.pass_on(k, 0, 0, self.at(k, p.z, p.x, 1 - p.y, p.c), p.across_y()).wait_recv()
            self.to_block(k, 1, p.z, p.x, p.across_x())
        elif step == 1:
            self.from_block(k, p.z, 1 - p.x)
        elif step in (2, 3):
            self.to_block(k, step, p.z, p.x if step == 2 else 1 - p.x, to_far)
        elif step in (4, 5):
            self.to_block(k, step, p.z, p.x if step == 4 else 1 - p.x, to_near)
        elif step in (6, 7):
            x = p.x if step == 6 else 1 - p.x
            self.from_block(k, far, x)
            self.to_block(k, step, far, x, to_near)
        else:
            for z in (near, lax.rem(near + 2, 4)):
                for x in range(2):
                    self.from_block(k, z, x)
            self.pass_on(k, 8, 9, self.cores(k, p.c), p.across_core()).start()

    def from_z(self, k, hop):
        p = self.peers
        for side in (1, -1):
            z = p.z - side * hop
            place = (z, p.x, p.y, p.c)

            @pl.when(self.inside(z))
            def _():
                self.arrived(k, place)
                if hop < 3:
                    @pl.when(self.inside(p.z + side))
                    def _():
                        self.send(k, place, p.device(p.z + side, p.x, p.y, p.c), self.z_slot(hop, side))
                self.send(k, place, p.across_x(), 9 + z)
                self.send(k, place, p.across_y(), 13 + z)
                self.send(k, place, p.across_core(), 17 + z)

    def from_plane(self, k):
        p = self.peers
        for z in range(4):
            place = (z, 1 - p.x, p.y, p.c)
            self.arrived(k, place)
            if z % 2 == 1:
                self.send(k, place, p.across_y(), 29 + z)
            self.send(k, place, p.across_core(), 21 + z)
            place = (z, p.x, 1 - p.y, p.c)
            self.arrived(k, place)
            if z % 2 == 0:
                self.send(k, place, p.across_x(), 29 + z)
            self.send(k, place, p.across_core(), 25 + z)

    def from_corner(self, k):
        p = self.peers
        for z in range(4):
            place = (z, 1 - p.x, 1 - p.y, p.c)
            self.arrived(k, place)
            self.send(k, place, p.across_core(), 33 + z)

    def ready(self, k):
        p = self.peers
        if k == DOUBLED:
            self.pass_on(k, 0, 9, self.cores(k, 1 - p.c), p.across_core()).wait_recv()
            return
        self.own_copy(k).wait()
        for z in range(4):
            for x in range(2):
                for y in range(2):
                    self.arrived(k, (z, x, y, 1 - p.c))

    def close(self, k):
        if k in self.closed:
            return
        self.closed.add(k)
        p = self.peers
        own = (p.z, p.x, p.y, p.c)

        if k == DOUBLED:
            self.pass_on(k, 0, 0, self.at(k, *own), p.across_y()).wait_send()
            for slot in range(1, 8):
                self.pass_on(k, slot, 0, self.block(k, p.z, p.x), p.across_x()).wait_send()
            self.pass_on(k, 8, 9, self.cores(k, p.c), p.across_core()).wait_send()
            return

        def sent(slot):
            self.copy(k, own, p.across_core(), slot).wait_send()

        for slot in (0, 1, 2) + tuple(range(21, 37)):
            sent(slot)
        for step in (1, 2, 3):
            z = lax.rem(p.z + step, 4)
            for base in (9, 13, 17):
                sent(base + z)
        for hop in range(3):
            for side in (1, -1):
                @pl.when(self.inside(p.z - side * hop) & self.inside(p.z + side))
                def _():
                    sent(self.z_slot(hop, side))


class Loaded:
    def __init__(self, blocks, full, own_sem):
        self.blocks, self.full, self.own_sem = blocks, full, own_sem

    def own_copy(self, k):
        return pltpu.make_async_copy(self.blocks[k], self.full.at[k], self.own_sem.at[k])

    def launch(self, k):
        self.own_copy(k).start()

    def from_z(self, *_):
        pass

    from_plane = from_corner = close = doubling = from_z

    def ready(self, k):
        self.own_copy(k).wait()


ORDER = (5, 4, 3, 2, 0, 1)
JOBS = len(ORDER)


class Scatter:
    def __init__(self, full, outs, first_x, first_y, last_x, last_y, own, far, out_vmem, send_sem, recv_sem, credit, out_sem):
        self.full, self.own, self.far, self.outs = full, own, far, outs
        self.first_x, self.first_y, self.last_x, self.last_y = first_x, first_y, last_x, last_y
        self.out_vmem, self.out_sem = out_vmem, out_sem
        self.send_sem, self.recv_sem, self.credit = send_sem, recv_sem, credit
        self.peers = Peers()
        self.depth, self.width = own.shape[2:]
        self.left = [4] * JOBS
        self.sent = set()

    def remote(self, j, slot, source, there, target):
        return pltpu.make_async_remote_copy(
            src_ref=source,
            dst_ref=there,
            send_sem=self.send_sem.at[j, slot],
            recv_sem=self.recv_sem.at[j, slot],
            device_id=target,
            device_id_type=MESH,
        )

    def grad(self, j):
        return self.full.at[j % 2].reshape(8, 2, self.depth, 2 * self.width)

    def pair(self, j):
        return self.full.at[2].reshape(2, 8, self.depth, 2 * self.width).at[j % 2]

    def half(self, which):
        return pl.ds(pl.multiple_of(which * self.width, 128), self.width)

    def cores(self, j):
        return self.remote(j, 0, self.grad(j).at[:, 1 - self.peers.c], self.pair(j), self.peers.across_core())

    def out_x(self, j, n):
        p = self.peers
        return self.remote(j, 1 + n, self.pair(j).at[2 * n + 1 - p.x], self.first_x.at[j, n], p.across_x())

    def out_y(self, j, n):
        p = self.peers
        z = 3 - n
        return self.remote(
            j, 3 + n, self.pair(j).at[2 * z : 2 * z + 2, :, self.half(1 - p.y)], self.first_y.at[j, n], p.across_y()
        )

    def then_y(self, j, n):
        p = self.peers
        return self.remote(j, 5 + n, self.first_x.at[j, n, :, self.half(1 - p.y)], self.last_y.at[j, n], p.across_y())

    def then_x(self, j, n):
        p = self.peers
        return self.remote(j, 7 + n, self.first_y.at[j, n, 1 - p.x], self.last_x.at[j, n], p.across_x())

    def along(self, j, z):
        p = self.peers
        place = lax.rem(p.z - z + 4, 4) - 1
        return self.remote(j, 9 + place, self.own.at[j % 3, z], self.far.at[j, place], p.device(z, p.x, p.y, p.c))

    def open(self):
        pl.semaphore_signal(self.credit, inc=2, device_id=self.peers.across_core(), device_id_type=MESH)

    def start(self, j):
        pl.semaphore_wait(self.credit, 1)
        self.cores(j).start()

    def pair_sum(self, j):
        p = self.peers
        self.cores(j).wait_recv()
        mine, sums = self.grad(j), self.pair(j)

        @pl.loop(0, 8)
        def _(n):
            sums[n] = mine[n, p.c] + sums[n]

        for n in range(2):
            self.out_x(j, n).start()
            self.out_y(j, n).start()
        self.cores(j).wait_send()

    def used(self, j):
        self.left[j] -= 1
        if self.left[j] == 0:
            for n in range(2):
                self.out_x(j, n).wait_send()
                self.out_y(j, n).wait_send()
            if j + 2 < JOBS:
                pl.semaphore_signal(self.credit, inc=1, device_id=self.peers.across_core(), device_id_type=MESH)

    def plane_x(self, j, n):
        p = self.peers
        self.out_x(j, n).wait_recv()
        self.first_x[j, n] = self.first_x[j, n] + self.pair(j)[2 * n + p.x]
        self.then_y(j, n).start()
        self.used(j)

    def plane_y(self, j, n):
        p = self.peers
        self.out_y(j, n).wait_recv()
        for x in range(2):
            mine = self.pair(j)[2 * (3 - n) + x, :, self.half(p.y)]
            self.first_y[j, n, x] = self.first_y[j, n, x] + mine
        self.then_x(j, n).start()
        self.used(j)

    def all_sent(self, j):
        if j >= 0 and j not in self.sent:
            self.sent.add(j)
            for step in (1, 2, 3):
                self.along(j, lax.rem(self.peers.z + step, 4)).wait_send()

    def plane_last(self, j, n):
        p = self.peers
        self.all_sent(j - 3)
        self.then_y(j, n).wait_recv()
        self.own[j % 3, n] = self.first_x[j, n, :, self.half(p.y)] + self.last_y[j, n]
        self.then_x(j, n).wait_recv()
        self.own[j % 3, 3 - n] = self.first_y[j, n, p.x] + self.last_x[j, n]
        for z in (n, 3 - n):
            @pl.when(p.z != z)
            def _():
                self.along(j, z).start()

    def out_copy(self, j):
        return pltpu.make_async_copy(self.out_vmem.at[j], self.outs[ORDER[j]], self.out_sem.at[j])

    def finish(self, j):
        p = self.peers
        total = self.own[j % 3, p.z].astype(F32)
        for step in (1, 2, 3):
            self.along(j, lax.rem(p.z + 4 - step, 4)).wait_recv()
        for place in range(3):
            total += self.far[j, place].astype(F32)
        self.out_vmem[j] = total
        self.out_copy(j).start()

    def end(self):
        p = self.peers
        for j in range(JOBS):
            for n in range(2):
                self.then_y(j, n).wait_send()
                self.then_x(j, n).wait_send()
            self.all_sent(j)
            self.out_copy(j).wait()


class Kept:
    def __init__(self, full, outs, sems):
        self.full, self.outs, self.sems = full, outs, sems

    def copy(self, j):
        return pltpu.make_async_copy(self.full.at[j % 2], self.outs[ORDER[j]], self.sems.at[j])

    def start(self, j):
        self.copy(j).start()

    def pair_sum(self, j):
        self.copy(j).wait()

    def open(self, *_):
        pass

    plane_x = plane_y = plane_last = finish = end = open


class Totals:
    def __init__(self, sums, got, far, send_sem, recv_sem):
        self.sums, self.got, self.far, self.send_sem, self.recv_sem = sums, got, far, send_sem, recv_sem
        self.peers = Peers()

    def copy(self, n, source, there, target):
        return pltpu.make_async_remote_copy(
            src_ref=source, dst_ref=there, send_sem=self.send_sem.at[n], recv_sem=self.recv_sem.at[n],
            device_id=target, device_id_type=MESH,
        )

    def pair(self, n):
        target = (self.peers.across_core, self.peers.across_x, self.peers.across_y)[n]()
        return self.copy(n, self.sums.at[n], self.got.at[n], target)

    def along(self, step):
        z = self.peers.z
        return self.copy(2 + step, self.sums.at[3], self.far.at[z], self.peers.along_z(step))

    def coming(self, step):
        z = lax.rem(self.peers.z - step + 4, 4)
        return self.copy(2 + step, self.sums.at[3], self.far.at[z], self.peers.along_z(step))

    def start(self, n):
        if n < 3:
            self.pair(n).start()
            return
        self.far[self.peers.z] = self.sums[3]
        for step in (1, 2, 3):
            self.along(step).start()

    def take(self, n):
        if n < 3:
            self.pair(n).wait_recv()
            self.sums[n + 1] = self.sums[n] + self.got[n]
            return None
        for step in (1, 2, 3):
            self.coming(step).wait_recv()
        return (self.far[0] + self.far[1]) + (self.far[2] + self.far[3])

    def end(self):
        for n in range(3):
            self.pair(n).wait_send()
        for step in (1, 2, 3):
            self.along(step).wait_send()


def gather_back(packed, group, right_ref, rows):
    row, col = block_offset()
    diagonal = jnp.where(row == col, 1.0, 0.0).astype(BF)
    parts = []
    for pair in range(4 * group, 4 * group + 4):
        left = jnp.concatenate(
            [roll_rows(packed, -(2 * pair + side)) * diagonal for side in range(2)], axis=1
        )
        win = pl.ds(head_window(pair), 256)
        parts.append(nn(left, split_heads(right_ref[rows, win], head_masks(pair))))
    return join_windows(parts)


def norm_back(values, gain, grad_in):
    factor = inverse_rms(values)
    inner = jnp.mean(grad_in * gain * values, axis=-1, keepdims=True)
    grad_out = factor * gain * grad_in - values * (factor * factor * factor * inner)
    return grad_out, jnp.sum(grad_in * values * factor, axis=0, keepdims=True)


def allowed_keys(segments):
    query = jnp.broadcast_to(segments.astype(F32), (SEQ, SEQ))
    row, col = block_offset()
    key_at = lax.broadcasted_iota(jnp.int32, (SEQ, SEQ), 0)
    query_at = lax.broadcasted_iota(jnp.int32, (SEQ, SEQ), 1)
    seen = (query.T == query) & (row == col) & (key_at <= query_at)
    return jnp.sum(jnp.where(seen, 1.0, 0.0).reshape(8, PATCHES, SEQ), axis=0)


SCHEDULE = (
    ("launch", 0), ("launch", 3), ("launch", 2), ("launch", 1), ("Z", 2, 1), ("n1", 0, 1), ("Z", 1, 1), ("n1", 1, 4),
    ("tr", 0, 1), ("D", 3, 0), ("Z", 1, 2), ("D", 3, 2), ("D", 3, 4), ("Z", 1, 3), ("Z", 0, 1), ("P", 1),
    ("Z", 2, 2), ("Z", 0, 2), ("C", 1), ("D", 3, 1), ("Z", 2, 3), ("tr", 1, 2), ("D", 3, 5), ("D", 3, 3),
    ("tr", 2, 3), ("Z", 0, 3), ("R", 1), ("tr", 3, 4), ("k", 0, 2), ("P", 2), ("P", 0), ("k", 2, 3), ("launch", 4),
    ("k", 3, 4), ("launch", 5), ("C", 2), ("Z", 4, 1), ("D", 3, 6), ("R", 2), ("v", 0, 3), ("C", 0), ("v", 3, 4),
    ("Z", 4, 2), ("Z", 5, 1), ("R", 0), ("D", 3, 7), ("q", 0, 4), ("af", 0, 3), ("Z", 4, 3), ("af", 3, 4),
    ("Z", 5, 2), ("af", 4, 6), ("D", 3, 8), ("P", 4), ("af", 6, 8), ("Z", 5, 3), ("R", 3), ("o", 0, 2), ("C", 4),
    ("o", 2, 4), ("R", 4), ("P", 5), ("u", 0, 4), ("C", 5), ("gwd", 0, 3), ("R", 5), ("ga", 0, 1), ("gwd", 3, 4),
    ("ga", 1, 4), ("gwu", 0, 1), ("gwd", 4, 5), ("s", 0), ("gwu", 1, 5), ("p", 0), ("y", 0, 4), ("gn2", 0, 1),
    ("Y", 0, 0), ("s", 1), ("gn2", 1, 3), ("X", 0, 0), ("gn2", 3, 4), ("p", 1), ("gwo", 0, 4), ("X", 0, 1),
    ("Y", 0, 1), ("gwo", 4, 5), ("s", 2), ("gatt", 0, 1), ("X", 1, 0), ("gatt", 1, 4), ("p", 2), ("Y", 1, 1),
    ("ab", 0, 2), ("Y", 1, 0), ("ab", 2, 6), ("Y", 2, 0), ("ab", 6, 8), ("L", 0, 0), ("X", 1, 1), ("gwv", 0, 1),
    ("X", 2, 1), ("gwv", 1, 5), ("s", 3), ("L", 0, 1), ("X", 2, 0), ("gwq", 0, 1), ("Y", 2, 1), ("gwq", 1, 2),
    ("L", 1, 1), ("gwq", 2, 3), ("p", 3), ("gn1", 0, 1), ("F", 0), ("L", 2, 1), ("gwq", 3, 5), ("Y", 3, 0),
    ("X", 3, 0), ("gwk", 0, 1), ("L", 1, 0), ("s", 4), ("gn1", 1, 2), ("Y", 3, 1), ("X", 3, 1), ("gwk", 1, 2),
    ("L", 2, 0), ("p", 4), ("L", 3, 0), ("gwk", 2, 3), ("gn1", 2, 4), ("X", 4, 0), ("Y", 4, 0), ("L", 3, 1),
    ("t", 0), ("gwk", 3, 5), ("s", 5), ("T", 0), ("t", 1), ("X", 4, 1), ("Y", 4, 1), ("F", 1), ("F", 2), ("T", 1),
    ("t", 2), ("L", 4, 0), ("p", 5), ("T", 2), ("t", 3), ("Y", 5, 0), ("X", 5, 0), ("L", 4, 1), ("Y", 5, 1),
    ("L", 5, 0), ("F", 4), ("X", 5, 1), ("T", 3), ("F", 3), ("L", 5, 1), ("F", 5),
)


def layer_kernel(
    remote,
    x_hbm, g_hbm, seg_ref, dim_ref, gain_attn_in, gain_mlp_in, bias_q_in, bias_v_in, bias_o_in, bias_up_in, bias_down_in,
    w0, w1, w2, w3, w4, w5,
    y_out, in_grad_out, g0, g1, g2, g3, g4, g5,
    s_query, s_value, s_out, s_up, s_down, s_dim, s_gain_attn, s_gain_mlp, spill, n1_spill,
    full, b0, b1, b2, b3, b4, b5, b6, b7, res, probs, sums, vecs,
    own_sem, load_sem, *rest,
):
    tokens, width = b0.shape
    half = pl.multiple_of(lax.axis_index("heads") * tokens, SEQ)
    outs = (g0, g1, g2, g3, g4, g5)
    loads, stores = {}, {}

    def move(name, source, target):
        copy = pltpu.make_async_copy(source, target, load_sem.at[len(loads) + len(stores)])
        copy.start()
        return copy

    def load(name, source, target):
        loads[name] = move(name, source, target)

    def store(name, source, target):
        stores[name] = move(name, source, target)

    def loaded(*names):
        for name in names:
            if name in loads and name not in waited:
                loads[name].wait()
                waited.add(name)

    def stored(*names):
        for name in names:
            if name not in waited:
                stores[name].wait()
                waited.add(name)

    waited = set()
    load("x", x_hbm.at[pl.ds(half, tokens)], b0)
    if remote:
        Peers().enter()
        gather = Gather((w0, w1, w2, w3, w4, w5), full, rest[0], rest[1], own_sem)
        scatter = Scatter(full, outs, *rest[2:13])
        totals = Totals(sums, *rest[13:17])
    else:
        gather = Loaded((w0, w1, w2, w3, w4, w5), full, own_sem)
        scatter, totals = Kept(full, outs, rest[0]), None
    sums[0] = jnp.zeros(sums.shape[1:], F32)
    inputs = (gain_attn_in, gain_mlp_in, bias_q_in, bias_v_in, bias_o_in, bias_up_in, bias_down_in)
    for n, vector in enumerate(inputs):
        vecs[n : n + 1] = vector[...].reshape(1, width)
    factor = QUERY_BASE / math.sqrt(DH)
    dims = dim_ref[...].reshape(1, DH)
    softplus = jnp.maximum(dims, 0.0) + jnp.log(1.0 + jnp.exp(-jnp.abs(dims)))
    vecs[7:8] = jnp.concatenate([factor * softplus] * (width // DH), axis=1)
    gain_attn_ref, gain_mlp_ref, bias_q_ref, bias_v_ref = (vecs.at[n : n + 1] for n in range(4))
    bias_o_ref, bias_up_ref, bias_down_ref, scale_ref = (vecs.at[n : n + 1] for n in range(4, 8))
    small = sums.at[0]
    every = slice(None)

    def add_to(row, cols, values):
        small[row : row + 1, cols] = small[row : row + 1, cols] + values

    def over(first, last, size, body, merge=False):
        if merge and last - first > 1:
            for n in range(first, last - 1, 2):
                body(pl.ds(n * size, 2 * size), n)
            first = last - (last - first) % 2
            if first == last:
                return
        if last - first == 1:
            body(pl.ds(first * size, size), first)
            return

        @pl.loop(first, last)
        def _(i):
            body(tile(i, size), i)

    def normed_one(first, last):
        loaded("x")

        def body(rows, i):
            values = b0[rows].astype(F32)
            b1[rows] = (values * inverse_rms(values) * gain_attn_ref[...]).astype(BF)

        over(first, last, ROWS, body)

    split = width // ROWS - 1

    def turn(first, last):
        for i in range(first, last):
            rows = pl.ds(i * ROWS, ROWS)
            for n in range(split + 1):
                piece = b1[rows, n * ROWS : (n + 1) * ROWS].T
                if n < split:
                    b3[n * ROWS : (n + 1) * ROWS, rows] = piece
                else:
                    b3[rows, n * ROWS :] = piece
        if last * ROWS == tokens:
            store("n1_out", b3, n1_spill)

    def query(first, last):
        def body(rows, i):
            b4[rows] = ((nn(b1[rows], full[0]) + bias_q_ref[...]) * scale_ref[...]).astype(BF)

        over(first, last, ROWS, body, True)

    def key(first, last):
        def body(rows, i):
            b5[rows] = nn(b1[rows], full[1]).astype(BF)

        over(first, last, ROWS, body, True)

    def value(first, last):
        def body(rows, i):
            b6[rows] = (nn(b1[rows], full[2]) + bias_v_ref[...]).astype(BF)

        over(first, last, ROWS, body, True)

    def attend(first, last):
        def body(rows, i):
            allowed = jnp.concatenate([allowed_keys(seg_ref[pl.ds(lax.axis_index("heads") * (tokens // SEQ) + i, 1)])] * 8, axis=0)
            for group in range(2):
                part = softmax_packed(pack_scores(b5, b4, rows, group), allowed)
                probs[i, group] = part.astype(BF)
                b1[rows, 640 * group : 640 * (group + 1)] = spread(part.T.astype(BF), group, b6, rows).astype(BF)

        over(first, last, SEQ, body)

    def attend_out(first, last):
        def body(rows, i):
            total = b0[rows].astype(F32) + nt(b1[rows], full[3]) + bias_o_ref[...]
            res[rows] = total
            b2[rows] = (total * inverse_rms(total) * gain_mlp_ref[...]).astype(BF)

        over(first, last, ROWS, body, True)
        if last * ROWS == tokens:
            load("g", g_hbm.at[pl.ds(half, tokens)], b0)

    def up(first, last):
        stored("n1_out")

        def body(rows, i):
            up_proj = nn(b2[rows], full[4]) + bias_up_ref[...]
            square = up_proj * up_proj
            tanh = jnp.tanh(GELU_C * up_proj * (1.0 + 0.044715 * square))
            b7[rows] = (0.5 * up_proj * (1.0 + tanh)).astype(BF)
            slope = 0.5 * (1.0 + tanh) + 0.5 * up_proj * (1.0 - tanh * tanh) * (
                GELU_C * (1.0 + 3 * 0.044715 * square)
            )
            b3[rows] = slope.astype(BF)

        over(first, last, ROWS, body, True)

    def weight_grad(slot, left, right):
        def run(first, last):
            def body(cols, i):
                full[slot, cols] = tn(left[:, cols], right[...]).astype(BF)

            over(first, last, ROWS, body)

        return run

    down_grad = weight_grad(0, b0, b7)

    def grad_down(first, last):
        loaded("g")
        if remote:
            stored("w0", "w2")
        gather.close(0)
        if first == 0:
            gather.close(2)
            scatter.open()
        down_grad(first, last)

    def down(first, last):
        def body(rows, i):
            b7[rows] = (res[rows] + nt(b7[rows], full[5]) + bias_down_ref[...]).astype(BF)

        over(first, last, ROWS, body, True)
        rows = pl.ds(first * ROWS, (last - first) * ROWS)
        store(f"y{first}", b7.at[rows], y_out.at[rows])

    def grad_act(first, last):
        def body(rows, i):
            grad_up = (nn(b0[rows], full[5]) * b3[rows].astype(F32)).astype(BF)
            b3[rows] = grad_up
            add_to(7, every, jnp.sum(grad_up.astype(F32), axis=0, keepdims=True))
            add_to(3, every, jnp.sum(b0[rows].astype(F32), axis=0, keepdims=True))

        over(first, last, ROWS, body, True)

    up_grad = weight_grad(1, b2, b3)

    def grad_up(first, last):
        if remote:
            stored("w1")
        gather.close(1)
        up_grad(first, last)

    def reload(k, slot):
        gather.close(slot)
        load(f"again{k}", spill.at[k] if remote else (w0, w1, w2)[k], full.at[slot])

    def norm_two_back(first, last):
        if first == 0:
            reload(0, 5)

        def body(rows, i):
            back, gain_sum = norm_back(res[rows], gain_mlp_ref[...], nt(b3[rows], full[4]))
            total = b0[rows].astype(F32) + back
            res[rows] = total
            b2[rows] = total.astype(BF)
            add_to(1, every, gain_sum)
            add_to(2, every, jnp.sum(total, axis=0, keepdims=True))

        over(first, last, ROWS, body, True)
        if last * ROWS == tokens:
            reload(1, 4)
            load("n1", n1_spill, b3)

    grad_out = weight_grad(0, b2, b1)

    def attended_grad(first, last):
        if first == 0:
            load("x2", x_hbm.at[pl.ds(half, tokens)], b1)

        def body(rows, i):
            b0[rows] = nn(b2[rows], full[3]).astype(BF)

        over(first, last, ROWS, body, True)
        if last * ROWS == tokens:
            reload(2, 3)

    def attend_back(first, last):
        def body(rows, i):
            for group in range(2):
                cols = slice(640 * group, 640 * (group + 1))
                soft = probs[i, group]
                grad_soft = pack_scores(b6, b0, rows, group).reshape(8, PATCHES, SEQ)
                soft_f = soft.astype(F32).reshape(8, PATCHES, SEQ)
                inner = jnp.sum(soft_f * grad_soft, axis=1, keepdims=True)
                grad_scores = (soft_f * (grad_soft - inner)).reshape(SEQ, SEQ)
                grad_q = spread(grad_scores.T.astype(BF), group, b5, rows)
                grad_k = gather_back(grad_scores.astype(BF), group, b4, rows).astype(BF)
                grad_v = gather_back(soft, group, b0, rows).astype(BF)
                add_to(4, cols, jnp.sum(grad_q * b4[rows, cols].astype(F32), axis=0, keepdims=True))
                grad_q = (grad_q * scale_ref[:, cols]).astype(BF)
                add_to(5, cols, jnp.sum(grad_q.astype(F32), axis=0, keepdims=True))
                add_to(6, cols, jnp.sum(grad_v.astype(F32), axis=0, keepdims=True))
                b4[rows, cols] = grad_q
                b5[rows, cols] = grad_k
                b6[rows, cols] = grad_v

        over(first, last, SEQ, body)

    def inward_grad(slot, right):
        def run(first, last):
            loaded("n1")

            def body(cols, i):
                full[slot, cols] = nn(b3[cols, : split * ROWS], right[...]).astype(BF)

            if first < min(last, split):
                over(first, min(last, split), ROWS, body)
            if last > split:
                left = jnp.concatenate([b3[n * ROWS : (n + 1) * ROWS, split * ROWS :] for n in range(split)], axis=1)
                full[slot, split * ROWS :] = nn(left, right[...]).astype(BF)

        return run

    def norm_one_back(first, last):
        loaded("again0", "again1", "again2", "x2")

        def body(rows, i):
            grad_norm = nt(b4[rows], full[5]) + nt(b5[rows], full[4]) + nt(b6[rows], full[3])
            back, gain_sum = norm_back(b1[rows].astype(F32), gain_attn_ref[...], grad_norm)
            res[rows] = res[rows] + back
            add_to(0, every, gain_sum)

        over(first, last, ROWS, body)
        rows = pl.ds(first * ROWS, (last - first) * ROWS)
        store(f"dx{first}", res.at[rows], in_grad_out.at[rows])

    def arrived(k):
        gather.ready(k)
        if remote and k < 3:
            store(f"w{k}", full.at[k], spill.at[k])

    def total_start(n):
        if remote:
            totals.start(n)

    def total_take(n):
        done = totals.take(n) if remote else sums[0]
        if n < 3:
            return
        by_lane = done[4:5] / scale_ref[...]
        by_dim = by_lane[:, :DH]
        for head in range(1, width // DH):
            by_dim = by_dim + by_lane[:, DH * head : DH * (head + 1)]
        s_dim[...] = (by_dim * (factor / (1.0 + jnp.exp(-dims)))).reshape(DH)
        rows = ((s_query, 5), (s_value, 6), (s_out, 2), (s_up, 7), (s_down, 3), (s_gain_attn, 0), (s_gain_mlp, 1))
        for target, row in rows:
            target[...] = done[row : row + 1].reshape(width)

    steps = {
        "launch": gather.launch, "Z": gather.from_z, "P": gather.from_plane, "C": gather.from_corner, "R": arrived, "D": gather.doubling,
        "n1": normed_one, "q": query, "k": key, "v": value, "af": attend, "o": attend_out, "u": up, "gwd": grad_down,
        "y": down, "ga": grad_act, "gwu": grad_up, "gn2": norm_two_back, "gwo": grad_out, "gatt": attended_grad,
        "ab": attend_back, "gwv": inward_grad(1, b6), "gwq": inward_grad(0, b4), "gwk": inward_grad(1, b5), "tr": turn,
        "gn1": norm_one_back, "s": scatter.start, "p": scatter.pair_sum, "X": scatter.plane_x, "Y": scatter.plane_y,
        "L": scatter.plane_last, "F": scatter.finish, "t": total_start, "T": total_take,
    }
    for name, *numbers in SCHEDULE:
        steps[name](*numbers)
    for name, copy in list(stores.items()):
        if name not in waited:
            copy.wait()
    scatter.end()
    if remote:
        totals.end()


def layer(remote, tokens, x, g, segments, vectors, weights):
    d = x.shape[1]
    hbm, vmem = pl.BlockSpec(memory_space=pl.ANY), pl.BlockSpec(memory_space=pltpu.VMEM)
    dma, regular = pltpu.SemaphoreType.DMA, pltpu.SemaphoreType.REGULAR
    big = pltpu.VMEM((tokens, d), BF)
    sums = pltpu.VMEM((4 if remote else 1, 8, d), F32)
    scratch = [pltpu.VMEM((6, d, d), BF)] + [big] * 8
    scratch += [pltpu.VMEM((tokens, d), F32), pltpu.VMEM((tokens // SEQ, 2, SEQ, SEQ), BF), sums, pltpu.VMEM((8, d), F32), dma((6,)), dma((24,))]
    if remote:
        depth, width = d // lax.axis_size("wide"), d // lax.axis_size("heads")
        block = (depth, width)
        scratch += [
            dma((6, Gather.SLOTS)), dma((6, 32)),
            pltpu.VMEM((JOBS, 2, depth, d), BF), pltpu.VMEM((JOBS, 2, 2) + block, BF),
            pltpu.VMEM((JOBS, 2) + block, BF), pltpu.VMEM((JOBS, 2) + block, BF),
            pltpu.VMEM((3, 4) + block, BF), pltpu.VMEM((JOBS, 3) + block, BF),
            pltpu.VMEM((JOBS,) + block, F32),
            dma((JOBS, 12)), dma((JOBS, 12)), regular, dma((JOBS,)),
            pltpu.VMEM((3, 8, d), F32), pltpu.VMEM((4, 8, d), F32), dma((6,)), dma((6,)),
        ]
        grads = [jax.ShapeDtypeStruct(block, F32)] * 6
    else:
        scratch += [dma((JOBS,))]
        grads = [jax.ShapeDtypeStruct((d, d), BF)] * 6
    outs = [
        jax.ShapeDtypeStruct((tokens, d), BF), jax.ShapeDtypeStruct((tokens, d), F32), *grads,
        *[jax.ShapeDtypeStruct((DH if n == 5 else d,), F32) for n in range(8)], jax.ShapeDtypeStruct((3, d, d), BF), jax.ShapeDtypeStruct((tokens, d), BF),
    ]
    return pl.pallas_call(
        functools.partial(layer_kernel, remote),
        out_shape=outs,
        in_specs=[hbm, hbm] + [vmem] * 9 + [hbm] * 6,
        out_specs=[hbm] * 8 + [vmem] * 8 + [hbm] * 2,
        scratch_shapes=scratch,
        compiler_params=pltpu.CompilerParams(
            collective_id=0 if remote else None,
            has_side_effects=remote,
            vmem_limit_bytes=127 * 2**19,
        ),
        name="layer",
    )(x, g, segments, *vectors, *weights)


def deliver_kernel(parts, *refs):
    count = len(parts)
    sources, targets, held, sems = refs[:count], refs[count : 2 * count], refs[2 * count : 3 * count], refs[3 * count]
    steps = []
    for source, target, middle, cut in zip(sources, targets, held, parts):
        depth = source.shape[0] // cut
        for n in range(cut):
            rows = pl.ds(n * depth, depth)
            first = pltpu.make_async_copy(source.at[rows], middle.at[rows], sems.at[0, len(steps)])
            first.start()
            steps.append((first, pltpu.make_async_copy(middle.at[rows], target.at[rows], sems.at[1, len(steps)])))
    for first, second in steps:
        first.wait()
        second.start()
    for first, second in steps:
        second.wait()


def deliver(arrays):
    parts = [8 if a.size >= 2**20 else 1 for a in arrays]
    hbm = pl.BlockSpec(memory_space=pl.ANY)
    return pl.pallas_call(
        functools.partial(deliver_kernel, parts),
        out_shape=[jax.ShapeDtypeStruct(a.shape, a.dtype) for a in arrays],
        in_specs=[hbm] * len(arrays),
        out_specs=[hbm] * len(arrays),
        scratch_shapes=[pltpu.VMEM(a.shape, a.dtype) for a in arrays] + [pltpu.SemaphoreType.DMA((2, sum(parts)))],
        compiler_params=pltpu.CompilerParams(vmem_limit_bytes=62 * 2**20),
        name="deliver",
    )(*arrays)


def shards(
    inputs, segment_ids, cotangent, w_query, w_key, w_value, w_out, w_up, w_down,
    b_query, b_value, b_out, b_up, b_down, dim_scale, gain_attn, gain_mlp,
):
    tokens = inputs.shape[0] // lax.axis_size("heads")
    remote = lax.axis_size("wide") == 16 and lax.axis_size("heads") == 2
    vectors = (dim_scale, gain_attn, gain_mlp, b_query, b_value, b_out, b_up, b_down)
    weights = [w_query, w_key, w_value, w_out.T, w_up, w_down.T]
    if not remote:
        weights = [
            lax.all_gather(lax.all_gather(w, "heads", axis=1, tiled=True), "wide", axis=0, tiled=True) for w in weights
        ]
    output, input_grad, *rest = layer(remote, tokens, inputs, cotangent, segment_ids.reshape(-1, SEQ), vectors, weights)
    rest = rest[:14]
    if remote:
        output, input_grad, *rest = deliver([output, input_grad, *rest])
    grads, sums = rest[:6], rest[6:]
    if not remote:
        grads = [lax.psum_scatter(grad, "wide", scatter_dimension=0, tiled=True) for grad in grads]
        grads = [lax.psum_scatter(grad, "heads", scatter_dimension=1, tiled=True).astype(F32) for grad in grads]
        sums = lax.psum(sums, ("wide", "heads"))
    grads[3], grads[5] = grads[3].T, grads[5].T
    return (output, input_grad, *grads, *sums)


def solution(mesh):
    token, both = P("wide", None), P(("wide", "heads"), None)
    tall, flat = P("wide", "heads"), P("heads", "wide")
    return jax.shard_map(
        shards,
        mesh=mesh,
        in_specs=(token, P("wide"), token, tall, tall, tall, flat, tall, flat) + (P(),) * 8,
        out_specs=(both, both, tall, tall, tall, flat, tall, flat) + (P(),) * 8,
        check_vma=False,
    )
```
